32 devices in a mesh: pos: 16 (over z, y, x), clip: 2 (over core).
Axes of the slice: x: 2, y: 2, z: 4, core: 2. Of those that a mesh axis runs over, the one named last changes fastest.
Arguments:
- tokens: bfloat16 [4, 16, 1024, 384], P('clip', None, 'pos'), may hold values from -18 to 18
- timesteps: int32 [4], P('clip'), may hold values from 0 to 999
- weight_codes: int32 [4], P('clip'), may hold values from 0 to 7
- cotangent: bfloat16 [4, 16, 1024, 384], P('clip', None, 'pos'), may hold values from -6 to 6
- ada_weight: bfloat16 [2, 384, 2304], replicated, may hold values from -0.3125 to 0.3125
- qkv_weight: bfloat16 [2, 384, 1152], replicated, may hold values from -0.3125 to 0.3125
- out_weight: bfloat16 [2, 384, 384], replicated, may hold values from -2.5 to 2.5
- up_weight: bfloat16 [2, 384, 1536], replicated, may hold values from -0.3125 to 0.3125
- down_weight: bfloat16 [2, 1536, 384], replicated, may hold values from -0.15625 to 0.15625
Outputs:
- activations: bfloat16 [4, 16, 1024, 384], P('clip', None, 'pos')
- grad_tokens: float32 [4, 16, 1024, 384], P('clip', None, 'pos')
- ada_grad: float32 [2, 384, 2304], replicated
- qkv_grad: float32 [2, 384, 1152], replicated
- out_grad: float32 [2, 384, 384], replicated
- up_grad: float32 [2, 384, 1536], replicated
- down_grad: float32 [2, 1536, 384], replicated
- stream_rms: float32 [2, 3], replicated
The draws below stay inside these ranges and needn't reach their ends.
All inputs are finite; a program needn't handle non-finite values.
Results may differ from the reference program's by a relative error of at most 0.017.
Values may be sent and summed in bfloat16 or wider, within the bound.
No kernel may reach another device: no remote copies, remote signals or barrier semaphores. Data moves between devices by JAX's collectives and lax.ppermute only.
A program may use at most 512 MiB of HBM per device.

```python
import math
import jax
import jax.numpy as jnp
from jax import lax

D = 384
HEADS = 6
HEAD = 64
FF = 1536
P_SIZE = 1024
F = 16
BLOCKS = 2
CLIPS = 4
TOKENS = 65536


def draw_tokens(key, part):
    key = jax.random.fold_in(key, 11)
    shape = (CLIPS, F, P_SIZE, D)
    pos_scale = 3.0 ** (jnp.arange(P_SIZE, dtype=jnp.float32) / max(P_SIZE - 1, 1))
    clip_scale = 0.5 * 3.0 ** (jnp.arange(CLIPS, dtype=jnp.float32) / max(CLIPS - 1, 1))
    base = jnp.clip(jax.random.normal(key, shape, jnp.float32), -4.0, 4.0)
    return (base * clip_scale[:, None, None, None] * pos_scale[None, None, :, None]).astype(jnp.bfloat16)


def pin_ends(key, values, low_value, high_value):
    first_key, second_key = jax.random.split(key)
    high_place = jax.random.randint(first_key, (), 0, CLIPS)
    low_place = (high_place + jax.random.randint(second_key, (), 1, CLIPS)) % CLIPS
    places = jnp.arange(CLIPS, dtype=jnp.int32)
    values = jnp.where(places == high_place, high_value, values)
    values = jnp.where(places == low_place, low_value, values)
    return values.astype(jnp.int32)


def draw_timesteps(key, part):
    key = jax.random.fold_in(key, 23)
    first_key, second_key, third_key = jax.random.split(key, 3)
    first_draw = jax.random.randint(first_key, (CLIPS,), 0, 1000)
    second_draw = jax.random.randint(second_key, (CLIPS,), 0, 1000)
    return pin_ends(third_key, jnp.maximum(first_draw, second_draw), 0, 999)


def draw_weight_codes(key, part):
    key = jax.random.fold_in(key, 37)
    first_key, second_key, third_key, fourth_key = jax.random.split(key, 4)
    first_draw = jax.random.randint(first_key, (CLIPS,), 0, 8)
    second_draw = jax.random.randint(second_key, (CLIPS,), 0, 8)
    third_draw = jax.random.randint(third_key, (CLIPS,), 0, 8)
    codes = jnp.minimum(jnp.minimum(first_draw, second_draw), third_draw)
    return pin_ends(fourth_key, codes, 0, 7)


def steps_of(own_key, shape, pieces, least, top_value):
    level, own = 1.0, jax.random.fold_in(own_key, 6)
    for position, blocks in pieces:
        heights = jnp.exp(jax.random.uniform(jax.random.fold_in(own, position), (blocks,), jnp.float32, least / len(pieces), top_value / len(pieces)))
        level = level * jnp.repeat(heights, shape[position] // blocks).reshape([-1 if axis == position else 1 for axis in range(len(shape))])
    return level


def scatter_about(key, shape, scale, limit, shards=(), kind=jnp.bfloat16):
    values = scale * jax.random.normal(key, shape, jnp.float32)
    if shards:
        values = values * steps_of(key, shape, shards, -0.22, 0.18)
    return jnp.clip(values, -limit, limit).astype(kind)


def setup_inputs(seed: int = 0) -> dict:
    splits = jax.random.split(jax.random.key(seed), 10)
    tokens = draw_tokens(jax.random.fold_in(splits[9], 71), 0)
    timesteps = draw_timesteps(jax.random.fold_in(splits[9], 71), 0)
    weight_codes = draw_weight_codes(jax.random.fold_in(splits[9], 71), 0)
    cotangent = scatter_about(splits[3], (CLIPS, F, P_SIZE, D), 1.0, 6.0, ((0, 2), (2, 16)))
    ada_weight = scatter_about(splits[4], (BLOCKS, D, 6 * D), D ** -0.5, 0.3125)
    qkv_weight = scatter_about(splits[5], (BLOCKS, D, 3 * D), D ** -0.5, 0.3125)
    out_weight = scatter_about(splits[6], (BLOCKS, D, D), (max(D // 64, 2)) ** -0.5, 2.5)
    up_weight = scatter_about(splits[7], (BLOCKS, D, FF), D ** -0.5, 0.3125)
    down_weight = scatter_about(splits[8], (BLOCKS, FF, D), FF ** -0.5, 0.15625)
    return dict(tokens=tokens, timesteps=timesteps, weight_codes=weight_codes, cotangent=cotangent, ada_weight=ada_weight, qkv_weight=qkv_weight, out_weight=out_weight, up_weight=up_weight, down_weight=down_weight)


EPS = 1e-06

@jax.custom_vjp
def low(v):
    return lax.optimization_barrier(v.astype(jnp.bfloat16)).astype(jnp.float32)

@jax.custom_vjp
def low_back(v):
    return v

def low_keep(v):
    return (low(v), None)

def low_pass(kept, grad):
    return (grad,)

def back_keep(v):
    return (v, None)

def back_low(kept, grad):
    return (low(grad),)
low.defvjp(low_keep, low_pass)
low_back.defvjp(back_keep, back_low)

def layer_norm(values):
    center = values - lax.optimization_barrier(jnp.mean(values, axis=-1, keepdims=True))
    spread = lax.optimization_barrier(jnp.mean(center * center, axis=-1, keepdims=True))
    return center * lax.rsqrt(spread + EPS)

def modulate(values, shift_part, scale_part):
    return layer_norm(values) * (1.0 + scale_part[:, None, None, :]) + shift_part[:, None, None, :]

def embed_steps(timesteps):
    half_width = D // 2
    frequencies = jnp.exp(-math.log(10000.0) * jnp.arange(half_width, dtype=jnp.float32) / half_width)
    angles = timesteps.astype(jnp.float32)[:, None] * frequencies[None, :]
    return jax.nn.silu(jnp.concatenate([jnp.cos(angles), jnp.sin(angles)], axis=-1))

def split_heads(values):
    return values.reshape(values.shape[:-1] + (HEADS, HEAD))

def merge_heads(values):
    return values.reshape(values.shape[:-2] + (HEADS * HEAD,))

def frame_attention(triple):
    query_rows, key_rows, value_rows = triple
    scores = jnp.einsum('fqhd,fkhd->fhqk', split_heads(query_rows), split_heads(key_rows), precision=lax.Precision.HIGHEST) * HEAD ** (-0.5)
    scores = low_back(scores)
    attn_probs = low(jax.nn.softmax(scores, axis=-1))
    mixed_heads = jnp.einsum('fhqk,fkhd->fqhd', attn_probs, split_heads(value_rows), precision=lax.Precision.HIGHEST)
    return merge_heads(mixed_heads)

def spatial_attention(query_rows, key_rows, value_rows):
    return lax.map(jax.checkpoint(frame_attention), (query_rows, key_rows, value_rows))

def temporal_attention(query_rows, key_rows, value_rows):
    scores = jnp.einsum('cqphd,ckphd->cphqk', split_heads(query_rows), split_heads(key_rows), precision=lax.Precision.HIGHEST) * HEAD ** (-0.5)
    scores = low_back(scores)
    attn_probs = low(jax.nn.softmax(scores, axis=-1))
    mixed_heads = jnp.einsum('cphqk,ckphd->cqphd', attn_probs, split_heads(value_rows), precision=lax.Precision.HIGHEST)
    return merge_heads(mixed_heads)

def dense(left_rows, weight):
    return jnp.einsum('cfpd,de->cfpe', left_rows, weight, precision=lax.Precision.HIGHEST)

def apply_block(stream, modulation, qkv_matrix, out_matrix, up_matrix, down_matrix, across):
    mod_parts = jnp.split(modulation, 6, axis=-1)
    hidden = low(modulate(stream, mod_parts[0], mod_parts[1]))
    projected = low(low_back(dense(hidden, qkv_matrix)))
    query_rows, key_rows, value_rows = jnp.split(projected, 3, axis=-1)
    if across:
        attended = spatial_attention(query_rows, key_rows, value_rows)
    else:
        attended = temporal_attention(query_rows, key_rows, value_rows)
    attended = low(low_back(attended))
    branch_out = low_back(dense(attended, out_matrix))
    attn_branch = mod_parts[2][:, None, None, :] * branch_out
    middle = stream + attn_branch
    hidden_two = low(modulate(middle, mod_parts[3], mod_parts[4]))
    inner_rows = low_back(dense(hidden_two, up_matrix))
    activated = low(jax.nn.gelu(inner_rows, approximate=True))
    mlp_out = low_back(dense(activated, down_matrix))
    mlp_branch = mod_parts[5][:, None, None, :] * mlp_out
    squares = jnp.stack([jnp.sum(stream * stream), jnp.sum(attn_branch * attn_branch), jnp.sum(mlp_branch * mlp_branch)])
    return (middle + mlp_branch, squares)

def reference(tokens, timesteps, weight_codes, cotangent, ada_weight, qkv_weight, out_weight, up_weight, down_weight):
    embedded = embed_steps(timesteps)

    def forward(stream, ada_all, qkv_all, out_all, up_all, down_all):
        squares_all = []
        for block_index in range(BLOCKS):
            modulation = jnp.dot(embedded, ada_all[block_index], precision=lax.Precision.HIGHEST)
            stream, squares = apply_block(stream, modulation, qkv_all[block_index], out_all[block_index], up_all[block_index], down_all[block_index], block_index % 2 == 0)
            squares_all.append(squares)
        return (stream, jnp.stack(squares_all))
    result, pullback, squares_total = jax.vjp(forward, tokens.astype(jnp.float32), ada_weight.astype(jnp.float32), qkv_weight.astype(jnp.float32), out_weight.astype(jnp.float32), up_weight.astype(jnp.float32), down_weight.astype(jnp.float32), has_aux=True)
    scaling = jnp.exp2(0.5 * weight_codes.astype(jnp.float32) - 1.0)
    scaled_cotangent = cotangent.astype(jnp.float32) * scaling[:, None, None, None]
    gradients = pullback(scaled_cotangent)
    stream_rms = jnp.sqrt(squares_total / TOKENS)
    return (result.astype(jnp.bfloat16), gradients[0], gradients[1], gradients[2], gradients[3], gradients[4], gradients[5], stream_rms)
```

```python
import functools
import math

import jax
import jax.numpy as jnp
from jax import lax
from jax.experimental import pallas as pl
from jax.experimental.pallas import tpu as pltpu
from jax.sharding import PartitionSpec as P

D = 384
HEAD = 64
PAIRS = 3
FF = 1536
EPS = 1e-06
LOG_SCALE = HEAD**-0.5 * math.log2(math.e)
GROUP = 16
FEED_SHAPES = [(D, FF), (FF, D), (D, D)]
VMEM_LIMIT = 56 * 2**20

NN = (((1,), (0,)), ((), ()))
NT = (((1,), (1,)), ((), ()))
TN = (((0,), (0,)), ((), ()))
F32 = jnp.float32
BF = jnp.bfloat16


def mm(left, right, dims=NN):
    return lax.dot_general(left, right, dims, preferred_element_type=F32)


def params():
    return pltpu.CompilerParams(vmem_limit_bytes=VMEM_LIMIT)


def cost(micros):
    return pl.CostEstimate(
        flops=int(micros * 1e9), transcendentals=0, bytes_accessed=int(micros * 3e6)
    )


def norm_rows(values):
    center = values - jnp.mean(values, axis=-1, keepdims=True)
    rstd = lax.rsqrt(jnp.mean(center * center, axis=-1, keepdims=True) + EPS)
    return center * rstd, rstd


def norm_back(grad_normed, normed, rstd):
    mean_grad = jnp.mean(grad_normed, axis=-1, keepdims=True)
    mean_cross = jnp.mean(grad_normed * normed, axis=-1, keepdims=True)
    return rstd * (grad_normed - mean_grad - normed * mean_cross)


def col_sum(values):
    return jnp.sum(values, axis=0, keepdims=True)


def gelu_pair(inner):
    square = inner * inner
    slope = math.sqrt(2.0 / math.pi)
    tanh = jnp.tanh(inner * (slope + (slope * 0.044715) * square))
    half = 0.5 + 0.5 * tanh
    value = inner * half
    grad = half + (value * (1.0 - tanh)) * (slope + (3.0 * 0.044715 * slope) * square)
    return value, grad


def low_lanes():
    return lax.broadcasted_iota(jnp.int32, (1, 2 * HEAD), 1) < HEAD


def both_heads(values, low, fill=0.0):
    other = jnp.full_like(values, fill)
    return (jnp.where(low, values, other), jnp.where(low, other, values))


def whole(shape):
    return pl.BlockSpec(shape, lambda *_: (0,) * len(shape))


def once(shape):
    return pl.BlockSpec(shape, lambda *_: (0,) * len(shape), pipeline_mode=pl.Buffered(1))


def weight_spec(rows, cols, block):
    return pl.BlockSpec((None, rows, cols), lambda *_: (block, 0, 0), pipeline_mode=pl.Buffered(1))


def project_kernel(x_ref, mod_ref, w_ref, out_ref):
    normed, _ = norm_rows(x_ref[...].astype(F32))
    hidden = (normed * (1.0 + mod_ref[1:2]) + mod_ref[0:1]).astype(BF)
    out_ref[...] = mm(hidden, w_ref[...]).astype(BF)


def project(x, mod, qkv_weight, rows):
    n = x.shape[0]
    return pl.pallas_call(
        project_kernel,
        grid=(n // rows,),
        in_specs=[
            pl.BlockSpec((rows, D), lambda i: (i, 0)),
            whole((6, D)),
            weight_spec(D, 3 * D, 0),
        ],
        out_specs=pl.BlockSpec((rows, 3 * D), lambda i: (i, 0)),
        out_shape=jax.ShapeDtypeStruct((n, 3 * D), BF),
        compiler_params=params(),
        cost_estimate=cost(5),
        name="project",
    )(x, mod, qkv_weight)


def attend_kernel(rows, q_ref, k_ref, v_ref, out_ref, log_ref):
    low = low_lanes()
    keys = k_ref[...]
    values = both_heads(v_ref[...], low, 1.0)

    def step(index, carry):
        part = pl.ds(index * rows, rows)
        queries = both_heads(q_ref[part, :], low)
        mixed, tops = [], []
        for head in range(2):
            scores = mm(queries[head], keys, NT)
            top = jnp.max(scores, axis=1, keepdims=True)
            raised = jnp.exp2((scores - top) * LOG_SCALE).astype(BF)
            mixed.append(mm(raised, values[head]))
            tops.append(top * LOG_SCALE)
        total = pltpu.roll(jnp.where(low, mixed[1], mixed[0]), HEAD, 1)
        out_ref[part, :] = (jnp.where(low, mixed[0], mixed[1]) / total).astype(BF)
        log_ref[part, :] = jnp.where(low, tops[0], tops[1]) + jnp.log2(total)
        return carry

    lax.fori_loop(0, q_ref.shape[0] // rows, step, 0)


def attend(qkv, rows):
    n = qkv.shape[0]
    pair = lambda start: pl.BlockSpec((n, 2 * HEAD), lambda p: (0, start + p))
    return pl.pallas_call(
        functools.partial(attend_kernel, rows),
        grid=(PAIRS,),
        in_specs=[pair(0), pair(PAIRS), pair(2 * PAIRS)],
        out_specs=[pair(0), pair(0)],
        out_shape=[jax.ShapeDtypeStruct((n, D), BF), jax.ShapeDtypeStruct((n, D), F32)],
        compiler_params=params(),
        cost_estimate=cost(14),
        name="attend",
    )(qkv, qkv, qkv)


def feed_kernel(
    x_ref,
    att_ref,
    mod_ref,
    wo_ref,
    wu_ref,
    wd_ref,
    next_ref,
    middle_ref,
    branch_ref,
    mlp_ref,
    act_ref,
    slope_ref,
    squares_ref,
):
    @pl.when(pl.program_id(0) == 0)
    def _():
        squares_ref[...] = jnp.zeros_like(squares_ref)

    x = x_ref[...].astype(F32)
    branch = mm(att_ref[...], wo_ref[...])
    gated = mod_ref[2:3] * branch
    middle = x + gated
    normed, _ = norm_rows(middle)
    hidden = (normed * (1.0 + mod_ref[4:5]) + mod_ref[3:4]).astype(BF)
    value, slope = gelu_pair(mm(hidden, wu_ref[...]))
    act = value.astype(BF)
    mlp = mm(act, wd_ref[...])
    fed = mod_ref[5:6] * mlp
    next_ref[...] = (middle + fed).astype(BF)
    middle_ref[...] = middle
    branch_ref[...] = branch.astype(BF)
    mlp_ref[...] = mlp.astype(BF)
    act_ref[...] = act
    slope_ref[...] = slope.astype(BF)
    squares_ref[0:1] += col_sum(x * x)
    squares_ref[1:2] += col_sum(gated * gated)
    squares_ref[2:3] += col_sum(fed * fed)


def feed(x, att, mod, out_weight, up_weight, down_weight, rows):
    n = x.shape[0]
    row = lambda width: pl.BlockSpec((rows, width), lambda i: (i, 0))
    out = lambda width, kind: jax.ShapeDtypeStruct((n, width), kind)
    return pl.pallas_call(
        feed_kernel,
        grid=(n // rows,),
        in_specs=[
            row(D),
            row(D),
            whole((6, D)),
            weight_spec(D, D, 0),
            weight_spec(D, FF, 0),
            weight_spec(FF, D, 0),
        ],
        out_specs=[row(D), row(D), row(D), row(D), row(FF), row(FF), whole((8, D))],
        out_shape=[
            out(D, BF),
            out(D, F32),
            out(D, BF),
            out(D, BF),
            out(FF, BF),
            out(FF, BF),
            jax.ShapeDtypeStruct((8, D), F32),
        ],
        compiler_params=params(),
        cost_estimate=cost(11),
        name="feed",
    )(x, att, mod, out_weight, up_weight, down_weight)


def start_sums(sums, carried):
    for index, total in enumerate(sums):
        total[...] = carried[index][...] if carried else jnp.zeros_like(total)


def row_blocks(total):
    height, width = total.shape
    return [(start, height) for start in range(0, width, D)]


def load_rows(rows_ref, sums):
    at = 0
    for total in sums:
        for start, height in row_blocks(total):
            total[:, start : start + D] = rows_ref[at : at + height]
            at += height


def store_rows(sums, rows_ref):
    at = 0
    for total in sums:
        for start, height in row_blocks(total):
            rows_ref[at : at + height] = total[:, start : start + D].astype(rows_ref.dtype)
            at += height
    if at < rows_ref.shape[0]:
        rows_ref[at:] = jnp.zeros((rows_ref.shape[0] - at, D), rows_ref.dtype)


def split_rows(rows, shapes):
    found, at = [], 0
    for height, width in shapes:
        blocks = []
        for _ in range(width // D):
            blocks.append(rows[at : at + height])
            at += height
        found.append(jnp.concatenate(blocks, axis=1))
    return found


def feed_back_kernel(n_carried, *refs):
    (
        g_ref,
        middle_ref,
        branch_ref,
        mlp_ref,
        act_ref,
        slope_ref,
        att_ref,
        mod_ref,
        wo_ref,
        wu_ref,
        wd_ref,
    ) = refs[:11]
    carried = refs[11 : 11 + n_carried]
    gmid_ref, gatt_ref, part_ref, rows_ref, *sums = refs[11 + n_carried :]

    @pl.when(pl.program_id(0) == 0)
    def _():
        part_ref[...] = jnp.zeros_like(part_ref)
        if carried:
            load_rows(carried[0], sums)
        else:
            start_sums(sums, ())

    up_sum, down_sum, out_sum = sums
    g = g_ref[...].astype(F32)
    part_ref[5:6] += col_sum(mlp_ref[...].astype(F32) * g)
    gm = (mod_ref[5:6] * g).astype(BF)
    down_sum[...] += mm(act_ref[...], gm, TN)
    gi = (slope_ref[...].astype(F32) * mm(gm, wd_ref[...], NT)).astype(BF)
    normed, rstd = norm_rows(middle_ref[...])
    scale = 1.0 + mod_ref[4:5]
    hidden = (normed * scale + mod_ref[3:4]).astype(BF)
    up_sum[...] += mm(hidden, gi, TN)
    gh = mm(gi, wu_ref[...], NT)
    part_ref[3:4] += col_sum(gh)
    part_ref[4:5] += col_sum(gh * normed)
    gmid = g + norm_back(gh * scale, normed, rstd)
    gmid_ref[...] = gmid
    part_ref[2:3] += col_sum(branch_ref[...].astype(F32) * gmid)
    gb = (mod_ref[2:3] * gmid).astype(BF)
    out_sum[...] += mm(att_ref[...], gb, TN)
    gatt_ref[...] = mm(gb, wo_ref[...], NT).astype(BF)

    @pl.when(pl.program_id(0) == pl.num_programs(0) - 1)
    def _():
        store_rows(sums, rows_ref)


def feed_back(g, kept, att, mod, out_weight, up_weight, down_weight, carried, kind, rows, height):
    n = g.shape[0]
    row = lambda width: pl.BlockSpec((rows, width), lambda i: (i, 0))
    shapes = FEED_SHAPES
    return pl.pallas_call(
        functools.partial(feed_back_kernel, len(carried)),
        grid=(n // rows,),
        in_specs=[
            row(D),
            row(D),
            row(D),
            row(D),
            row(FF),
            row(FF),
            row(D),
            whole((6, D)),
            weight_spec(D, D, 0),
            weight_spec(D, FF, 0),
            weight_spec(FF, D, 0),
        ]
        + [once((height, D))] * len(carried),
        out_specs=[row(D), row(D), whole((8, D)), once((height, D))],
        out_shape=[
            jax.ShapeDtypeStruct((n, D), F32),
            jax.ShapeDtypeStruct((n, D), BF),
            jax.ShapeDtypeStruct((8, D), F32),
            jax.ShapeDtypeStruct((height, D), kind),
        ],
        scratch_shapes=[pltpu.VMEM(shape, F32) for shape in shapes],
        compiler_params=params(),
        cost_estimate=cost(16),
        name="feed_back",
    )(g, *kept, att, mod, out_weight, up_weight, down_weight, *carried)


def attend_back_kernel(
    rows, q_ref, k_ref, v_ref, o_ref, log_ref, g_ref, dq_ref, dk_ref, dv_ref, dk_sum, dv_sum
):
    low = low_lanes()
    keys, values = k_ref[...], v_ref[...]
    dk_sum[...] = jnp.zeros_like(dk_sum)
    dv_sum[...] = jnp.zeros_like(dv_sum)

    def step(index, carry):
        part = pl.ds(index * rows, rows)
        queries = both_heads(q_ref[part, :], low)
        grads = both_heads(g_ref[part, :], low)
        cross = both_heads(g_ref[part, :].astype(F32) * o_ref[part, :].astype(F32), low)
        logs = log_ref[part, :]
        found = []
        for head in range(2):
            delta = jnp.sum(cross[head], axis=1, keepdims=True)
            scores = mm(queries[head], keys, NT)
            probs = jnp.exp2(scores * LOG_SCALE - logs[:, HEAD * head : HEAD * head + 1])
            grad_probs = mm(grads[head], values, NT)
            grad_scores = (probs * (grad_probs - delta)).astype(BF)
            found.append(mm(grad_scores, keys))
            dv_sum[...] += mm(grads[head].T, probs.astype(BF))
            dk_sum[...] += mm(queries[head].T, grad_scores)
        dq_ref[part, :] = (jnp.where(low, found[0], found[1]) * HEAD**-0.5).astype(BF)
        return carry

    lax.fori_loop(0, q_ref.shape[0] // rows, step, 0)
    dk_ref[...] = (dk_sum[...] * HEAD**-0.5).T.astype(BF)
    dv_ref[...] = dv_sum[...].T.astype(BF)


def attend_back(qkv, att, logs, grad, rows):
    n = qkv.shape[0]
    pair = lambda start: pl.BlockSpec((n, 2 * HEAD), lambda p: (0, start + p))
    return pl.pallas_call(
        functools.partial(attend_back_kernel, rows),
        grid=(PAIRS,),
        in_specs=[pair(0), pair(PAIRS), pair(2 * PAIRS), pair(0), pair(0), pair(0)],
        out_specs=[pair(0)] * 3,
        out_shape=[jax.ShapeDtypeStruct((n, D), BF)] * 3,
        scratch_shapes=[pltpu.VMEM((2 * HEAD, n), F32)] * 2,
        compiler_params=params(),
        cost_estimate=cost(20),
        name="attend_back",
    )(qkv, qkv, qkv, att, logs, grad)


def project_back_kernel(n_carried, *refs):
    x_ref, dq_ref, dk_ref, dv_ref, gmid_ref, mod_ref, w_ref = refs[:7]
    carried = refs[7 : 7 + n_carried]
    out_ref, part_ref, grad_ref, total = refs[7 + n_carried :]

    @pl.when(pl.program_id(0) == 0)
    def _():
        part_ref[...] = jnp.zeros_like(part_ref)
        if carried:
            load_rows(carried[0], [total])
        else:
            start_sums([total], ())

    normed, rstd = norm_rows(x_ref[...].astype(F32))
    scale = 1.0 + mod_ref[1:2]
    hidden = (normed * scale + mod_ref[0:1]).astype(BF)
    gp = jnp.concatenate([dq_ref[...], dk_ref[...], dv_ref[...]], axis=1)
    total[...] += mm(hidden, gp, TN)
    gh = mm(gp, w_ref[...], NT)
    part_ref[0:1] += col_sum(gh)
    part_ref[1:2] += col_sum(gh * normed)
    out_ref[...] = (gmid_ref[...] + norm_back(gh * scale, normed, rstd)).astype(BF)

    @pl.when(pl.program_id(0) == pl.num_programs(0) - 1)
    def _():
        store_rows([total], grad_ref)


def project_back(x, grads, gmid, mod, qkv_weight, carried, kind, rows):
    n = x.shape[0]
    row = lambda width: pl.BlockSpec((rows, width), lambda i: (i, 0))
    return pl.pallas_call(
        functools.partial(project_back_kernel, len(carried)),
        grid=(n // rows,),
        in_specs=[row(D)] * 5
        + [whole((6, D)), weight_spec(D, 3 * D, 0)]
        + [once((3 * D, D))] * len(carried),
        out_specs=[row(D), whole((8, D)), once((3 * D, D))],
        out_shape=[
            jax.ShapeDtypeStruct((n, D), BF),
            jax.ShapeDtypeStruct((8, D), F32),
            jax.ShapeDtypeStruct((3 * D, D), kind),
        ],
        scratch_shapes=[pltpu.VMEM((D, 3 * D), F32)],
        compiler_params=params(),
        cost_estimate=cost(8),
        name="project_back",
    )(x, *grads, gmid, mod, qkv_weight, *carried)


def temporal_kernel(n_carried, *refs):
    x_ref, cot_ref, code_ref, mod_ref, wq_ref, wo_ref, wu_ref, wd_ref = refs[:8]
    carried = refs[8 : 8 + n_carried]
    refs = refs[8 + n_carried :]
    act_out_ref, g_ref, part_ref = refs[:3]
    out_refs = refs[3:7]
    sums = refs[7:11]
    qkv_ref, att_ref, probs_ref, inv_ref, gatt_ref, gqkv_ref = refs[11:]
    frames, places = x_ref.shape[0], x_ref.shape[1]
    tokens = frames * places
    wide = frames * GROUP
    first = jnp.logical_and(pl.program_id(0) == 0, pl.program_id(1) == 0)
    last = jnp.logical_and(
        pl.program_id(0) == pl.num_programs(0) - 1, pl.program_id(1) == pl.num_programs(1) - 1
    )

    @pl.when(first)
    def _():
        start_sums(sums, carried)

    @pl.when(pl.program_id(1) == 0)
    def _():
        part_ref[...] = jnp.zeros_like(part_ref)

    qkv_sum, out_sum, up_sum, down_sum = sums
    low = low_lanes()
    mod = mod_ref[...]
    x = x_ref[...].reshape(tokens, D).astype(F32)
    normed, rstd = norm_rows(x)
    scale = 1.0 + mod[1:2]
    hidden = (normed * scale + mod[0:1]).astype(BF)
    qkv_ref[...] = mm(hidden, wq_ref[...]).astype(BF).reshape(qkv_ref.shape)

    place = lambda axis: lax.broadcasted_iota(jnp.int32, (wide, wide), axis) % GROUP
    same = place(0) == place(1)
    groups = places // GROUP

    def cut(ref, group, column):
        rows = pl.ds(pl.multiple_of(group * GROUP, GROUP), GROUP)
        return ref[:, rows, column * 2 * HEAD : (column + 1) * 2 * HEAD].reshape(wide, 2 * HEAD)

    def put(ref, group, column, value):
        rows = pl.ds(pl.multiple_of(group * GROUP, GROUP), GROUP)
        ref[:, rows, column * 2 * HEAD : (column + 1) * 2 * HEAD] = value.reshape(
            frames, GROUP, 2 * HEAD
        )

    def attend_group(group, carry):
        for pair in range(PAIRS):
            queries = both_heads(cut(qkv_ref, group, pair), low)
            keys = cut(qkv_ref, group, PAIRS + pair)
            values = both_heads(cut(qkv_ref, group, 2 * PAIRS + pair), low, 1.0)
            mixed = []
            for head in range(2):
                scores = jnp.where(same, mm(queries[head], keys, NT), -1e38)
                top = jnp.max(scores, axis=1, keepdims=True)
                raised = jnp.exp2((scores - top) * LOG_SCALE).astype(BF)
                probs_ref[group * 2 * PAIRS + 2 * pair + head] = raised
                mixed.append(mm(raised, values[head]))
            inverse = 1.0 / pltpu.roll(jnp.where(low, mixed[1], mixed[0]), HEAD, 1)
            put(inv_ref, group, pair, inverse)
            put(att_ref, group, pair, (jnp.where(low, mixed[0], mixed[1]) * inverse).astype(BF))
        return carry

    lax.fori_loop(0, groups, attend_group, 0)

    att = att_ref[...].reshape(tokens, D)
    branch = mm(att, wo_ref[...])
    gated = mod[2:3] * branch
    middle = x + gated
    normed_two, rstd_two = norm_rows(middle)
    scale_two = 1.0 + mod[4:5]
    hidden_two = (normed_two * scale_two + mod[3:4]).astype(BF)
    value, slope = gelu_pair(mm(hidden_two, wu_ref[...]))
    act = value.astype(BF)
    mlp = mm(act, wd_ref[...])
    fed = mod[5:6] * mlp
    act_out_ref[...] = (middle + fed).astype(BF).reshape(act_out_ref.shape)
    part_ref[6:7] += col_sum(x * x)
    part_ref[7:8] += col_sum(gated * gated)
    part_ref[8:9] += col_sum(fed * fed)

    g = cot_ref[...].reshape(tokens, D).astype(F32) * code_ref[0:1]
    part_ref[5:6] += col_sum(mlp * g)
    gm = (mod[5:6] * g).astype(BF)
    down_sum[...] += mm(act, gm, TN)
    gi = (slope * mm(gm, wd_ref[...], NT)).astype(BF)
    up_sum[...] += mm(hidden_two, gi, TN)
    gh = mm(gi, wu_ref[...], NT)
    part_ref[3:4] += col_sum(gh)
    part_ref[4:5] += col_sum(gh * normed_two)
    gmid = g + norm_back(gh * scale_two, normed_two, rstd_two)
    part_ref[2:3] += col_sum(branch * gmid)
    gb = (mod[2:3] * gmid).astype(BF)
    out_sum[...] += mm(att, gb, TN)
    gatt_ref[...] = mm(gb, wo_ref[...], NT).astype(BF).reshape(gatt_ref.shape)

    def back_group(group, carry):
        for pair in range(PAIRS):
            queries = both_heads(cut(qkv_ref, group, pair), low)
            keys = cut(qkv_ref, group, PAIRS + pair)
            values = cut(qkv_ref, group, 2 * PAIRS + pair)
            grad = cut(gatt_ref, group, pair)
            grads = both_heads(grad, low)
            cross = both_heads(grad.astype(F32) * cut(att_ref, group, pair).astype(F32), low)
            inverse = cut(inv_ref, group, pair)
            found = []
            dk = jnp.zeros((wide, 2 * HEAD), F32)
            dv = jnp.zeros((wide, 2 * HEAD), F32)
            for head in range(2):
                delta = jnp.sum(cross[head], axis=1, keepdims=True)
                raised = probs_ref[group * 2 * PAIRS + 2 * pair + head].astype(F32)
                probs = raised * inverse[:, HEAD * head : HEAD * head + 1]
                grad_scores = (probs * (mm(grads[head], values, NT) - delta)).astype(BF)
                found.append(mm(grad_scores, keys))
                dv += mm(probs.astype(BF), grads[head], TN)
                dk += mm(grad_scores, queries[head], TN)
            put(gqkv_ref, group, pair, (jnp.where(low, found[0], found[1]) * HEAD**-0.5).astype(BF))
            put(gqkv_ref, group, PAIRS + pair, (dk * HEAD**-0.5).astype(BF))
            put(gqkv_ref, group, 2 * PAIRS + pair, dv.astype(BF))
        return carry

    lax.fori_loop(0, groups, back_group, 0)

    gp = gqkv_ref[...].reshape(tokens, 3 * D)
    qkv_sum[...] += mm(hidden, gp, TN)
    gh_one = mm(gp, wq_ref[...], NT)
    part_ref[0:1] += col_sum(gh_one)
    part_ref[1:2] += col_sum(gh_one * normed)
    g_next = gmid + norm_back(gh_one * scale, normed, rstd)
    g_ref[...] = g_next.astype(BF).reshape(g_ref.shape)

    @pl.when(last)
    def _():
        for total, out_ref in zip(sums, out_refs):
            out_ref[...] = total[...].astype(out_ref.dtype)


def temporal(x, cot, chunk, codes, mods, weights, carried, kind, places):
    clips, frames, spots, _ = x.shape
    block = lambda offset: pl.BlockSpec(
        (None, frames, places, D), lambda c, p: (offset * clips + c, 0, p, 0)
    )
    per_clip = lambda rows: pl.BlockSpec((None, rows, D), lambda c, p: (chunk * clips + c, 0, 0))
    shapes = [(D, 3 * D), (D, D), (D, FF), (FF, D)]
    kept = lambda width, kind: pltpu.VMEM((frames, places, width), kind)
    groups = places // GROUP
    return pl.pallas_call(
        functools.partial(temporal_kernel, len(carried)),
        grid=(clips, spots // places),
        in_specs=[block(0), block(chunk), per_clip(1), per_clip(6)]
        + [weight_spec(*shape, 1) for shape in shapes]
        + [once(shape) for shape in shapes[: len(carried)]],
        out_specs=[block(0), block(0), pl.BlockSpec((None, 16, D), lambda c, p: (c, 0, 0))]
        + [once(shape) for shape in shapes],
        out_shape=[
            jax.ShapeDtypeStruct(x.shape, BF),
            jax.ShapeDtypeStruct(x.shape, BF),
            jax.ShapeDtypeStruct((clips, 16, D), F32),
        ]
        + [jax.ShapeDtypeStruct(shape, kind) for shape in shapes],
        scratch_shapes=[pltpu.VMEM(shape, F32) for shape in shapes]
        + [
            kept(3 * D, BF),
            kept(D, BF),
            pltpu.VMEM((groups * 2 * PAIRS, frames * GROUP, frames * GROUP), BF),
            kept(D, F32),
            kept(D, BF),
            kept(3 * D, BF),
        ],
        compiler_params=params(),
        cost_estimate=cost(36),
        name="temporal",
    )(x, cot, codes, mods, *weights, *carried)


def embed_steps(timesteps):
    half_width = D // 2
    frequencies = jnp.exp(
        -math.log(10000.0) * jnp.arange(half_width, dtype=F32) / half_width
    )
    angles = timesteps.astype(F32)[:, None] * frequencies[None, :]
    return jax.nn.silu(jnp.concatenate([jnp.cos(angles), jnp.sin(angles)], axis=-1))


def swap(values):
    return lax.all_to_all(values, "pos", split_axis=0, concat_axis=0, tiled=True)


def spread(values, axes, size):
    copies = jnp.broadcast_to(values[None], (size,) + values.shape)
    return lax.all_to_all(copies, axes, split_axis=0, concat_axis=0, tiled=True)


def scatter_rows(rows, n_pos, n_clip):
    me = lax.axis_index("clip")
    part = rows.shape[0] // n_clip
    parts = rows.reshape(n_clip, part, D)
    total = lax.dynamic_index_in_dim(parts, me, 0, keepdims=False).astype(F32)
    for s in range(1, n_clip):
        shift = [(i, (i + s) % n_clip) for i in range(n_clip)]
        give = lax.dynamic_index_in_dim(parts, (me + s) % n_clip, 0, keepdims=False)
        total += lax.ppermute(give, "clip", shift).astype(F32)
    pieces = swap(total.astype(BF).reshape(n_pos, part // n_pos, D))
    return jnp.sum(pieces.astype(F32), axis=0).astype(BF)


def gather_rows(piece, n_pos, n_clip):
    me = lax.axis_index("clip")
    mine = spread(piece, "pos", n_pos)
    if n_clip == 2:
        other = lax.ppermute(mine, "clip", [(0, 1), (1, 0)])
        return jnp.stack([jnp.where(me == 0, mine, other), jnp.where(me == 0, other, mine)])
    full = jnp.zeros((n_clip,) + mine.shape, mine.dtype)
    full = lax.dynamic_update_index_in_dim(full, mine, me, 0)
    for s in range(1, n_clip):
        got = lax.ppermute(mine, "clip", [(i, (i + s) % n_clip) for i in range(n_clip)])
        full = lax.dynamic_update_index_in_dim(full, got, (me - s) % n_clip, 0)
    return full


def round_up(value, unit):
    return -(-value // unit) * unit


def on_device(
    tokens,
    timesteps,
    weight_codes,
    cotangent,
    ada_weight,
    qkv_weight,
    out_weight,
    up_weight,
    down_weight,
):
    clips, frames, spots, _ = tokens.shape
    n_pos = lax.axis_size("pos")
    n_clip = lax.axis_size("clip")
    chunks = clips * frames // n_pos
    span = clips // chunks
    n = n_pos * spots
    rows = 256
    places = min(spots, 32)

    n_all = n_pos * n_clip
    feed_height = round_up(sum(a * b for a, b in FEED_SHAPES) // D, 16 * n_all)
    if feed_height > 4096:
        feed_height = round_up(sum(a * b for a, b in FEED_SHAPES) // D, n_all)

    def send(c):
        return tokens[c * span : (c + 1) * span].reshape(n_pos, spots, D)

    first = swap(send(0))
    embedded = embed_steps(timesteps)
    mods = [
        jnp.dot(
            embedded, ada_weight[block].astype(F32), precision=lax.Precision.HIGHEST
        ).reshape(clips, 6, D)
        for block in range(2)
    ]
    embed_rows = lax.all_gather(embedded, "clip", axis=0, tiled=True)
    scaling = jnp.exp2(0.5 * weight_codes.astype(F32) - 1.0)
    codes = jnp.broadcast_to(scaling[:, None, None], (clips, 1, D))
    mine = lax.axis_index("pos") // frames
    arrived = [first.reshape(n, D)]
    for c in range(1, chunks):
        later, embed_rows, *mods = lax.optimization_barrier((send(c), embed_rows, *mods))
        arrived.append(swap(later).reshape(n, D))

    kept_all = []
    streams = []
    for c in range(chunks):
        x = arrived[c]
        mod = lax.dynamic_index_in_dim(mods[0], c * span + mine, 0, keepdims=False)
        qkv = project(x, mod, qkv_weight, rows)
        att, logs = attend(qkv, 512)
        x_next, *kept, squares = feed(x, att, mod, out_weight, up_weight, down_weight, rows)
        streams.append(swap(x_next.reshape(n_pos, spots, D)).reshape(span, frames, spots, D))
        kept_all.append((x, mod, qkv, att, logs, kept, squares))

    weights = (qkv_weight, out_weight, up_weight, down_weight)
    results, returned, parts_one = [], [], []
    carried = ()
    for c in range(chunks):
        kind = BF if c == chunks - 1 else F32
        result, g, part, *carried = temporal(
            streams[c], cotangent, c, codes, mods[1], weights, carried, kind, places
        )
        results.append(result)
        parts_one.append(part)
        returned.append(swap(g.reshape(n_pos, spots, D)).reshape(n, D))
    sums_one = carried

    axes = ("pos", "clip")
    part_one = jnp.concatenate(parts_one, axis=0)
    squares_zero = sum(kept[-1] for kept in kept_all)[:3]
    squares_one = jnp.sum(part_one[:, 6:9], axis=0)
    squares = jnp.concatenate([squares_zero, squares_one], axis=0)

    def back_of_feed(c, g, carried):
        x, mod, qkv, att, logs, kept, squares = kept_all[c]
        kind = BF if c == chunks - 1 else F32
        weights = (out_weight, up_weight, down_weight)
        return feed_back(g, kept, att, mod, *weights, carried, kind, rows, feed_height)

    def last_block_back(squares, part_one, later, kept_all, middle, carried):
        squares_all = spread(jnp.sum(squares, axis=1).reshape(1, 6), axes, n_all)

        middles = [middle]
        parts_zero = []
        for c in range(1, chunks):
            gmid, gatt, part, *carried = back_of_feed(c, later[c - 1], carried)
            middles.append((gmid, gatt, part))
        feed_piece = scatter_rows(carried[0], n_pos, n_clip)

        carried = ()
        grads = []
        for c in range(chunks):
            kind = BF if c == chunks - 1 else F32
            x, mod, qkv, att, logs, kept, squares = kept_all[c]
            gmid, gatt, part = middles[c]
            found = attend_back(qkv, att, logs, gatt, 256)
            g, part_first, *carried = project_back(
                x, found, gmid, mod, qkv_weight, carried, kind, rows
            )
            grads.append(
                swap(g.reshape(n_pos, spots, D)).reshape(span, frames, spots, D)
            )
            parts_zero.append(part[:6] + part_first[:6])

        own = lax.axis_index("clip") * clips
        mod_all = jnp.zeros((2, n_clip * clips, 6, D), F32)
        for c in range(chunks):
            mod_all = lax.dynamic_update_slice(
                mod_all, parts_zero[c][None, None], (0, own + c * span + mine, 0, 0)
            )
        mod_all = lax.dynamic_update_slice(mod_all, part_one[None, :, :6], (1, own, 0, 0))
        tail = jnp.concatenate([carried[0], mod_all.reshape(-1, D).astype(BF)], axis=0)
        fill = round_up(tail.shape[0], 8 * n_all if n_all <= 32 else n_all) - tail.shape[0]
        tail = jnp.pad(tail, ((0, fill), (0, 0)))
        tail, feed_piece, grads[0] = lax.optimization_barrier((tail, feed_piece, grads[0]))
        piece = jnp.concatenate([feed_piece, scatter_rows(tail, n_pos, n_clip)], axis=0)
        full = gather_rows(piece, n_pos, n_clip)
        feed_rows = feed_piece.shape[0]
        feed_sums = full[:, :, :feed_rows].reshape(-1, D)
        tail = full[:, :, feed_rows:].reshape(-1, D)
        return squares_all, feed_sums, jnp.concatenate(grads, axis=0).astype(F32), tail

    def skip(*operands):
        shapes = jax.eval_shape(last_block_back, *operands)
        return jax.tree.map(lambda leaf: jnp.zeros(leaf.shape, leaf.dtype), shapes)

    gmid, gatt, part, *carried = back_of_feed(0, returned[0], ())
    squares_all, feed_sums, grads, tail = lax.cond(
        timesteps[0] >= 0,
        last_block_back,
        skip,
        squares,
        part_one,
        returned[1:],
        kept_all,
        (gmid, gatt, part),
        carried,
    )
    summed_one = lax.psum(tuple(sums_one), axes)

    n_clips = n_clip * clips
    mod_rows = tail[3 * D : 3 * D + 2 * n_clips * 6].astype(F32).reshape(2, n_clips, 6 * D)
    ada_grad = sum(embed_rows[c][None, :, None] * mod_rows[:, c, None, :] for c in range(n_clips))
    squares_total = jnp.sum(squares_all, axis=(0, 1)).reshape(2, 3)
    stream_rms = jnp.sqrt(squares_total / (clips * frames * spots * n_all))
    up_zero, down_zero, out_zero = split_rows(feed_sums, FEED_SHAPES)
    (qkv_zero,) = split_rows(tail, [(D, 3 * D)])
    stacked = [
        jnp.stack([first.astype(F32), second.astype(F32)])
        for first, second in zip((qkv_zero, out_zero, up_zero, down_zero), summed_one)
    ]
    return (
        jnp.concatenate(results, axis=0),
        grads,
        ada_grad,
        *stacked,
        stream_rms,
    )


def solution(mesh):
    placed = (
        P("clip", None, "pos", None),
        P("clip"),
        P("clip"),
        P("clip", None, "pos", None),
        P(),
        P(),
        P(),
        P(),
        P(),
    )
    return jax.shard_map(
        on_device,
        mesh=mesh,
        in_specs=placed,
        out_specs=(
            P("clip", None, "pos", None),
            P("clip", None, "pos", None),
            P(),
            P(),
            P(),
            P(),
            P(),
            P(),
        ),
        check_vma=False,
    )
```

```python
import functools
import math

import jax
import jax.numpy as jnp
from jax import lax
from jax.experimental import pallas as pl
from jax.experimental.pallas import tpu as pltpu
from jax.sharding import PartitionSpec as P

D = 384
HEAD = 64
PAIRS = 3
FF = 1536
EPS = 1e-06
LOG_SCALE = HEAD**-0.5 * math.log2(math.e)
GROUP = 16
FEED_SHAPES = [(D, FF), (FF, D), (D, D)]
VMEM_LIMIT = 56 * 2**20

NN = (((1,), (0,)), ((), ()))
NT = (((1,), (1,)), ((), ()))
TN = (((0,), (0,)), ((), ()))
F32 = jnp.float32
BF = jnp.bfloat16


def mm(left, right, dims=NN):
    return lax.dot_general(left, right, dims, preferred_element_type=F32)


def params():
    return pltpu.CompilerParams(vmem_limit_bytes=VMEM_LIMIT)


def cost(micros):
    return pl.CostEstimate(
        flops=int(micros * 1e9), transcendentals=0, bytes_accessed=int(micros * 3e6)
    )


def norm_rows(values):
    center = values - jnp.mean(values, axis=-1, keepdims=True)
    rstd = lax.rsqrt(jnp.mean(center * center, axis=-1, keepdims=True) + EPS)
    return center * rstd, rstd


def norm_back(grad_normed, normed, rstd):
    mean_grad = jnp.mean(grad_normed, axis=-1, keepdims=True)
    mean_cross = jnp.mean(grad_normed * normed, axis=-1, keepdims=True)
    return rstd * (grad_normed - mean_grad - normed * mean_cross)


def col_sum(values):
    return jnp.sum(values, axis=0, keepdims=True)


def gelu_pair(inner):
    square = inner * inner
    slope = math.sqrt(2.0 / math.pi)
    tanh = jnp.tanh(inner * (slope + (slope * 0.044715) * square))
    half = 0.5 + 0.5 * tanh
    value = inner * half
    grad = half + (value * (1.0 - tanh)) * (slope + (3.0 * 0.044715 * slope) * square)
    return value, grad


def low_lanes():
    return lax.broadcasted_iota(jnp.int32, (1, 2 * HEAD), 1) < HEAD


def both_heads(values, low, fill=0.0):
    other = jnp.full_like(values, fill)
    return (jnp.where(low, values, other), jnp.where(low, other, values))


def whole(shape):
    return pl.BlockSpec(shape, lambda *_: (0,) * len(shape))


def once(shape):
    return pl.BlockSpec(shape, lambda *_: (0,) * len(shape), pipeline_mode=pl.Buffered(1))


def weight_spec(rows, cols, block):
    return pl.BlockSpec((None, rows, cols), lambda *_: (block, 0, 0), pipeline_mode=pl.Buffered(1))


def project_kernel(x_ref, mod_ref, w_ref, out_ref):
    normed, _ = norm_rows(x_ref[...].astype(F32))
    hidden = (normed * (1.0 + mod_ref[1:2]) + mod_ref[0:1]).astype(BF)
    out_ref[...] = mm(hidden, w_ref[...]).astype(BF)


def project(x, mod, qkv_weight, rows):
    n = x.shape[0]
    return pl.pallas_call(
        project_kernel,
        grid=(n // rows,),
        in_specs=[
            pl.BlockSpec((rows, D), lambda i: (i, 0)),
            whole((6, D)),
            weight_spec(D, 3 * D, 0),
        ],
        out_specs=pl.BlockSpec((rows, 3 * D), lambda i: (i, 0)),
        out_shape=jax.ShapeDtypeStruct((n, 3 * D), BF),
        compiler_params=params(),
        cost_estimate=cost(5),
        name="project",
    )(x, mod, qkv_weight)


def attend_kernel(rows, q_ref, k_ref, v_ref, out_ref, log_ref):
    low = low_lanes()
    keys = k_ref[...]
    values = both_heads(v_ref[...], low, 1.0)
    tasks = [(start, head) for start in range(0, q_ref.shape[0], rows) for head in range(2)]

    def score(task):
        start, head = task
        q = q_ref[start : start + rows, :]
        return mm(both_heads(q, low)[head], keys, NT)

    ahead = score(tasks[0])
    mixed, tops = [], []
    for index, (start, head) in enumerate(tasks):
        scores = ahead
        if index + 1 < len(tasks):
            ahead = score(tasks[index + 1])
        top = jnp.max(scores, axis=1, keepdims=True)
        raised = jnp.exp2((scores - top) * LOG_SCALE).astype(BF)
        mixed.append(mm(raised, values[head]))
        tops.append(top * LOG_SCALE)
        if head == 1:
            part = slice(start, start + rows)
            total = pltpu.roll(jnp.where(low, mixed[1], mixed[0]), HEAD, 1)
            out_ref[part, :] = (jnp.where(low, mixed[0], mixed[1]) / total).astype(BF)
            log_ref[part, :] = jnp.where(low, tops[0], tops[1]) + jnp.log2(total)
            mixed, tops = [], []


def attend(qkv, rows):
    n = qkv.shape[0]
    pair = lambda start: pl.BlockSpec((n, 2 * HEAD), lambda p: (0, start + p))
    return pl.pallas_call(
        functools.partial(attend_kernel, rows),
        grid=(PAIRS,),
        in_specs=[pair(0), pair(PAIRS), pair(2 * PAIRS)],
        out_specs=[pair(0), pair(0)],
        out_shape=[jax.ShapeDtypeStruct((n, D), BF), jax.ShapeDtypeStruct((n, D), F32)],
        compiler_params=params(),
        cost_estimate=cost(14),
        name="attend",
    )(qkv, qkv, qkv)


def feed_kernel(
    x_ref,
    att_ref,
    mod_ref,
    wo_ref,
    wu_ref,
    wd_ref,
    next_ref,
    middle_ref,
    branch_ref,
    mlp_ref,
    act_ref,
    slope_ref,
    squares_ref,
):
    @pl.when(pl.program_id(0) == 0)
    def _():
        squares_ref[...] = jnp.zeros_like(squares_ref)

    x = x_ref[...].astype(F32)
    branch = mm(att_ref[...], wo_ref[...])
    gated = mod_ref[2:3] * branch
    middle = x + gated
    normed, _ = norm_rows(middle)
    hidden = (normed * (1.0 + mod_ref[4:5]) + mod_ref[3:4]).astype(BF)
    value, slope = gelu_pair(mm(hidden, wu_ref[...]))
    act = value.astype(BF)
    mlp = mm(act, wd_ref[...])
    fed = mod_ref[5:6] * mlp
    next_ref[...] = (middle + fed).astype(BF)
    middle_ref[...] = middle
    branch_ref[...] = branch.astype(BF)
    mlp_ref[...] = mlp.astype(BF)
    act_ref[...] = act
    slope_ref[...] = slope.astype(BF)
    squares_ref[0:1] += col_sum(x * x)
    squares_ref[1:2] += col_sum(gated * gated)
    squares_ref[2:3] += col_sum(fed * fed)


def feed(x, att, mod, out_weight, up_weight, down_weight, rows):
    n = x.shape[0]
    row = lambda width: pl.BlockSpec((rows, width), lambda i: (i, 0))
    out = lambda width, kind: jax.ShapeDtypeStruct((n, width), kind)
    return pl.pallas_call(
        feed_kernel,
        grid=(n // rows,),
        in_specs=[
            row(D),
            row(D),
            whole((6, D)),
            weight_spec(D, D, 0),
            weight_spec(D, FF, 0),
            weight_spec(FF, D, 0),
        ],
        out_specs=[row(D), row(D), row(D), row(D), row(FF), row(FF), whole((8, D))],
        out_shape=[
            out(D, BF),
            out(D, F32),
            out(D, BF),
            out(D, BF),
            out(FF, BF),
            out(FF, BF),
            jax.ShapeDtypeStruct((8, D), F32),
        ],
        compiler_params=params(),
        cost_estimate=cost(11),
        name="feed",
    )(x, att, mod, out_weight, up_weight, down_weight)


def start_sums(sums, carried):
    for index, total in enumerate(sums):
        total[...] = carried[index][...].astype(F32) if carried else jnp.zeros_like(total)


def row_blocks(total):
    height, width = total.shape
    return [(start, height) for start in range(0, width, D)]


def load_rows(rows_ref, sums):
    at = 0
    for total in sums:
        for start, height in row_blocks(total):
            total[:, start : start + D] = rows_ref[at : at + height].astype(F32)
            at += height


def store_rows(sums, rows_ref, extra=None):
    at = 0
    for total in sums:
        for start, height in row_blocks(total):
            rows_ref[at : at + height] = total[:, start : start + D].astype(rows_ref.dtype)
            at += height
    if extra is not None:
        rows_ref[at : at + extra.shape[0]] = extra.astype(rows_ref.dtype)
        at += extra.shape[0]
    if at < rows_ref.shape[0]:
        rows_ref[at:] = jnp.zeros((rows_ref.shape[0] - at, D), rows_ref.dtype)


def store_parts(where_ref, held_ref, rows_refs):
    part = rows_refs[0].shape[0]
    for s, rows_ref in enumerate(rows_refs):
        start = pl.multiple_of((where_ref[1] ^ s) * part, part)
        rows_ref[...] = held_ref[pl.ds(start, part)]


def feed_back_kernel(n_carried, n_parts, where_ref, extra_ref, *refs):
    (
        g_ref,
        middle_ref,
        branch_ref,
        mlp_ref,
        act_ref,
        slope_ref,
        att_ref,
        mod_ref,
        wo_ref,
        wu_ref,
        wd_ref,
    ) = refs[:11]
    carried = refs[11 : 11 + n_carried]
    gmid_ref, gatt_ref, part_ref = refs[11 + n_carried : 14 + n_carried]
    n_out = max(n_parts, 1)
    rows_refs = refs[14 + n_carried : 14 + n_carried + n_out]
    *sums, held_ref = refs[14 + n_carried + n_out :]

    @pl.when(pl.program_id(0) == 0)
    def _():
        part_ref[...] = jnp.zeros_like(part_ref)
        if carried:
            load_rows(carried[0], sums)
        else:
            start_sums(sums, ())

    up_sum, down_sum, out_sum = sums
    g = g_ref[...].astype(F32)
    part_ref[5:6] += col_sum(mlp_ref[...].astype(F32) * g)
    gm = (mod_ref[5:6] * g).astype(BF)
    down_sum[...] += mm(act_ref[...], gm, TN)
    gi = (slope_ref[...].astype(F32) * mm(gm, wd_ref[...], NT)).astype(BF)
    normed, rstd = norm_rows(middle_ref[...])
    scale = 1.0 + mod_ref[4:5]
    hidden = (normed * scale + mod_ref[3:4]).astype(BF)
    up_sum[...] += mm(hidden, gi, TN)
    gh = mm(gi, wu_ref[...], NT)
    part_ref[3:4] += col_sum(gh)
    part_ref[4:5] += col_sum(gh * normed)
    gmid = g + norm_back(gh * scale, normed, rstd)
    gmid_ref[...] = gmid
    part_ref[2:3] += col_sum(branch_ref[...].astype(F32) * gmid)
    gb = (mod_ref[2:3] * gmid).astype(BF)
    out_sum[...] += mm(att_ref[...], gb, TN)
    gatt_ref[...] = mm(gb, wo_ref[...], NT).astype(BF)

    @pl.when(pl.program_id(0) == pl.num_programs(0) - 1)
    def _():
        if n_parts == 0:
            store_rows(sums, rows_refs[0])
        else:
            store_rows(sums, held_ref, extra_ref[...])
            store_parts(where_ref, held_ref, rows_refs)


def feed_back(where, extra, g, kept, att, mod, out_weight, up_weight, down_weight, carried, kind, rows, height, n_parts):
    n = g.shape[0]
    row = lambda width: pl.BlockSpec((rows, width), lambda i, *_: (i, 0))
    shapes = FEED_SHAPES
    n_out = max(n_parts, 1)
    return pl.pallas_call(
        functools.partial(feed_back_kernel, len(carried), n_parts),
        grid=(n // rows,),
        in_specs=[
            pl.BlockSpec(memory_space=pltpu.SMEM),
            whole(extra.shape),
            row(D),
            row(D),
            row(D),
            row(D),
            row(FF),
            row(FF),
            row(D),
            whole((6, D)),
            weight_spec(D, D, 0),
            weight_spec(D, FF, 0),
            weight_spec(FF, D, 0),
        ]
        + [once((height, D))] * len(carried),
        out_specs=[row(D), row(D), whole((8, D)), once((height // n_out, D))]
        + [once((height // n_out, D))] * (n_out - 1),
        out_shape=[
            jax.ShapeDtypeStruct((n, D), F32),
            jax.ShapeDtypeStruct((n, D), BF),
            jax.ShapeDtypeStruct((8, D), F32),
        ]
        + [jax.ShapeDtypeStruct((height // n_out, D), kind)] * n_out,
        scratch_shapes=[pltpu.VMEM(shape, F32) for shape in shapes] + [pltpu.VMEM((height, D), BF)],
        compiler_params=params(),
        cost_estimate=cost(16),
        name="feed_back",
    )(where, extra, g, *kept, att, mod, out_weight, up_weight, down_weight, *carried)


def attend_back_kernel(
    rows, q_ref, k_ref, v_ref, o_ref, log_ref, g_ref, dq_ref, dk_ref, dv_ref
):
    low = low_lanes()
    keys, values = k_ref[...], v_ref[...]
    tasks = [(start, head) for start in range(0, q_ref.shape[0], rows) for head in range(2)]

    def begin(task):
        start, head = task
        part = slice(start, start + rows)
        query = both_heads(q_ref[part, :], low)[head]
        grad = both_heads(g_ref[part, :], low)[head]
        return query, grad, mm(query, keys, NT), mm(grad, values, NT)

    ahead = begin(tasks[0])
    found = []
    for index, (start, head) in enumerate(tasks):
        query, grad, scores, grad_probs = ahead
        if index + 1 < len(tasks):
            ahead = begin(tasks[index + 1])
        part = slice(start, start + rows)
        delta = jnp.sum(grad.astype(F32) * o_ref[part, :].astype(F32), axis=1, keepdims=True)
        log = log_ref[part, HEAD * head : HEAD * head + 1]
        probs = jnp.exp2(scores * LOG_SCALE - log)
        grad_scores = (probs * (grad_probs - delta)).astype(BF)
        found.append(mm(grad_scores, keys))
        values_part = mm(grad.T, probs.astype(BF))
        keys_part = mm(query.T, grad_scores)
        dv = values_part if index == 0 else dv + values_part
        dk = keys_part if index == 0 else dk + keys_part
        if head == 1:
            dq_ref[part, :] = (jnp.where(low, found[0], found[1]) * HEAD**-0.5).astype(BF)
            found = []
    dk_ref[...] = (dk * HEAD**-0.5).T.astype(BF)
    dv_ref[...] = dv.T.astype(BF)


def attend_back(qkv, att, logs, grad, first, count, rows):
    n = qkv.shape[0]
    pair = lambda start: pl.BlockSpec((n, 2 * HEAD), lambda p: (0, start + p))
    return pl.pallas_call(
        functools.partial(attend_back_kernel, rows),
        grid=(count,),
        in_specs=[pair(third * PAIRS + first) for third in (0, 1, 2, 0, 0, 0)],
        out_specs=[pair(0)] * 3,
        out_shape=[jax.ShapeDtypeStruct((n, count * 2 * HEAD), BF)] * 3,
        compiler_params=params(),
        cost_estimate=cost(5 * count),
        name="attend_back",
    )(qkv, qkv, qkv, att, logs, grad)


def project_back_kernel(n_grads, n_carried, n_parts, where_ref, mods_ref, *refs):
    grad_refs, refs = refs[:n_grads], refs[n_grads:]
    x_ref, gmid_ref, mod_ref, w_ref = refs[:4]
    carried = refs[4 : 4 + n_carried]
    out_ref, part_ref = refs[4 + n_carried : 6 + n_carried]
    *rows_refs, total, held_ref, mods_sum = refs[6 + n_carried :]

    @pl.when(pl.program_id(0) == 0)
    def _():
        part_ref[...] = jnp.zeros_like(part_ref)
        if carried:
            load_rows(carried[0], [total])
        else:
            start_sums([total], ())

    normed, rstd = norm_rows(x_ref[...].astype(F32))
    scale = 1.0 + mod_ref[1:2]
    hidden = (normed * scale + mod_ref[0:1]).astype(BF)
    gp = jnp.concatenate([ref[...] for ref in grad_refs], axis=1)
    total[...] += mm(hidden, gp, TN)
    gh = mm(gp, w_ref[...], NT)
    part_ref[0:1] += col_sum(gh)
    part_ref[1:2] += col_sum(gh * normed)
    out_ref[...] = (gmid_ref[...] + norm_back(gh * scale, normed, rstd)).astype(BF)

    @pl.when(pl.program_id(0) == pl.num_programs(0) - 1)
    def _():
        if n_parts == 0:
            store_rows([total], rows_refs[0])
        else:
            mods_sum[...] = mods_ref[...]
            for k in range(2):
                mods_sum[pl.ds(where_ref[2] + k, 1)] += part_ref[k : k + 1]
            store_rows([total], held_ref, mods_sum[...])
            store_parts(where_ref, held_ref, rows_refs)


def project_back(where, mods, x, grads, gmid, mod, qkv_weight, carried, rows, height, n_parts):
    n = x.shape[0]
    row = lambda width: pl.BlockSpec((rows, width), lambda i: (i, 0))
    n_out = max(n_parts, 1)
    if n_parts == 0:
        height = 3 * D
    return pl.pallas_call(
        functools.partial(project_back_kernel, len(grads), len(carried), n_parts),
        grid=(n // rows,),
        in_specs=[pl.BlockSpec(memory_space=pltpu.SMEM), whole(mods.shape)]
        + [row(grad.shape[1]) for grad in grads]
        + [row(D), row(D), whole((6, D)), weight_spec(D, 3 * D, 0)]
        + [once((3 * D, D))] * len(carried),
        out_specs=[row(D), whole((8, D))] + [once((height // n_out, D))] * n_out,
        out_shape=[
            jax.ShapeDtypeStruct((n, D), BF),
            jax.ShapeDtypeStruct((8, D), F32),
        ]
        + [jax.ShapeDtypeStruct((height // n_out, D), BF)] * n_out,
        scratch_shapes=[
            pltpu.VMEM((D, 3 * D), F32),
            pltpu.VMEM((height, D), BF),
            pltpu.VMEM(mods.shape, F32),
        ],
        compiler_params=params(),
        cost_estimate=cost(4),
        name="project_back",
    )(where, mods, *grads, x, gmid, mod, qkv_weight, *carried)


def temporal_kernel(n_carried, n_before, *refs):
    x_ref, cot_ref, code_ref, mod_ref, wq_ref, wo_ref, wu_ref, wd_ref = refs[:8]
    carried = refs[8 : 8 + n_carried]
    refs = refs[8 + n_carried + n_before :]
    act_out_ref, g_ref, part_ref = refs[:3]
    out_refs = refs[3:7]
    sums = refs[7:11]
    qkv_ref, att_ref, probs_ref, inv_ref, gatt_ref, gqkv_ref = refs[11:]
    frames, places = x_ref.shape[0], x_ref.shape[1]
    tokens = frames * places
    wide = frames * GROUP
    first = jnp.logical_and(pl.program_id(0) == 0, pl.program_id(1) == 0)
    last = jnp.logical_and(
        pl.program_id(0) == pl.num_programs(0) - 1, pl.program_id(1) == pl.num_programs(1) - 1
    )

    @pl.when(first)
    def _():
        start_sums(sums, carried)

    @pl.when(pl.program_id(1) == 0)
    def _():
        part_ref[...] = jnp.zeros_like(part_ref)

    qkv_sum, out_sum, up_sum, down_sum = sums
    low = low_lanes()
    mod = mod_ref[...]
    x = x_ref[...].reshape(tokens, D).astype(F32)
    normed, rstd = norm_rows(x)
    scale = 1.0 + mod[1:2]
    hidden = (normed * scale + mod[0:1]).astype(BF)
    qkv_ref[...] = mm(hidden, wq_ref[...]).astype(BF).reshape(qkv_ref.shape)

    place = lambda axis: lax.broadcasted_iota(jnp.int32, (wide, wide), axis) % GROUP
    same = place(0) == place(1)
    groups = places // GROUP

    def cut(ref, group, column):
        rows = slice(group * GROUP, (group + 1) * GROUP)
        return ref[:, rows, column * 2 * HEAD : (column + 1) * 2 * HEAD].reshape(wide, 2 * HEAD)

    def put(ref, group, column, value):
        rows = slice(group * GROUP, (group + 1) * GROUP)
        ref[:, rows, column * 2 * HEAD : (column + 1) * 2 * HEAD] = value.reshape(
            frames, GROUP, 2 * HEAD
        )

    tasks = [(g, pair, head) for g in range(groups) for pair in range(PAIRS) for head in range(2)]

    def score(task):
        group, pair, head = task
        query = both_heads(cut(qkv_ref, group, pair), low)[head]
        return mm(query, cut(qkv_ref, group, PAIRS + pair), NT)

    ahead = score(tasks[0])
    mixed = []
    for index, (group, pair, head) in enumerate(tasks):
        scores = jnp.where(same, ahead, -1e38)
        if index + 1 < len(tasks):
            ahead = score(tasks[index + 1])
        top = jnp.max(scores, axis=1, keepdims=True)
        raised = jnp.exp2((scores - top) * LOG_SCALE).astype(BF)
        probs_ref[index] = raised
        mixed.append(mm(raised, both_heads(cut(qkv_ref, group, 2 * PAIRS + pair), low, 1.0)[head]))
        if head == 1:
            inverse = 1.0 / pltpu.roll(jnp.where(low, mixed[1], mixed[0]), HEAD, 1)
            put(inv_ref, group, pair, inverse)
            put(att_ref, group, pair, (jnp.where(low, mixed[0], mixed[1]) * inverse).astype(BF))
            mixed = []

    att = att_ref[...].reshape(tokens, D)
    branch = mm(att, wo_ref[...])
    gated = mod[2:3] * branch
    middle = x + gated
    normed_two, rstd_two = norm_rows(middle)
    scale_two = 1.0 + mod[4:5]
    hidden_two = (normed_two * scale_two + mod[3:4]).astype(BF)
    value, slope = gelu_pair(mm(hidden_two, wu_ref[...]))
    act = value.astype(BF)
    mlp = mm(act, wd_ref[...])
    fed = mod[5:6] * mlp
    act_out_ref[...] = (middle + fed).astype(BF).reshape(act_out_ref.shape)
    part_ref[6:7] += col_sum(x * x)
    part_ref[7:8] += col_sum(gated * gated)
    part_ref[8:9] += col_sum(fed * fed)

    g = cot_ref[...].reshape(tokens, D).astype(F32) * code_ref[0:1]
    part_ref[5:6] += col_sum(mlp * g)
    gm = (mod[5:6] * g).astype(BF)
    down_sum[...] += mm(act, gm, TN)
    gi = (slope * mm(gm, wd_ref[...], NT)).astype(BF)
    up_sum[...] += mm(hidden_two, gi, TN)
    gh = mm(gi, wu_ref[...], NT)
    part_ref[3:4] += col_sum(gh)
    part_ref[4:5] += col_sum(gh * normed_two)
    gmid = g + norm_back(gh * scale_two, normed_two, rstd_two)
    part_ref[2:3] += col_sum(branch * gmid)
    gb = (mod[2:3] * gmid).astype(BF)
    out_sum[...] += mm(att, gb, TN)
    gatt_ref[...] = mm(gb, wo_ref[...], NT).astype(BF).reshape(gatt_ref.shape)

    def begin(task):
        group, pair, head = task
        grad = both_heads(cut(gatt_ref, group, pair), low)[head]
        return grad, mm(grad, cut(qkv_ref, group, 2 * PAIRS + pair), NT)

    ahead = begin(tasks[0])
    found = []
    for index, (group, pair, head) in enumerate(tasks):
        grad, grad_probs = ahead
        if index + 1 < len(tasks):
            ahead = begin(tasks[index + 1])
        query = both_heads(cut(qkv_ref, group, pair), low)[head]
        cross = grad.astype(F32) * cut(att_ref, group, pair).astype(F32)
        delta = jnp.sum(cross, axis=1, keepdims=True)
        inverse = cut(inv_ref, group, pair)[:, HEAD * head : HEAD * head + 1]
        probs = probs_ref[index].astype(F32) * inverse
        grad_scores = (probs * (grad_probs - delta)).astype(BF)
        found.append(mm(grad_scores, cut(qkv_ref, group, PAIRS + pair)))
        values_part = mm(grad.T, probs.astype(BF))
        keys_part = mm(query.T, grad_scores)
        if head == 0:
            dv, dk = values_part, keys_part
        else:
            dq = jnp.where(low, found[0], found[1])
            put(gqkv_ref, group, pair, (dq * HEAD**-0.5).astype(BF))
            put(gqkv_ref, group, PAIRS + pair, ((dk + keys_part) * HEAD**-0.5).T.astype(BF))
            put(gqkv_ref, group, 2 * PAIRS + pair, (dv + values_part).T.astype(BF))
            found = []

    gp = gqkv_ref[...].reshape(tokens, 3 * D)
    qkv_sum[...] += mm(hidden, gp, TN)
    gh_one = mm(gp, wq_ref[...], NT)
    part_ref[0:1] += col_sum(gh_one)
    part_ref[1:2] += col_sum(gh_one * normed)
    g_next = gmid + norm_back(gh_one * scale, normed, rstd)
    g_ref[...] = g_next.astype(BF).reshape(g_ref.shape)

    @pl.when(last)
    def _():
        for total, out_ref in zip(sums, out_refs):
            out_ref[...] = total[...].astype(out_ref.dtype)


def temporal(x, cot, chunk, codes, mods, weights, carried, before, kind, places):
    clips, frames, spots, _ = x.shape
    block = lambda offset: pl.BlockSpec(
        (None, frames, places, D), lambda c, p: (offset * clips + c, 0, p, 0)
    )
    per_clip = lambda rows: pl.BlockSpec((None, rows, D), lambda c, p: (chunk * clips + c, 0, 0))
    shapes = [(D, 3 * D), (D, D), (D, FF), (FF, D)]
    kept = lambda width, kind: pltpu.VMEM((frames, places, width), kind)
    groups = places // GROUP
    return pl.pallas_call(
        functools.partial(temporal_kernel, len(carried), len(before)),
        grid=(clips, spots // places),
        in_specs=[block(0), block(chunk), per_clip(1), per_clip(6)]
        + [weight_spec(*shape, 1) for shape in shapes]
        + [once(shape) for shape in shapes[: len(carried)]]
        + [pl.BlockSpec(memory_space=pl.ANY)] * len(before),
        out_specs=[block(chunk), block(0), pl.BlockSpec((None, 16, D), lambda c, p: (c, 0, 0))]
        + [once(shape) for shape in shapes],
        out_shape=[
            jax.ShapeDtypeStruct(cot.shape, BF),
            jax.ShapeDtypeStruct(x.shape, BF),
            jax.ShapeDtypeStruct((clips, 16, D), F32),
        ]
        + [jax.ShapeDtypeStruct(shape, kind) for shape in shapes],
        scratch_shapes=[pltpu.VMEM(shape, F32) for shape in shapes]
        + [
            kept(3 * D, BF),
            kept(D, BF),
            pltpu.VMEM((groups * 2 * PAIRS, frames * GROUP, frames * GROUP), BF),
            kept(D, F32),
            kept(D, BF),
            kept(3 * D, BF),
        ],
        compiler_params=params(),
        cost_estimate=cost(36),
        name="temporal",
        input_output_aliases={8 + len(carried): 0} if before else {},
    )(x, cot, codes, mods, *weights, *carried, *before)


def embed_steps(timesteps):
    half_width = D // 2
    frequencies = jnp.exp(
        -math.log(10000.0) * jnp.arange(half_width, dtype=F32) / half_width
    )
    angles = timesteps.astype(F32)[:, None] * frequencies[None, :]
    return jax.nn.silu(jnp.concatenate([jnp.cos(angles), jnp.sin(angles)], axis=-1))


def swap(values):
    return lax.all_to_all(values, "pos", split_axis=0, concat_axis=0, tiled=True)


def sum_clips(parts):
    total = parts[0].astype(F32)
    for s, give in enumerate(parts[1:], 1):
        total += exchange(give, "clip", len(parts), s).astype(F32)
    return total.astype(BF)


def sum_positions(part, n_pos):
    pieces = swap(part.reshape(n_pos, part.shape[0] // n_pos, D))
    return jnp.sum(pieces.astype(F32), axis=0).astype(BF)


INNER = 4


def exchange(values, axis, size, distance):
    return lax.ppermute(values, axis, [(i, i ^ distance) for i in range(size)])


def gather_outer(piece, n_pos):
    rest = [exchange(piece, "pos", n_pos, k * INNER) for k in range(1, n_pos // INNER)]
    return jnp.stack([piece] + rest)


def gather_inner(pieces, n_pos):
    rest = [exchange(pieces, "pos", n_pos, k) for k in range(1, INNER)]
    return jnp.stack([pieces] + rest)


def gather_clips(pieces, n_clip):
    return [pieces] + [exchange(pieces, "clip", n_clip, k) for k in range(1, n_clip)]


def place_pieces(where_ref, piece_refs, rows_ref):
    inner, outer, height, _ = piece_refs[0].shape
    for s, piece_ref in enumerate(piece_refs):
        clip = where_ref[1] ^ s
        for p in range(inner * outer):
            owner = where_ref[0] ^ p
            row = (clip * (inner * outer) + owner) * height
            rows_ref[pl.ds(pl.multiple_of(row, height), height)] = piece_ref[p % inner, p // inner]


def unstack(rows_ref, at, out_ref):
    height, width = out_ref.shape
    for start in range(0, width, D):
        out_ref[:, start : start + D] = rows_ref[at : at + height].astype(F32)
        at += height
    return at


def first_block(shape):
    return pl.BlockSpec((None,) + shape, lambda *_: (0, 0, 0))


def outer_products(embed_ref, rows_ref, first, ada_ref):
    n_clips = embed_ref.shape[1]
    for part in range(6):
        total = 0.0
        for clip in range(n_clips):
            row = first + clip * 6 + part
            total += embed_ref[:, clip : clip + 1] * rows_ref[row : row + 1].astype(F32)
        ada_ref[:, part * D : (part + 1) * D] = total


def finish_feed_kernel(n_pieces, where_ref, *refs):
    pieces, embed_ref = refs[:n_pieces], refs[n_pieces]
    *outs, ada_ref, rest_ref, rows_ref = refs[n_pieces + 1 :]
    place_pieces(where_ref, pieces, rows_ref)
    at = 0
    for out_ref in outs:
        at = unstack(rows_ref, at, out_ref)
    outer_products(embed_ref, rows_ref, at, ada_ref)
    at += embed_ref.shape[1] * 6
    rest_ref[...] = rows_ref[at : at + rest_ref.shape[0]].astype(F32)


def block_of(shape, block):
    return pl.BlockSpec((None,) + shape, lambda *_: (block, 0, 0))


def finish_feed(where, pieces, embed_columns, rest_rows):
    height = len(pieces) * math.prod(pieces[0].shape[:3])
    ada = (D, 6 * D)
    return pl.pallas_call(
        functools.partial(finish_feed_kernel, len(pieces)),
        grid_spec=pltpu.PrefetchScalarGridSpec(
            num_scalar_prefetch=1,
            grid=(1,),
            in_specs=[once(piece.shape) for piece in pieces] + [once(embed_columns.shape)],
            out_specs=[block_of(shape, 0) for shape in FEED_SHAPES]
            + [block_of(ada, 1), whole((rest_rows, D))],
            scratch_shapes=[pltpu.VMEM((height, D), BF)],
        ),
        out_shape=[jax.ShapeDtypeStruct((2,) + shape, F32) for shape in FEED_SHAPES + [ada]]
        + [jax.ShapeDtypeStruct((rest_rows, D), F32)],
        compiler_params=params(),
        cost_estimate=cost(5),
        name="finish_feed",
    )(where, *pieces, embed_columns)


def finish_kernel(n_pieces, chunks, where_ref, *refs):
    pieces, refs = refs[:n_pieces], refs[n_pieces:]
    embed_ref, qkv_one_ref, *ones = refs[:5]
    grads = refs[5 : 5 + chunks]
    qkv_ref, ada_ref, *outs, grad_ref, rows_ref = refs[9 + chunks :]
    step = pl.program_id(0)

    @pl.when(step == 0)
    def _():
        place_pieces(where_ref, pieces, rows_ref)

    height = qkv_ref.shape[1]
    for part in range(3):
        start = pl.multiple_of(part * D + step * height, height)
        block = rows_ref[pl.ds(start, height)].astype(F32)
        qkv_ref[0, :, part * D : (part + 1) * D] = block
    qkv_ref[1] = qkv_one_ref[...].astype(F32)
    outer_products(embed_ref, rows_ref, 3 * D, ada_ref)
    for one_ref, out_ref in zip(ones, outs):
        out_ref[...] = one_ref[...].astype(F32)
    per = pl.num_programs(0) // chunks
    for c, ref in enumerate(grads):

        @pl.when(step // per == c)
        def _():
            grad_ref[...] = ref[...].astype(F32)


def finish(where, pieces, embed_columns, qkv_one, ones, ada, halves, grads):
    chunks = len(grads)
    per = 4 // chunks if chunks in (1, 2, 4) else 1
    steps = per * chunks
    height = len(pieces) * math.prod(pieces[0].shape[:3])
    cut = lambda shape: (shape[0] // steps,) + shape[1:]
    piece = (grads[0].shape[0] // per,) + grads[0].shape[1:]
    chunk = lambda c: pl.BlockSpec(
        piece, lambda i, *_: (jnp.minimum(jnp.maximum(i - c * per, 0), per - 1), 0, 0)
    )
    rows = lambda shape: pl.BlockSpec(cut(shape), lambda i, *_: (i, 0))
    block = lambda shape, b: pl.BlockSpec((None,) + cut(shape), lambda i, *_: (b, i, 0))
    first = len(pieces) + 6 + chunks
    return pl.pallas_call(
        functools.partial(finish_kernel, len(pieces), chunks),
        grid_spec=pltpu.PrefetchScalarGridSpec(
            num_scalar_prefetch=1,
            grid=(steps,),
            in_specs=[once(piece.shape) for piece in pieces]
            + [rows(embed_columns.shape), rows(qkv_one.shape)]
            + [rows(one.shape) for one in ones]
            + [chunk(c) for c in range(chunks)]
            + [pl.BlockSpec(memory_space=pl.ANY)] * (1 + len(halves)),
            out_specs=[
                pl.BlockSpec((2, D // steps, 3 * D), lambda i, *_: (0, i, 0)),
                block((D, 6 * D), 0),
            ]
            + [block(one.shape, 1) for one in ones]
            + [pl.BlockSpec(piece, lambda i, *_: (i, 0, 0))],
            scratch_shapes=[pltpu.VMEM((height, D), BF)],
        ),
        out_shape=[
            jax.ShapeDtypeStruct((2, D, 3 * D), F32),
            jax.ShapeDtypeStruct(ada.shape, F32),
        ]
        + [jax.ShapeDtypeStruct(half.shape, F32) for half in halves]
        + [jax.ShapeDtypeStruct((chunks * grads[0].shape[0],) + grads[0].shape[1:], F32)],
        input_output_aliases={first + k: 1 + k for k in range(1 + len(halves))},
        compiler_params=params(),
        cost_estimate=cost(8),
        name="finish",
    )(where, *pieces, embed_columns, qkv_one, *ones, *grads, ada, *halves)


def round_up(value, unit):
    return -(-value // unit) * unit


def as_one_step(timesteps, function, *operands):
    def skip(*operands):
        shapes = jax.eval_shape(function, *operands)
        return jax.tree.map(lambda leaf: jnp.zeros(leaf.shape, leaf.dtype), shapes)

    return lax.cond(timesteps[0] >= 0, function, skip, *operands)


def on_device(
    tokens,
    timesteps,
    weight_codes,
    cotangent,
    ada_weight,
    qkv_weight,
    out_weight,
    up_weight,
    down_weight,
):
    clips, frames, spots, _ = tokens.shape
    n_pos = lax.axis_size("pos")
    n_clip = lax.axis_size("clip")
    chunks = clips * frames // n_pos
    span = clips // chunks
    n = n_pos * spots
    rows = 512
    places = min(spots, 32)

    n_all = n_pos * n_clip
    n_clips = n_clip * clips
    square_height = round_up(n_all * 18, D) // D
    feed_height = sum(a * b for a, b in FEED_SHAPES) // D + n_clips * 6 + square_height
    feed_height = round_up(feed_height, 16 * n_all)
    tail_height = round_up(3 * D + n_clips * 6, 16 * n_all)
    pos, clip = lax.axis_index("pos"), lax.axis_index("clip")
    mine = pos // frames
    own = clip * clips
    where = [pos, clip, (own + (chunks - 1) * span + mine) * 6, pos % INNER, pos // INNER]
    where = jnp.stack(where).astype(jnp.int32)

    def send(tokens, c):
        return tokens[c * span : (c + 1) * span].reshape(n_pos, spots, D)

    first = swap(send(tokens, 0))
    embedded = embed_steps(timesteps)
    mods = [
        jnp.dot(
            embedded, ada_weight[block].astype(F32), precision=lax.Precision.HIGHEST
        ).reshape(clips, 6, D)
        for block in range(2)
    ]
    embed_rows = lax.all_gather(embedded, "clip", axis=0, tiled=True)
    scaling = jnp.exp2(0.5 * weight_codes.astype(F32) - 1.0)
    codes = jnp.broadcast_to(scaling[:, None, None], (clips, 1, D))
    arrived = [first.reshape(n, D)]
    for c in range(1, chunks):
        held, embed_rows, *mods = lax.optimization_barrier((tokens, embed_rows, *mods))
        arrived.append(swap(send(held, c)).reshape(n, D))

    kept_all = []
    streams = []
    for c in range(chunks):
        x = arrived[c]
        mod = lax.dynamic_index_in_dim(mods[0], c * span + mine, 0, keepdims=False)
        qkv = project(x, mod, qkv_weight, rows)
        att, logs = attend(qkv, 256)
        x_next, *kept, squares = feed(x, att, mod, out_weight, up_weight, down_weight, rows)
        streams.append(swap(x_next.reshape(n_pos, spots, D)).reshape(span, frames, spots, D))
        kept_all.append((x, mod, qkv, att, logs, kept, squares))

    weights = (qkv_weight, out_weight, up_weight, down_weight)
    results, returned, parts_one = (), [], []
    carried = ()
    for c in range(chunks):
        kind = BF
        result, g, part, *carried = temporal(
            streams[c], cotangent, c, codes, mods[1], weights, carried, results, kind, places
        )
        results = (result,)
        parts_one.append(part)
        returned.append(swap(g.reshape(n_pos, spots, D)).reshape(n, D))
    sums_one = carried

    part_one = jnp.concatenate(parts_one, axis=0)
    squares_zero = sum(kept[-1] for kept in kept_all)[:3]
    squares_one = jnp.sum(part_one[:, 6:9], axis=0)
    squares = jnp.sum(jnp.concatenate([squares_zero, squares_one], axis=0), axis=1)
    terms = []
    for _ in range(3):
        terms.append(squares.astype(BF))
        squares = squares - terms[-1].astype(F32)
    square_rows = lax.dynamic_update_slice(
        jnp.zeros((square_height * D,), BF), jnp.concatenate(terms), ((pos * n_clip + clip) * 18,)
    ).reshape(square_height, D)
    mod_one = lax.dynamic_update_slice(
        jnp.zeros((n_clips, 6, D), BF), part_one[:, :6].astype(BF), (own, 0, 0)
    )
    extra = jnp.concatenate([mod_one.reshape(n_clips * 6, D), square_rows], axis=0)

    def back_of_feed(c, g, carried):
        x, mod, qkv, att, logs, kept, squares = kept_all[c]
        weights = (out_weight, up_weight, down_weight)
        n_parts = n_clip if c == chunks - 1 else 0
        return feed_back(
            where, extra, g, kept, att, mod, *weights, carried, BF, 256, feed_height, n_parts
        )

    def back_of_project(c, found, gmid, mods, carried):
        x, mod, qkv, att, logs, kept, squares = kept_all[c]
        n_parts = n_clip if c == chunks - 1 else 0
        found = [third[k] for k in range(3) for third in found]
        g, part, *carried = project_back(
            where, mods, x, found, gmid, mod, qkv_weight, carried, rows, tail_height, n_parts
        )
        return g.reshape(n_pos, spots, D), part[:6], carried

    def some_pairs(c, gatt, first, count):
        x, mod, qkv, att, logs, kept, squares = kept_all[c]
        return attend_back(qkv, att, logs, gatt, first, count, rows)

    def last_block_back(later, middle, found, carried):
        middles = [middle]
        for c in range(1, chunks):
            gmid, gatt, part, *carried = back_of_feed(c, later[c - 1], carried)
            middles.append((gmid, gatt, part))
        feed_part = sum_clips(carried)
        carried = ()
        grads = []
        mods = jnp.zeros((n_clips, 6, D), F32)
        for c, (gmid, gatt, part) in enumerate(middles):
            if c == 0:
                feed_part, gatt = lax.optimization_barrier((feed_part, gatt))
                feed_piece = sum_positions(feed_part, n_pos)
                found = [found]
            else:
                found = [some_pairs(c, gatt, 0, 1)]
            if c == chunks - 1:
                break
            found.append(some_pairs(c, gatt, 1, 2))
            grad, part_first, carried = back_of_project(c, found, gmid, mods.reshape(-1, D), carried)
            grads.append(grad)
            mods = lax.dynamic_update_index_in_dim(
                mods, part[:6] + part_first, own + c * span + mine, 0
            )
        mods = lax.dynamic_update_index_in_dim(mods, part[:6], own + (chunks - 1) * span + mine, 0)
        mods = mods.reshape(-1, D)

        gatt, found, feed_piece, *grads = lax.optimization_barrier((gatt, found, feed_piece, *grads))
        feed_pieces = gather_outer(feed_piece, n_pos)
        found.append(some_pairs(chunks - 1, gatt, 1, 1))
        found, feed_pieces, *grads = lax.optimization_barrier((found, feed_pieces, *grads))
        feed_pieces = gather_inner(feed_pieces, n_pos)
        grads = [swap(grad) for grad in grads]

        def last_step(gatt, found, gmid, mods, carried):
            found = found + [some_pairs(chunks - 1, gatt, 2, 1)]
            grad, _, parts = back_of_project(chunks - 1, found, gmid, mods, carried)
            return grad, sum_clips(parts)

        grad, part = as_one_step(timesteps, last_step, gatt, found, gmid, mods, carried)
        feed_pieces, part, *grads = lax.optimization_barrier((feed_pieces, part, *grads))
        pieces = swap(part.reshape(n_pos, part.shape[0] // n_pos, D))
        embed_columns = embed_rows.T
        *halves, ada_grad, rest = finish_feed(
            where, gather_clips(feed_pieces, n_clip), embed_columns, extra.shape[0] - n_clips * 6
        )
        pieces, ada_grad = lax.optimization_barrier((pieces, ada_grad))
        piece = jnp.sum(pieces.astype(F32), axis=0).astype(BF)
        tail_pieces = gather_outer(piece, n_pos)
        grad, tail_pieces = lax.optimization_barrier((grad, tail_pieces))
        grads.append(swap(grad))
        tail_pieces = gather_clips(gather_inner(tail_pieces, n_pos), n_clip)
        return grads, tail_pieces, embed_columns, ada_grad, rest, halves

    gmid, gatt, part, *carried = back_of_feed(0, returned[0], ())
    found = some_pairs(0, gatt, 0, 1)
    grads, tail_pieces, embed_columns, ada_grad, rest, halves = as_one_step(
        timesteps, last_block_back, returned[1:], (gmid, gatt, part), found, carried
    )
    qkv_one, out_one, up_one, down_one = lax.psum(tuple(sums_one), ("pos", "clip"))
    qkv_grad, ada_grad, up_grad, down_grad, out_grad, grad_tokens = finish(
        where,
        tail_pieces,
        embed_columns,
        qkv_one,
        (up_one, down_one, out_one),
        ada_grad,
        halves,
        grads,
    )
    squares_total = jnp.sum(rest.reshape(-1)[: n_all * 18].reshape(n_all, 3, 6), axis=(0, 1))
    stream_rms = jnp.sqrt(squares_total.reshape(2, 3) / (clips * frames * spots * n_all))
    return (
        results[0],
        grad_tokens.reshape(tokens.shape),
        ada_grad,
        qkv_grad,
        out_grad,
        up_grad,
        down_grad,
        stream_rms,
    )


def solution(mesh):
    placed = (
        P("clip", None, "pos", None),
        P("clip"),
        P("clip"),
        P("clip", None, "pos", None),
        P(),
        P(),
        P(),
        P(),
        P(),
    )
    return jax.shard_map(
        on_device,
        mesh=mesh,
        in_specs=placed,
        out_specs=(
            P("clip", None, "pos", None),
            P("clip", None, "pos", None),
            P(),
            P(),
            P(),
            P(),
            P(),
            P(),
        ),
        check_vma=False,
    )
```

```python
import functools
import math

import jax
import jax.numpy as jnp
from jax import lax
from jax.experimental import pallas as pl
from jax.experimental.pallas import tpu as pltpu
from jax.sharding import PartitionSpec as P

D = 384
HEAD = 64
PAIRS = 3
FF = 1536
EPS = 1e-06
LOG_SCALE = HEAD**-0.5 * math.log2(math.e)
GROUP = 16
FEED_SHAPES = [(D, FF), (FF, D), (D, D)]

NN = (((1,), (0,)), ((), ()))
NT = (((1,), (1,)), ((), ()))
TN = (((0,), (0,)), ((), ()))
F32 = jnp.float32
BF = jnp.bfloat16


def mm(left, right, dims=NN):
    return lax.dot_general(left, right, dims, preferred_element_type=F32)


def params(mebibytes):
    return pltpu.CompilerParams(vmem_limit_bytes=mebibytes * 2**20)


def cost(micros):
    return pl.CostEstimate(
        flops=int(micros * 1e9), transcendentals=0, bytes_accessed=int(micros * 3e6)
    )


def norm_rows(values):
    center = values - jnp.mean(values, axis=-1, keepdims=True)
    rstd = lax.rsqrt(jnp.mean(center * center, axis=-1, keepdims=True) + EPS)
    return center * rstd, rstd


def norm_back(grad_normed, normed, rstd):
    mean_grad = jnp.mean(grad_normed, axis=-1, keepdims=True)
    mean_cross = jnp.mean(grad_normed * normed, axis=-1, keepdims=True)
    return rstd * (grad_normed - mean_grad - normed * mean_cross)


def col_sum(values):
    return jnp.sum(values, axis=0, keepdims=True)


def gelu_pair(inner):
    square = inner * inner
    slope = math.sqrt(2.0 / math.pi)
    tanh = jnp.tanh(inner * (slope + (slope * 0.044715) * square))
    half = 0.5 + 0.5 * tanh
    value = inner * half
    grad = half + (value * (1.0 - tanh)) * (slope + (3.0 * 0.044715 * slope) * square)
    return value, grad


def low_lanes():
    return lax.broadcasted_iota(jnp.int32, (1, 2 * HEAD), 1) < HEAD


def both_heads(values, low, fill=0.0):
    other = jnp.full_like(values, fill)
    return (jnp.where(low, values, other), jnp.where(low, other, values))


def whole(shape):
    return pl.BlockSpec(shape, lambda *_: (0,) * len(shape))


def once(shape):
    return pl.BlockSpec(shape, lambda *_: (0,) * len(shape), pipeline_mode=pl.Buffered(1))


def weight_spec(rows, cols, block):
    return pl.BlockSpec((None, rows, cols), lambda *_: (block, 0, 0), pipeline_mode=pl.Buffered(1))


def project_kernel(x_ref, mod_ref, w_ref, out_ref):
    normed, _ = norm_rows(x_ref[...].astype(F32))
    hidden = (normed * (1.0 + mod_ref[1:2]) + mod_ref[0:1]).astype(BF)
    out_ref[...] = mm(hidden, w_ref[...]).astype(BF)


def project(x, mod, qkv_weight, rows):
    n = x.shape[0]
    return pl.pallas_call(
        project_kernel,
        grid=(n // rows,),
        in_specs=[
            pl.BlockSpec((rows, D), lambda i: (i, 0)),
            whole((6, D)),
            weight_spec(D, 3 * D, 0),
        ],
        out_specs=pl.BlockSpec((rows, 3 * D), lambda i: (i, 0)),
        out_shape=jax.ShapeDtypeStruct((n, 3 * D), BF),
        compiler_params=params(16),
        cost_estimate=cost(5),
        name="project",
    )(x, mod, qkv_weight)


def attend_kernel(rows, q_ref, k_ref, v_ref, out_ref, log_ref):
    low = low_lanes()
    keys = k_ref[...]
    values = both_heads(v_ref[...], low, 1.0)
    tasks = [(start, head) for start in range(0, q_ref.shape[0], rows) for head in range(2)]

    def score(task):
        start, head = task
        q = q_ref[start : start + rows, :]
        return mm(both_heads(q, low)[head], keys, NT)

    ahead = score(tasks[0])
    mixed, tops = [], []
    for index, (start, head) in enumerate(tasks):
        scores = ahead
        if index + 1 < len(tasks):
            ahead = score(tasks[index + 1])
        top = jnp.max(scores, axis=1, keepdims=True)
        raised = jnp.exp2((scores - top) * LOG_SCALE).astype(BF)
        mixed.append(mm(raised, values[head]))
        tops.append(top * LOG_SCALE)
        if head == 1:
            part = slice(start, start + rows)
            total = pltpu.roll(jnp.where(low, mixed[1], mixed[0]), HEAD, 1)
            out_ref[part, :] = (jnp.where(low, mixed[0], mixed[1]) / total).astype(BF)
            log_ref[part, :] = jnp.where(low, tops[0], tops[1]) + jnp.log2(total)
            mixed, tops = [], []


def attend(qkv, rows):
    n = qkv.shape[0]
    pair = lambda start: pl.BlockSpec((n, 2 * HEAD), lambda p: (0, start + p))
    return pl.pallas_call(
        functools.partial(attend_kernel, rows),
        grid=(PAIRS,),
        in_specs=[pair(0), pair(PAIRS), pair(2 * PAIRS)],
        out_specs=[pair(0), pair(0)],
        out_shape=[jax.ShapeDtypeStruct((n, D), BF), jax.ShapeDtypeStruct((n, D), F32)],
        compiler_params=params(24),
        cost_estimate=cost(14),
        name="attend",
    )(qkv, qkv, qkv)


def feed_kernel(
    x_ref,
    att_ref,
    mod_ref,
    wo_ref,
    wu_ref,
    wd_ref,
    next_ref,
    middle_ref,
    branch_ref,
    mlp_ref,
    act_ref,
    slope_ref,
    squares_ref,
):
    @pl.when(pl.program_id(0) == 0)
    def _():
        squares_ref[...] = jnp.zeros_like(squares_ref)

    x = x_ref[...].astype(F32)
    branch = mm(att_ref[...], wo_ref[...])
    gated = mod_ref[2:3] * branch
    middle = x + gated
    normed, _ = norm_rows(middle)
    hidden = (normed * (1.0 + mod_ref[4:5]) + mod_ref[3:4]).astype(BF)
    value, slope = gelu_pair(mm(hidden, wu_ref[...]))
    act = value.astype(BF)
    mlp = mm(act, wd_ref[...])
    fed = mod_ref[5:6] * mlp
    next_ref[...] = (middle + fed).astype(BF)
    middle_ref[...] = middle.astype(BF)
    branch_ref[...] = branch.astype(BF)
    mlp_ref[...] = mlp.astype(BF)
    act_ref[...] = act
    slope_ref[...] = slope.astype(BF)
    squares_ref[0:1] += col_sum(x * x)
    squares_ref[1:2] += col_sum(gated * gated)
    squares_ref[2:3] += col_sum(fed * fed)


def feed(x, att, mod, out_weight, up_weight, down_weight, rows):
    n = x.shape[0]
    row = lambda width: pl.BlockSpec((rows, width), lambda i: (i, 0))
    out = lambda width, kind: jax.ShapeDtypeStruct((n, width), kind)
    return pl.pallas_call(
        feed_kernel,
        grid=(n // rows,),
        in_specs=[
            row(D),
            row(D),
            whole((6, D)),
            weight_spec(D, D, 0),
            weight_spec(D, FF, 0),
            weight_spec(FF, D, 0),
        ],
        out_specs=[row(D), row(D), row(D), row(D), row(FF), row(FF), whole((8, D))],
        out_shape=[
            out(D, BF),
            out(D, BF),
            out(D, BF),
            out(D, BF),
            out(FF, BF),
            out(FF, BF),
            jax.ShapeDtypeStruct((8, D), F32),
        ],
        compiler_params=params(56),
        cost_estimate=cost(11),
        name="feed",
    )(x, att, mod, out_weight, up_weight, down_weight)


def start_sums(sums, carried):
    for index, total in enumerate(sums):
        total[...] = carried[index][...].astype(F32) if carried else jnp.zeros_like(total)


def row_blocks(total):
    height, width = total.shape
    return [(start, height) for start in range(0, width, D)]


def load_rows(rows_ref, sums):
    at = 0
    for total in sums:
        for start, height in row_blocks(total):
            total[:, start : start + D] = rows_ref[at : at + height].astype(F32)
            at += height


def store_rows(sums, rows_ref, extra=None):
    at = 0
    for total in sums:
        for start, height in row_blocks(total):
            rows_ref[at : at + height] = total[:, start : start + D].astype(rows_ref.dtype)
            at += height
    if extra is not None:
        rows_ref[at : at + extra.shape[0]] = extra.astype(rows_ref.dtype)
        at += extra.shape[0]
    if at < rows_ref.shape[0]:
        rows_ref[at:] = jnp.zeros((rows_ref.shape[0] - at, D), rows_ref.dtype)


def store_parts(where_ref, held_ref, rows_refs):
    part = rows_refs[0].shape[0]
    for s, rows_ref in enumerate(rows_refs):
        start = pl.multiple_of((where_ref[1] ^ s) * part, part)
        rows_ref[...] = held_ref[pl.ds(start, part)]


def feed_back_kernel(n_carried, n_parts, where_ref, extra_ref, *refs):
    (
        g_ref,
        middle_ref,
        branch_ref,
        mlp_ref,
        act_ref,
        slope_ref,
        att_ref,
        mod_ref,
        wo_ref,
        wu_ref,
        wd_ref,
    ) = refs[:11]
    carried = refs[11 : 11 + n_carried]
    gmid_ref, gatt_ref, part_ref = refs[11 + n_carried : 14 + n_carried]
    n_out = max(n_parts, 1)
    rows_refs = refs[14 + n_carried : 14 + n_carried + n_out]
    *sums, held_ref = refs[14 + n_carried + n_out :]

    @pl.when(pl.program_id(0) == 0)
    def _():
        part_ref[...] = jnp.zeros_like(part_ref)
        if carried:
            load_rows(carried[0], sums)
        else:
            start_sums(sums, ())

    up_sum, down_sum, out_sum = sums
    g = g_ref[...].astype(F32)
    part_ref[5:6] += col_sum(mlp_ref[...].astype(F32) * g)
    gm = (mod_ref[5:6] * g).astype(BF)
    down_sum[...] += mm(act_ref[...], gm, TN)
    gi = (slope_ref[...].astype(F32) * mm(gm, wd_ref[...], NT)).astype(BF)
    normed, rstd = norm_rows(middle_ref[...].astype(F32))
    scale = 1.0 + mod_ref[4:5]
    hidden = (normed * scale + mod_ref[3:4]).astype(BF)
    up_sum[...] += mm(hidden, gi, TN)
    gh = mm(gi, wu_ref[...], NT)
    part_ref[3:4] += col_sum(gh)
    part_ref[4:5] += col_sum(gh * normed)
    gmid = g + norm_back(gh * scale, normed, rstd)
    gmid_ref[...] = gmid
    part_ref[2:3] += col_sum(branch_ref[...].astype(F32) * gmid)
    gb = (mod_ref[2:3] * gmid).astype(BF)
    out_sum[...] += mm(att_ref[...], gb, TN)
    gatt_ref[...] = mm(gb, wo_ref[...], NT).astype(BF)

    @pl.when(pl.program_id(0) == pl.num_programs(0) - 1)
    def _():
        if n_parts == 0:
            store_rows(sums, rows_refs[0])
        else:
            store_rows(sums, held_ref, extra_ref[...])
            store_parts(where_ref, held_ref, rows_refs)


def feed_back(where, extra, g, kept, att, mod, out_weight, up_weight, down_weight, carried, kind, rows, height, n_parts):
    n = g.shape[0]
    row = lambda width: pl.BlockSpec((rows, width), lambda i, *_: (i, 0))
    shapes = FEED_SHAPES
    n_out = max(n_parts, 1)
    return pl.pallas_call(
        functools.partial(feed_back_kernel, len(carried), n_parts),
        grid=(n // rows,),
        in_specs=[
            pl.BlockSpec(memory_space=pltpu.SMEM),
            whole(extra.shape),
            row(D),
            row(D),
            row(D),
            row(D),
            row(FF),
            row(FF),
            row(D),
            whole((6, D)),
            weight_spec(D, D, 0),
            weight_spec(D, FF, 0),
            weight_spec(FF, D, 0),
        ]
        + [once((height, D))] * len(carried),
        out_specs=[row(D), row(D), whole((8, D)), once((height // n_out, D))]
        + [once((height // n_out, D))] * (n_out - 1),
        out_shape=[
            jax.ShapeDtypeStruct((n, D), F32),
            jax.ShapeDtypeStruct((n, D), BF),
            jax.ShapeDtypeStruct((8, D), F32),
        ]
        + [jax.ShapeDtypeStruct((height // n_out, D), kind)] * n_out,
        scratch_shapes=[pltpu.VMEM(shape, F32) for shape in shapes] + [pltpu.VMEM((height, D), BF)],
        compiler_params=params(56),
        cost_estimate=cost(16),
        name="feed_back",
    )(where, extra, g, *kept, att, mod, out_weight, up_weight, down_weight, *carried)


def attend_back_kernel(
    rows, q_ref, k_ref, v_ref, o_ref, log_ref, g_ref, dq_ref, dk_ref, dv_ref
):
    low = low_lanes()
    keys, values = k_ref[...], v_ref[...]
    tasks = [(start, head) for start in range(0, q_ref.shape[0], rows) for head in range(2)]

    def begin(task):
        start, head = task
        part = slice(start, start + rows)
        query = both_heads(q_ref[part, :], low)[head]
        grad = both_heads(g_ref[part, :], low)[head]
        return query, grad, mm(query, keys, NT), mm(grad, values, NT)

    ahead = begin(tasks[0])
    found = []
    for index, (start, head) in enumerate(tasks):
        query, grad, scores, grad_probs = ahead
        if index + 1 < len(tasks):
            ahead = begin(tasks[index + 1])
        part = slice(start, start + rows)
        delta = jnp.sum(grad.astype(F32) * o_ref[part, :].astype(F32), axis=1, keepdims=True)
        log = log_ref[part, HEAD * head : HEAD * head + 1]
        probs = jnp.exp2(scores * LOG_SCALE - log)
        grad_scores = (probs * (grad_probs - delta)).astype(BF)
        found.append(mm(grad_scores, keys))
        values_part = mm(grad.T, probs.astype(BF))
        keys_part = mm(query.T, grad_scores)
        dv = values_part if index == 0 else dv + values_part
        dk = keys_part if index == 0 else dk + keys_part
        if head == 1:
            dq_ref[part, :] = (jnp.where(low, found[0], found[1]) * HEAD**-0.5).astype(BF)
            found = []
    dk_ref[...] = (dk * HEAD**-0.5).T.astype(BF)
    dv_ref[...] = dv.T.astype(BF)


def attend_back(qkv, att, logs, grad, first, count, rows):
    n = qkv.shape[0]
    pair = lambda start: pl.BlockSpec((n, 2 * HEAD), lambda p: (0, start + p))
    return pl.pallas_call(
        functools.partial(attend_back_kernel, rows),
        grid=(count,),
        in_specs=[pair(third * PAIRS + first) for third in (0, 1, 2, 0, 0, 0)],
        out_specs=[pair(0)] * 3,
        out_shape=[jax.ShapeDtypeStruct((n, count * 2 * HEAD), BF)] * 3,
        compiler_params=params(24),
        cost_estimate=cost(5 * count),
        name="attend_back",
    )(qkv, qkv, qkv, att, logs, grad)


def project_back_kernel(n_grads, n_carried, n_parts, where_ref, mods_ref, *refs):
    grad_refs, refs = refs[:n_grads], refs[n_grads:]
    x_ref, gmid_ref, mod_ref, w_ref = refs[:4]
    carried = refs[4 : 4 + n_carried]
    out_ref, part_ref = refs[4 + n_carried : 6 + n_carried]
    *rows_refs, total, held_ref, mods_sum = refs[6 + n_carried :]

    @pl.when(pl.program_id(0) == 0)
    def _():
        part_ref[...] = jnp.zeros_like(part_ref)
        if carried:
            load_rows(carried[0], [total])
        else:
            start_sums([total], ())

    normed, rstd = norm_rows(x_ref[...].astype(F32))
    scale = 1.0 + mod_ref[1:2]
    hidden = (normed * scale + mod_ref[0:1]).astype(BF)
    gp = jnp.concatenate([ref[...] for ref in grad_refs], axis=1)
    total[...] += mm(hidden, gp, TN)
    gh = mm(gp, w_ref[...], NT)
    part_ref[0:1] += col_sum(gh)
    part_ref[1:2] += col_sum(gh * normed)
    out_ref[...] = (gmid_ref[...] + norm_back(gh * scale, normed, rstd)).astype(BF)

    @pl.when(pl.program_id(0) == pl.num_programs(0) - 1)
    def _():
        if n_parts == 0:
            store_rows([total], rows_refs[0])
        else:
            mods_sum[...] = mods_ref[...]
            for k in range(2):
                mods_sum[pl.ds(where_ref[2] + k, 1)] += part_ref[k : k + 1]
            store_rows([total], held_ref, mods_sum[...])
            store_parts(where_ref, held_ref, rows_refs)


def project_back(where, mods, x, grads, gmid, mod, qkv_weight, carried, rows, height, n_parts):
    n = x.shape[0]
    row = lambda width: pl.BlockSpec((rows, width), lambda i: (i, 0))
    n_out = max(n_parts, 1)
    if n_parts == 0:
        height = 3 * D
    return pl.pallas_call(
        functools.partial(project_back_kernel, len(grads), len(carried), n_parts),
        grid=(n // rows,),
        in_specs=[pl.BlockSpec(memory_space=pltpu.SMEM), whole(mods.shape)]
        + [row(grad.shape[1]) for grad in grads]
        + [row(D), row(D), whole((6, D)), weight_spec(D, 3 * D, 0)]
        + [once((3 * D, D))] * len(carried),
        out_specs=[row(D), whole((8, D))] + [once((height // n_out, D))] * n_out,
        out_shape=[
            jax.ShapeDtypeStruct((n, D), BF),
            jax.ShapeDtypeStruct((8, D), F32),
        ]
        + [jax.ShapeDtypeStruct((height // n_out, D), BF)] * n_out,
        scratch_shapes=[
            pltpu.VMEM((D, 3 * D), F32),
            pltpu.VMEM((height, D), BF),
            pltpu.VMEM(mods.shape, F32),
        ],
        compiler_params=params(24),
        cost_estimate=cost(4),
        name="project_back",
    )(where, mods, *grads, x, gmid, mod, qkv_weight, *carried)


def temporal_kernel(n_carried, n_before, *refs):
    x_ref, cot_ref, code_ref, mod_ref, wq_ref, wo_ref, wu_ref, wd_ref = refs[:8]
    carried = refs[8 : 8 + n_carried]
    refs = refs[8 + n_carried + n_before :]
    act_out_ref, g_ref, part_ref = refs[:3]
    out_refs = refs[3:7]
    sums = refs[7:11]
    qkv_ref, att_ref, probs_ref, inv_ref, gatt_ref, gqkv_ref = refs[11:]
    frames, places = x_ref.shape[0], x_ref.shape[1]
    tokens = frames * places
    wide = frames * GROUP
    first = jnp.logical_and(pl.program_id(0) == 0, pl.program_id(1) == 0)
    last = jnp.logical_and(
        pl.program_id(0) == pl.num_programs(0) - 1, pl.program_id(1) == pl.num_programs(1) - 1
    )

    @pl.when(first)
    def _():
        start_sums(sums, carried)

    @pl.when(pl.program_id(1) == 0)
    def _():
        part_ref[...] = jnp.zeros_like(part_ref)

    qkv_sum, out_sum, up_sum, down_sum = sums
    low = low_lanes()
    mod = mod_ref[...]
    x = x_ref[...].reshape(tokens, D).astype(F32)
    normed, rstd = norm_rows(x)
    scale = 1.0 + mod[1:2]
    hidden = (normed * scale + mod[0:1]).astype(BF)
    qkv_ref[...] = mm(hidden, wq_ref[...]).astype(BF).reshape(qkv_ref.shape)

    place = lambda axis: lax.broadcasted_iota(jnp.int32, (wide, wide), axis) % GROUP
    same = place(0) == place(1)
    groups = places // GROUP

    def cut(ref, group, column):
        rows = slice(group * GROUP, (group + 1) * GROUP)
        return ref[:, rows, column * 2 * HEAD : (column + 1) * 2 * HEAD].reshape(wide, 2 * HEAD)

    def put(ref, group, column, value):
        rows = slice(group * GROUP, (group + 1) * GROUP)
        ref[:, rows, column * 2 * HEAD : (column + 1) * 2 * HEAD] = value.reshape(
            frames, GROUP, 2 * HEAD
        )

    tasks = [(g, pair, head) for g in range(groups) for pair in range(PAIRS) for head in range(2)]

    def score(task):
        group, pair, head = task
        query = both_heads(cut(qkv_ref, group, pair), low)[head]
        return mm(query, cut(qkv_ref, group, PAIRS + pair), NT)

    ahead = score(tasks[0])
    mixed = []
    for index, (group, pair, head) in enumerate(tasks):
        scores = jnp.where(same, ahead, -1e38)
        if index + 1 < len(tasks):
            ahead = score(tasks[index + 1])
        top = jnp.max(scores, axis=1, keepdims=True)
        raised = jnp.exp2((scores - top) * LOG_SCALE).astype(BF)
        probs_ref[index] = raised
        mixed.append(mm(raised, both_heads(cut(qkv_ref, group, 2 * PAIRS + pair), low, 1.0)[head]))
        if head == 1:
            inverse = 1.0 / pltpu.roll(jnp.where(low, mixed[1], mixed[0]), HEAD, 1)
            put(inv_ref, group, pair, inverse)
            put(att_ref, group, pair, (jnp.where(low, mixed[0], mixed[1]) * inverse).astype(BF))
            mixed = []

    att = att_ref[...].reshape(tokens, D)
    branch = mm(att, wo_ref[...])
    gated = mod[2:3] * branch
    middle = x + gated
    normed_two, rstd_two = norm_rows(middle)
    scale_two = 1.0 + mod[4:5]
    hidden_two = (normed_two * scale_two + mod[3:4]).astype(BF)
    value, slope = gelu_pair(mm(hidden_two, wu_ref[...]))
    act = value.astype(BF)
    mlp = mm(act, wd_ref[...])
    fed = mod[5:6] * mlp
    act_out_ref[...] = (middle + fed).astype(BF).reshape(act_out_ref.shape)
    part_ref[6:7] += col_sum(x * x)
    part_ref[7:8] += col_sum(gated * gated)
    part_ref[8:9] += col_sum(fed * fed)

    g = cot_ref[...].reshape(tokens, D).astype(F32) * code_ref[0:1]
    part_ref[5:6] += col_sum(mlp * g)
    gm = (mod[5:6] * g).astype(BF)
    down_sum[...] += mm(act, gm, TN)
    gi = (slope * mm(gm, wd_ref[...], NT)).astype(BF)
    up_sum[...] += mm(hidden_two, gi, TN)
    gh = mm(gi, wu_ref[...], NT)
    part_ref[3:4] += col_sum(gh)
    part_ref[4:5] += col_sum(gh * normed_two)
    gmid = g + norm_back(gh * scale_two, normed_two, rstd_two)
    part_ref[2:3] += col_sum(branch * gmid)
    gb = (mod[2:3] * gmid).astype(BF)
    out_sum[...] += mm(att, gb, TN)
    gatt_ref[...] = mm(gb, wo_ref[...], NT).astype(BF).reshape(gatt_ref.shape)

    def begin(task):
        group, pair, head = task
        grad = both_heads(cut(gatt_ref, group, pair), low)[head]
        return grad, mm(grad, cut(qkv_ref, group, 2 * PAIRS + pair), NT)

    ahead = begin(tasks[0])
    found = []
    for index, (group, pair, head) in enumerate(tasks):
        grad, grad_probs = ahead
        if index + 1 < len(tasks):
            ahead = begin(tasks[index + 1])
        query = both_heads(cut(qkv_ref, group, pair), low)[head]
        cross = grad.astype(F32) * cut(att_ref, group, pair).astype(F32)
        delta = jnp.sum(cross, axis=1, keepdims=True)
        inverse = cut(inv_ref, group, pair)[:, HEAD * head : HEAD * head + 1]
        probs = probs_ref[index].astype(F32) * inverse
        grad_scores = (probs * (grad_probs - delta)).astype(BF)
        found.append(mm(grad_scores, cut(qkv_ref, group, PAIRS + pair)))
        values_part = mm(grad.T, probs.astype(BF))
        keys_part = mm(query.T, grad_scores)
        if head == 0:
            dv, dk = values_part, keys_part
        else:
            dq = jnp.where(low, found[0], found[1])
            put(gqkv_ref, group, pair, (dq * HEAD**-0.5).astype(BF))
            put(gqkv_ref, group, PAIRS + pair, ((dk + keys_part) * HEAD**-0.5).T.astype(BF))
            put(gqkv_ref, group, 2 * PAIRS + pair, (dv + values_part).T.astype(BF))
            found = []

    gp = gqkv_ref[...].reshape(tokens, 3 * D)
    qkv_sum[...] += mm(hidden, gp, TN)
    gh_one = mm(gp, wq_ref[...], NT)
    part_ref[0:1] += col_sum(gh_one)
    part_ref[1:2] += col_sum(gh_one * normed)
    g_next = gmid + norm_back(gh_one * scale, normed, rstd)
    g_ref[...] = g_next.astype(BF).reshape(g_ref.shape)

    @pl.when(last)
    def _():
        for total, out_ref in zip(sums, out_refs):
            out_ref[...] = total[...].astype(out_ref.dtype)


def temporal(x, cot, chunk, codes, mods, weights, carried, before, kind, places):
    clips, frames, spots, _ = x.shape
    block = lambda offset: pl.BlockSpec(
        (None, frames, places, D), lambda c, p: (offset * clips + c, 0, p, 0)
    )
    per_clip = lambda rows: pl.BlockSpec((None, rows, D), lambda c, p: (chunk * clips + c, 0, 0))
    shapes = [(D, 3 * D), (D, D), (D, FF), (FF, D)]
    kept = lambda width, kind: pltpu.VMEM((frames, places, width), kind)
    groups = places // GROUP
    return pl.pallas_call(
        functools.partial(temporal_kernel, len(carried), len(before)),
        grid=(clips, spots // places),
        in_specs=[block(0), block(chunk), per_clip(1), per_clip(6)]
        + [weight_spec(*shape, 1) for shape in shapes]
        + [once(shape) for shape in shapes[: len(carried)]]
        + [pl.BlockSpec(memory_space=pl.ANY)] * len(before),
        out_specs=[block(chunk), block(0), pl.BlockSpec((None, 16, D), lambda c, p: (c, 0, 0))]
        + [once(shape) for shape in shapes],
        out_shape=[
            jax.ShapeDtypeStruct(cot.shape, BF),
            jax.ShapeDtypeStruct(x.shape, BF),
            jax.ShapeDtypeStruct((clips, 16, D), F32),
        ]
        + [jax.ShapeDtypeStruct(shape, kind) for shape in shapes],
        scratch_shapes=[pltpu.VMEM(shape, F32) for shape in shapes]
        + [
            kept(3 * D, BF),
            kept(D, BF),
            pltpu.VMEM((groups * 2 * PAIRS, frames * GROUP, frames * GROUP), BF),
            kept(D, F32),
            kept(D, BF),
            kept(3 * D, BF),
        ],
        compiler_params=params(58),
        cost_estimate=cost(36),
        name="temporal",
        input_output_aliases={8 + len(carried): 0} if before else {},
    )(x, cot, codes, mods, *weights, *carried, *before)


def embed_steps(timesteps):
    half_width = D // 2
    frequencies = jnp.exp(
        -math.log(10000.0) * jnp.arange(half_width, dtype=F32) / half_width
    )
    angles = timesteps.astype(F32)[:, None] * frequencies[None, :]
    return jax.nn.silu(jnp.concatenate([jnp.cos(angles), jnp.sin(angles)], axis=-1))


def swap(values):
    return lax.all_to_all(values, "pos", split_axis=0, concat_axis=0, tiled=True)


def sum_clips(parts):
    total = parts[0].astype(F32)
    for s, give in enumerate(parts[1:], 1):
        total += exchange(give, "clip", len(parts), s).astype(F32)
    return total.astype(BF)


def sum_positions(part, n_pos):
    pieces = swap(part.reshape(n_pos, part.shape[0] // n_pos, D))
    return jnp.sum(pieces.astype(F32), axis=0).astype(BF)


INNER = 4


def exchange(values, axis, size, distance):
    return lax.ppermute(values, axis, [(i, i ^ distance) for i in range(size)])


def gather_outer(piece, n_pos):
    rest = [exchange(piece, "pos", n_pos, k * INNER) for k in range(1, n_pos // INNER)]
    return jnp.stack([piece] + rest)


def gather_inner(pieces, n_pos):
    rest = [exchange(pieces, "pos", n_pos, k) for k in range(1, INNER)]
    return [pieces] + rest


def gather_clips(pieces, n_clip):
    return [pieces] + [exchange(pieces, "clip", n_clip, k) for k in range(1, n_clip)]


def place_pieces(where_ref, piece_refs, rows_ref):
    inner, outer, height, _ = piece_refs[0].shape
    for s, piece_ref in enumerate(piece_refs):
        clip = where_ref[1] ^ s
        for p in range(inner * outer):
            owner = where_ref[0] ^ p
            row = (clip * (inner * outer) + owner) * height
            rows_ref[pl.ds(pl.multiple_of(row, height), height)] = piece_ref[p % inner, p // inner]


def unstack(rows_ref, at, out_ref):
    height, width = out_ref.shape
    for start in range(0, width, D):
        out_ref[:, start : start + D] = rows_ref[at : at + height].astype(F32)
        at += height
    return at


def first_block(shape):
    return pl.BlockSpec((None,) + shape, lambda *_: (0, 0, 0))


def outer_products(embed_ref, rows_ref, first, ada_ref):
    n_clips = embed_ref.shape[1]
    for part in range(6):
        total = 0.0
        for clip in range(n_clips):
            row = first + clip * 6 + part
            total += embed_ref[:, clip : clip + 1] * rows_ref[row : row + 1].astype(F32)
        ada_ref[:, part * D : (part + 1) * D] = total


def finish_feed_kernel(n_pieces, where_ref, *refs):
    pieces, embed_ref = refs[:n_pieces], refs[n_pieces]
    *outs, ada_ref, rest_ref, rows_ref = refs[n_pieces + 1 :]
    place_pieces(where_ref, pieces, rows_ref)
    at = 0
    for out_ref in outs:
        at = unstack(rows_ref, at, out_ref)
    outer_products(embed_ref, rows_ref, at, ada_ref)
    at += embed_ref.shape[1] * 6
    rest_ref[...] = rows_ref[at : at + rest_ref.shape[0]].astype(F32)


def block_of(shape, block):
    return pl.BlockSpec((None,) + shape, lambda *_: (block, 0, 0))


def finish_feed(where, pieces, embed_columns, rest_rows):
    height = len(pieces) * math.prod(pieces[0].shape[:3])
    ada = (D, 6 * D)
    return pl.pallas_call(
        functools.partial(finish_feed_kernel, len(pieces)),
        grid_spec=pltpu.PrefetchScalarGridSpec(
            num_scalar_prefetch=1,
            grid=(1,),
            in_specs=[once(piece.shape) for piece in pieces] + [once(embed_columns.shape)],
            out_specs=[block_of(shape, 0) for shape in FEED_SHAPES]
            + [block_of(ada, 1), whole((rest_rows, D))],
            scratch_shapes=[pltpu.VMEM((height, D), BF)],
        ),
        out_shape=[jax.ShapeDtypeStruct((2,) + shape, F32) for shape in FEED_SHAPES + [ada]]
        + [jax.ShapeDtypeStruct((rest_rows, D), F32)],
        compiler_params=params(56),
        cost_estimate=cost(5),
        name="finish_feed",
    )(where, *pieces, embed_columns)


def finish_kernel(n_pieces, chunks, where_ref, *refs):
    pieces, refs = refs[:n_pieces], refs[n_pieces:]
    embed_ref, qkv_one_ref, *ones = refs[:5]
    grads = refs[5 : 5 + chunks]
    qkv_ref, ada_ref, *outs, grad_ref, rows_ref = refs[9 + chunks :]
    step = pl.program_id(0)

    @pl.when(step == 0)
    def _():
        place_pieces(where_ref, pieces, rows_ref)

    height = qkv_ref.shape[1]
    for part in range(3):
        start = pl.multiple_of(part * D + step * height, height)
        block = rows_ref[pl.ds(start, height)].astype(F32)
        qkv_ref[0, :, part * D : (part + 1) * D] = block
    qkv_ref[1] = qkv_one_ref[...].astype(F32)
    outer_products(embed_ref, rows_ref, 3 * D, ada_ref)
    for one_ref, out_ref in zip(ones, outs):
        out_ref[...] = one_ref[...].astype(F32)
    per = pl.num_programs(0) // chunks
    for c, ref in enumerate(grads):

        @pl.when(step // per == c)
        def _():
            grad_ref[...] = ref[...].astype(F32)


def finish(where, pieces, embed_columns, qkv_one, ones, ada, halves, grads):
    chunks = len(grads)
    per = 4 // chunks if chunks in (1, 2, 4) else 1
    steps = per * chunks
    height = len(pieces) * math.prod(pieces[0].shape[:3])
    cut = lambda shape: (shape[0] // steps,) + shape[1:]
    piece = (grads[0].shape[0] // per,) + grads[0].shape[1:]
    chunk = lambda c: pl.BlockSpec(
        piece, lambda i, *_: (jnp.minimum(jnp.maximum(i - c * per, 0), per - 1), 0, 0)
    )
    rows = lambda shape: pl.BlockSpec(cut(shape), lambda i, *_: (i, 0))
    block = lambda shape, b: pl.BlockSpec((None,) + cut(shape), lambda i, *_: (b, i, 0))
    first = len(pieces) + 6 + chunks
    return pl.pallas_call(
        functools.partial(finish_kernel, len(pieces), chunks),
        grid_spec=pltpu.PrefetchScalarGridSpec(
            num_scalar_prefetch=1,
            grid=(steps,),
            in_specs=[once(piece.shape) for piece in pieces]
            + [rows(embed_columns.shape), rows(qkv_one.shape)]
            + [rows(one.shape) for one in ones]
            + [chunk(c) for c in range(chunks)]
            + [pl.BlockSpec(memory_space=pl.ANY)] * (1 + len(halves)),
            out_specs=[
                pl.BlockSpec((2, D // steps, 3 * D), lambda i, *_: (0, i, 0)),
                block((D, 6 * D), 0),
            ]
            + [block(one.shape, 1) for one in ones]
            + [pl.BlockSpec(piece, lambda i, *_: (i, 0, 0))],
            scratch_shapes=[pltpu.VMEM((height, D), BF)],
        ),
        out_shape=[
            jax.ShapeDtypeStruct((2, D, 3 * D), F32),
            jax.ShapeDtypeStruct(ada.shape, F32),
        ]
        + [jax.ShapeDtypeStruct(half.shape, F32) for half in halves]
        + [jax.ShapeDtypeStruct((chunks * grads[0].shape[0],) + grads[0].shape[1:], F32)],
        input_output_aliases={first + k: 1 + k for k in range(1 + len(halves))},
        compiler_params=params(56),
        cost_estimate=cost(8),
        name="finish",
    )(where, *pieces, embed_columns, qkv_one, *ones, *grads, ada, *halves)


def round_up(value, unit):
    return -(-value // unit) * unit


def as_one_step(timesteps, function, *operands):
    def skip(*operands):
        shapes = jax.eval_shape(function, *operands)
        return jax.tree.map(lambda leaf: jnp.zeros(leaf.shape, leaf.dtype), shapes)

    return lax.cond(timesteps[0] >= 0, function, skip, *operands)


def on_device(
    tokens,
    timesteps,
    weight_codes,
    cotangent,
    ada_weight,
    qkv_weight,
    out_weight,
    up_weight,
    down_weight,
):
    clips, frames, spots, _ = tokens.shape
    n_pos = lax.axis_size("pos")
    n_clip = lax.axis_size("clip")
    chunks = clips * frames // n_pos
    span = clips // chunks
    n = n_pos * spots
    rows = 512
    places = min(spots, 32)

    n_all = n_pos * n_clip
    n_clips = n_clip * clips
    square_height = round_up(n_all * 18, D) // D
    feed_height = sum(a * b for a, b in FEED_SHAPES) // D + n_clips * 6 + square_height
    feed_height = round_up(feed_height, 16 * n_all)
    tail_height = round_up(3 * D + n_clips * 6, 16 * n_all)
    pos, clip = lax.axis_index("pos"), lax.axis_index("clip")
    mine = pos // frames
    own = clip * clips
    where = [pos, clip, (own + (chunks - 1) * span + mine) * 6, pos % INNER, pos // INNER]
    where = jnp.stack(where).astype(jnp.int32)

    def send(tokens, c):
        return tokens[c * span : (c + 1) * span].reshape(n_pos, spots, D)

    first = swap(send(tokens, 0))
    embedded = embed_steps(timesteps)
    mods = [
        jnp.dot(
            embedded, ada_weight[block].astype(F32), precision=lax.Precision.HIGHEST
        ).reshape(clips, 6, D)
        for block in range(2)
    ]
    embed_rows = lax.all_gather(embedded, "clip", axis=0, tiled=True)
    scaling = jnp.exp2(0.5 * weight_codes.astype(F32) - 1.0)
    codes = jnp.broadcast_to(scaling[:, None, None], (clips, 1, D))
    arrived = [first.reshape(n, D)]
    for c in range(1, chunks):
        held, embed_rows, *mods = lax.optimization_barrier((tokens, embed_rows, *mods))
        arrived.append(swap(send(held, c)).reshape(n, D))

    kept_all = []
    streams = []
    for c in range(chunks):
        x = arrived[c]
        mod = lax.dynamic_index_in_dim(mods[0], c * span + mine, 0, keepdims=False)
        qkv = project(x, mod, qkv_weight, rows)
        att, logs = attend(qkv, 256)
        x_next, *kept, squares = feed(x, att, mod, out_weight, up_weight, down_weight, rows)
        streams.append(swap(x_next.reshape(n_pos, spots, D)).reshape(span, frames, spots, D))
        kept_all.append((x, mod, qkv, att, logs, kept, squares))

    weights = (qkv_weight, out_weight, up_weight, down_weight)
    results, returned, parts_one = (), [], []
    carried = ()
    for c in range(chunks):
        kind = BF
        result, g, part, *carried = temporal(
            streams[c], cotangent, c, codes, mods[1], weights, carried, results, kind, places
        )
        results = (result,)
        parts_one.append(part)
        returned.append(swap(g.reshape(n_pos, spots, D)).reshape(n, D))
    sums_one = carried

    part_one = jnp.concatenate(parts_one, axis=0)
    squares_zero = sum(kept[-1] for kept in kept_all)[:3]
    squares_one = jnp.sum(part_one[:, 6:9], axis=0)
    squares = jnp.sum(jnp.concatenate([squares_zero, squares_one], axis=0), axis=1)
    terms = []
    for _ in range(3):
        kept = lax.reduce_precision(squares, exponent_bits=8, mantissa_bits=7)
        terms.append(kept.astype(BF))
        squares = squares - kept
    square_rows = lax.dynamic_update_slice(
        jnp.zeros((square_height * D,), BF), jnp.concatenate(terms), ((pos * n_clip + clip) * 18,)
    ).reshape(square_height, D)
    mod_one = lax.dynamic_update_slice(
        jnp.zeros((n_clips, 6, D), BF), part_one[:, :6].astype(BF), (own, 0, 0)
    )
    extra = jnp.concatenate([mod_one.reshape(n_clips * 6, D), square_rows], axis=0)

    def back_of_feed(c, g, carried):
        x, mod, qkv, att, logs, kept, squares = kept_all[c]
        weights = (out_weight, up_weight, down_weight)
        n_parts = n_clip if c == chunks - 1 else 0
        return feed_back(
            where, extra, g, kept, att, mod, *weights, carried, BF, 256, feed_height, n_parts
        )

    def back_of_project(c, found, gmid, mods, carried):
        x, mod, qkv, att, logs, kept, squares = kept_all[c]
        n_parts = n_clip if c == chunks - 1 else 0
        found = [third[k] for k in range(3) for third in found]
        g, part, *carried = project_back(
            where, mods, x, found, gmid, mod, qkv_weight, carried, rows, tail_height, n_parts
        )
        return g.reshape(n_pos, spots, D), part[:6], carried

    def some_pairs(c, gatt, first, count):
        x, mod, qkv, att, logs, kept, squares = kept_all[c]
        return attend_back(qkv, att, logs, gatt, first, count, rows)

    def last_block_back(later, middle, found, carried):
        middles = [middle]
        for c in range(1, chunks):
            gmid, gatt, part, *carried = back_of_feed(c, later[c - 1], carried)
            middles.append((gmid, gatt, part))
        feed_part = sum_clips(carried)
        carried = ()
        grads = []
        mods = jnp.zeros((n_clips, 6, D), F32)
        for c, (gmid, gatt, part) in enumerate(middles):
            if c == 0:
                feed_part, gatt = lax.optimization_barrier((feed_part, gatt))
                feed_piece = sum_positions(feed_part, n_pos)
                found = [found]
            else:
                found = [some_pairs(c, gatt, 0, 2)]
            if c == chunks - 1:
                break
            found.append(some_pairs(c, gatt, 1, 2))
            grad, part_first, carried = back_of_project(c, found, gmid, mods.reshape(-1, D), carried)
            grads.append(grad)
            mods = lax.dynamic_update_index_in_dim(
                mods, part[:6] + part_first, own + c * span + mine, 0
            )
        mods = lax.dynamic_update_index_in_dim(mods, part[:6], own + (chunks - 1) * span + mine, 0)
        mods = mods.reshape(-1, D)

        gatt, found, feed_piece, *grads = lax.optimization_barrier((gatt, found, feed_piece, *grads))
        feed_pieces = gather_outer(feed_piece, n_pos)

        def last_step(grads, gatt, found, gmid, mods, carried):
            grads = [swap(grad) for grad in grads]
            done = 2 if chunks > 1 else 1
            found = found + [some_pairs(chunks - 1, gatt, done, PAIRS - done)]
            grad, _, parts = back_of_project(chunks - 1, found, gmid, mods, carried)
            return grads, grad, sum_clips(parts)

        grads, grad, part = as_one_step(
            timesteps, last_step, grads, gatt, found, gmid, mods, carried
        )
        part, feed_pieces = lax.optimization_barrier((part, feed_pieces))
        feed_pieces = gather_inner(feed_pieces, n_pos)
        piece = as_one_step(timesteps, lambda part: sum_positions(part, n_pos), part)
        piece, feed_pieces = lax.optimization_barrier((piece, feed_pieces))
        tail_pieces = gather_outer(piece, n_pos)
        grad, tail_pieces = lax.optimization_barrier((grad, tail_pieces))
        grads.append(swap(grad))
        tail_pieces = gather_inner(tail_pieces, n_pos)
        embed_columns = embed_rows.T
        rest_rows = extra.shape[0] - n_clips * 6

        def feed_step(feed_pieces):
            gathered = gather_clips(jnp.stack(feed_pieces), n_clip)
            *found, rest = finish_feed(where, gathered, embed_columns, rest_rows)
            total = jnp.sum(rest.reshape(-1)[: n_all * 18].reshape(n_all, 3, 6), axis=(0, 1))
            token_count = clips * frames * spots * n_all
            return found, jnp.sqrt(total.reshape(2, 3) / token_count)

        (*halves, ada_grad), stream_rms = as_one_step(timesteps, feed_step, feed_pieces)
        ada_grad, *tail_pieces = lax.optimization_barrier((ada_grad, *tail_pieces))
        tail_pieces = gather_clips(jnp.stack(tail_pieces), n_clip)
        return grads, tail_pieces, embed_columns, ada_grad, stream_rms, halves

    gmid, gatt, part, *carried = back_of_feed(0, returned[0], ())
    found = some_pairs(0, gatt, 0, 1)
    grads, tail_pieces, embed_columns, ada_grad, stream_rms, halves = as_one_step(
        timesteps, last_block_back, returned[1:], (gmid, gatt, part), found, carried
    )
    qkv_one, out_one, up_one, down_one = lax.psum(tuple(sums_one), ("pos", "clip"))
    qkv_grad, ada_grad, up_grad, down_grad, out_grad, grad_tokens = finish(
        where,
        tail_pieces,
        embed_columns,
        qkv_one,
        (up_one, down_one, out_one),
        ada_grad,
        halves,
        grads,
    )
    return (
        results[0],
        grad_tokens.reshape(tokens.shape),
        ada_grad,
        qkv_grad,
        out_grad,
        up_grad,
        down_grad,
        stream_rms,
    )


def solution(mesh):
    placed = (
        P("clip", None, "pos", None),
        P("clip"),
        P("clip"),
        P("clip", None, "pos", None),
        P(),
        P(),
        P(),
        P(),
        P(),
    )
    return jax.shard_map(
        on_device,
        mesh=mesh,
        in_specs=placed,
        out_specs=(
            P("clip", None, "pos", None),
            P("clip", None, "pos", None),
            P(),
            P(),
            P(),
            P(),
            P(),
            P(),
        ),
        check_vma=False,
    )
```

```python
import functools
import math

import jax
import jax.numpy as jnp
from jax import lax
from jax.experimental import pallas as pl
from jax.experimental.pallas import tpu as pltpu
from jax.sharding import PartitionSpec as P

D = 384
HEAD = 64
PAIRS = 3
FF = 1536
EPS = 1e-06
LOG_SCALE = HEAD**-0.5 * math.log2(math.e)
GROUP = 16
FEED_SHAPES = [(D, FF), (FF, D), (D, D)]

NN = (((1,), (0,)), ((), ()))
NT = (((1,), (1,)), ((), ()))
TN = (((0,), (0,)), ((), ()))
F32 = jnp.float32
BF = jnp.bfloat16


def mm(left, right, dims=NN):
    return lax.dot_general(left, right, dims, preferred_element_type=F32)


def params(mebibytes):
    return pltpu.CompilerParams(vmem_limit_bytes=mebibytes * 2**20)


def cost(micros):
    return pl.CostEstimate(
        flops=int(micros * 1e9), transcendentals=0, bytes_accessed=int(micros * 3e6)
    )


def norm_rows(values):
    center = values - jnp.mean(values, axis=-1, keepdims=True)
    rstd = lax.rsqrt(jnp.mean(center * center, axis=-1, keepdims=True) + EPS)
    return center * rstd, rstd


def norm_back(grad_normed, normed, rstd):
    mean_grad = jnp.mean(grad_normed, axis=-1, keepdims=True)
    mean_cross = jnp.mean(grad_normed * normed, axis=-1, keepdims=True)
    return rstd * (grad_normed - mean_grad - normed * mean_cross)


def col_sum(values):
    return jnp.sum(values, axis=0, keepdims=True)


def gelu_pair(inner):
    square = inner * inner
    slope = math.sqrt(2.0 / math.pi)
    tanh = jnp.tanh(inner * (slope + (slope * 0.044715) * square))
    half = 0.5 + 0.5 * tanh
    value = inner * half
    grad = half + (value * (1.0 - tanh)) * (slope + (3.0 * 0.044715 * slope) * square)
    return value, grad


def low_lanes():
    return lax.broadcasted_iota(jnp.int32, (1, 2 * HEAD), 1) < HEAD


def both_heads(values, low, fill=0.0):
    other = jnp.full_like(values, fill)
    return (jnp.where(low, values, other), jnp.where(low, other, values))


def whole(shape):
    return pl.BlockSpec(shape, lambda *_: (0,) * len(shape))


def once(shape):
    return pl.BlockSpec(shape, lambda *_: (0,) * len(shape), pipeline_mode=pl.Buffered(1))


def weight_spec(rows, cols, block):
    return pl.BlockSpec((None, rows, cols), lambda *_: (block, 0, 0), pipeline_mode=pl.Buffered(1))


def project_kernel(x_ref, mod_ref, w_ref, out_ref):
    normed, _ = norm_rows(x_ref[...].astype(F32))
    hidden = (normed * (1.0 + mod_ref[1:2]) + mod_ref[0:1]).astype(BF)
    out_ref[...] = mm(hidden, w_ref[...]).astype(BF)


def project(x, mod, qkv_weight, rows):
    n = x.shape[0]
    return pl.pallas_call(
        project_kernel,
        grid=(n // rows,),
        in_specs=[
            pl.BlockSpec((rows, D), lambda i: (i, 0)),
            whole((6, D)),
            weight_spec(D, 3 * D, 0),
        ],
        out_specs=pl.BlockSpec((rows, 3 * D), lambda i: (i, 0)),
        out_shape=jax.ShapeDtypeStruct((n, 3 * D), BF),
        compiler_params=params(16),
        cost_estimate=cost(5),
        name="project",
    )(x, mod, qkv_weight)


def attend_kernel(rows, q_ref, k_ref, v_ref, out_ref, log_ref):
    low = low_lanes()
    keys = k_ref[...]
    values = both_heads(v_ref[...], low, 1.0)
    tasks = [(start, head) for start in range(0, q_ref.shape[0], rows) for head in range(2)]

    def score(task):
        start, head = task
        q = q_ref[start : start + rows, :]
        return mm(both_heads(q, low)[head], keys, NT)

    ahead = score(tasks[0])
    mixed, tops = [], []
    for index, (start, head) in enumerate(tasks):
        scores = ahead
        if index + 1 < len(tasks):
            ahead = score(tasks[index + 1])
        top = jnp.max(scores, axis=1, keepdims=True)
        raised = jnp.exp2((scores - top) * LOG_SCALE).astype(BF)
        mixed.append(mm(raised, values[head]))
        tops.append(top * LOG_SCALE)
        if head == 1:
            part = slice(start, start + rows)
            total = pltpu.roll(jnp.where(low, mixed[1], mixed[0]), HEAD, 1)
            out_ref[part, :] = (jnp.where(low, mixed[0], mixed[1]) / total).astype(BF)
            log_ref[part, :] = jnp.where(low, tops[0], tops[1]) + jnp.log2(total)
            mixed, tops = [], []


def attend(qkv, rows):
    n = qkv.shape[0]
    pair = lambda start: pl.BlockSpec((n, 2 * HEAD), lambda p: (0, start + p))
    return pl.pallas_call(
        functools.partial(attend_kernel, rows),
        grid=(PAIRS,),
        in_specs=[pair(0), pair(PAIRS), pair(2 * PAIRS)],
        out_specs=[pair(0), pair(0)],
        out_shape=[jax.ShapeDtypeStruct((n, D), BF), jax.ShapeDtypeStruct((n, D), F32)],
        compiler_params=params(24),
        cost_estimate=cost(14),
        name="attend",
    )(qkv, qkv, qkv)


def feed_kernel(
    x_ref,
    att_ref,
    mod_ref,
    wo_ref,
    wu_ref,
    wd_ref,
    next_ref,
    middle_ref,
    branch_ref,
    mlp_ref,
    act_ref,
    slope_ref,
    squares_ref,
):
    @pl.when(pl.program_id(0) == 0)
    def _():
        squares_ref[...] = jnp.zeros_like(squares_ref)

    x = x_ref[...].astype(F32)
    branch = mm(att_ref[...], wo_ref[...])
    gated = mod_ref[2:3] * branch
    middle = x + gated
    normed, _ = norm_rows(middle)
    hidden = (normed * (1.0 + mod_ref[4:5]) + mod_ref[3:4]).astype(BF)
    value, slope = gelu_pair(mm(hidden, wu_ref[...]))
    act = value.astype(BF)
    mlp = mm(act, wd_ref[...])
    fed = mod_ref[5:6] * mlp
    next_ref[...] = (middle + fed).astype(BF)
    middle_ref[...] = middle.astype(BF)
    branch_ref[...] = branch.astype(BF)
    mlp_ref[...] = mlp.astype(BF)
    act_ref[...] = act
    slope_ref[...] = slope.astype(BF)
    squares_ref[0:1] += col_sum(x * x)
    squares_ref[1:2] += col_sum(gated * gated)
    squares_ref[2:3] += col_sum(fed * fed)


def feed(x, att, mod, out_weight, up_weight, down_weight, rows):
    n = x.shape[0]
    row = lambda width: pl.BlockSpec((rows, width), lambda i: (i, 0))
    out = lambda width, kind: jax.ShapeDtypeStruct((n, width), kind)
    return pl.pallas_call(
        feed_kernel,
        grid=(n // rows,),
        in_specs=[
            row(D),
            row(D),
            whole((6, D)),
            weight_spec(D, D, 0),
            weight_spec(D, FF, 0),
            weight_spec(FF, D, 0),
        ],
        out_specs=[row(D), row(D), row(D), row(D), row(FF), row(FF), whole((8, D))],
        out_shape=[
            out(D, BF),
            out(D, BF),
            out(D, BF),
            out(D, BF),
            out(FF, BF),
            out(FF, BF),
            jax.ShapeDtypeStruct((8, D), F32),
        ],
        compiler_params=params(56),
        cost_estimate=cost(11),
        name="feed",
    )(x, att, mod, out_weight, up_weight, down_weight)


def start_sums(sums, carried):
    for index, total in enumerate(sums):
        total[...] = carried[index][...].astype(F32) if carried else jnp.zeros_like(total)


def row_blocks(total):
    height, width = total.shape
    return [(start, height) for start in range(0, width, D)]


def load_rows(rows_ref, sums):
    at = 0
    for total in sums:
        for start, height in row_blocks(total):
            total[:, start : start + D] = rows_ref[at : at + height].astype(F32)
            at += height


def store_rows(sums, rows_ref, extra=None):
    at = 0
    for total in sums:
        for start, height in row_blocks(total):
            rows_ref[at : at + height] = total[:, start : start + D].astype(rows_ref.dtype)
            at += height
    if extra is not None:
        rows_ref[at : at + extra.shape[0]] = extra.astype(rows_ref.dtype)
        at += extra.shape[0]
    if at < rows_ref.shape[0]:
        rows_ref[at:] = jnp.zeros((rows_ref.shape[0] - at, D), rows_ref.dtype)


def store_parts(where_ref, held_ref, rows_refs):
    part = rows_refs[0].shape[0]
    for s, rows_ref in enumerate(rows_refs):
        start = pl.multiple_of((where_ref[1] ^ s) * part, part)
        rows_ref[...] = held_ref[pl.ds(start, part)]


def feed_back_kernel(n_carried, n_parts, where_ref, extra_ref, *refs):
    (
        g_ref,
        middle_ref,
        branch_ref,
        mlp_ref,
        act_ref,
        slope_ref,
        att_ref,
        mod_ref,
        wo_ref,
        wu_ref,
        wd_ref,
    ) = refs[:11]
    carried = refs[11 : 11 + n_carried]
    gmid_ref, gatt_ref, part_ref = refs[11 + n_carried : 14 + n_carried]
    n_out = max(n_parts, 1)
    rows_refs = refs[14 + n_carried : 14 + n_carried + n_out]
    *sums, held_ref = refs[14 + n_carried + n_out :]

    @pl.when(pl.program_id(0) == 0)
    def _():
        part_ref[...] = jnp.zeros_like(part_ref)
        if carried:
            load_rows(carried[0], sums)
        else:
            start_sums(sums, ())

    up_sum, down_sum, out_sum = sums
    g = g_ref[...].astype(F32)
    part_ref[5:6] += col_sum(mlp_ref[...].astype(F32) * g)
    gm = (mod_ref[5:6] * g).astype(BF)
    down_sum[...] += mm(act_ref[...], gm, TN)
    gi = (slope_ref[...].astype(F32) * mm(gm, wd_ref[...], NT)).astype(BF)
    normed, rstd = norm_rows(middle_ref[...].astype(F32))
    scale = 1.0 + mod_ref[4:5]
    hidden = (normed * scale + mod_ref[3:4]).astype(BF)
    up_sum[...] += mm(hidden, gi, TN)
    gh = mm(gi, wu_ref[...], NT)
    part_ref[3:4] += col_sum(gh)
    part_ref[4:5] += col_sum(gh * normed)
    gmid = g + norm_back(gh * scale, normed, rstd)
    gmid_ref[...] = gmid
    part_ref[2:3] += col_sum(branch_ref[...].astype(F32) * gmid)
    gb = (mod_ref[2:3] * gmid).astype(BF)
    out_sum[...] += mm(att_ref[...], gb, TN)
    gatt_ref[...] = mm(gb, wo_ref[...], NT).astype(BF)

    @pl.when(pl.program_id(0) == pl.num_programs(0) - 1)
    def _():
        if n_parts == 0:
            store_rows(sums, rows_refs[0])
        else:
            store_rows(sums, held_ref, extra_ref[...])
            store_parts(where_ref, held_ref, rows_refs)


def feed_back(where, extra, g, kept, att, mod, out_weight, up_weight, down_weight, carried, kind, rows, height, n_parts):
    n = g.shape[0]
    row = lambda width: pl.BlockSpec((rows, width), lambda i, *_: (i, 0))
    shapes = FEED_SHAPES
    n_out = max(n_parts, 1)
    return pl.pallas_call(
        functools.partial(feed_back_kernel, len(carried), n_parts),
        grid=(n // rows,),
        in_specs=[
            pl.BlockSpec(memory_space=pltpu.SMEM),
            whole(extra.shape),
            row(D),
            row(D),
            row(D),
            row(D),
            row(FF),
            row(FF),
            row(D),
            whole((6, D)),
            weight_spec(D, D, 0),
            weight_spec(D, FF, 0),
            weight_spec(FF, D, 0),
        ]
        + [once((height, D))] * len(carried),
        out_specs=[row(D), row(D), whole((8, D)), once((height // n_out, D))]
        + [once((height // n_out, D))] * (n_out - 1),
        out_shape=[
            jax.ShapeDtypeStruct((n, D), F32),
            jax.ShapeDtypeStruct((n, D), BF),
            jax.ShapeDtypeStruct((8, D), F32),
        ]
        + [jax.ShapeDtypeStruct((height // n_out, D), kind)] * n_out,
        scratch_shapes=[pltpu.VMEM(shape, F32) for shape in shapes] + [pltpu.VMEM((height, D), BF)],
        compiler_params=params(36 if n_parts else 56),
        cost_estimate=cost(16),
        name="feed_back",
    )(where, extra, g, *kept, att, mod, out_weight, up_weight, down_weight, *carried)


def attend_back_kernel(
    rows, q_ref, k_ref, v_ref, o_ref, log_ref, g_ref, dq_ref, dk_ref, dv_ref
):
    low = low_lanes()
    keys, values = k_ref[...], v_ref[...]
    tasks = [(start, head) for start in range(0, q_ref.shape[0], rows) for head in range(2)]

    def begin(task):
        start, head = task
        part = slice(start, start + rows)
        query = both_heads(q_ref[part, :], low)[head]
        grad = both_heads(g_ref[part, :], low)[head]
        return query, grad, mm(query, keys, NT), mm(grad, values, NT)

    ahead = begin(tasks[0])
    found = []
    for index, (start, head) in enumerate(tasks):
        query, grad, scores, grad_probs = ahead
        if index + 1 < len(tasks):
            ahead = begin(tasks[index + 1])
        part = slice(start, start + rows)
        delta = jnp.sum(grad.astype(F32) * o_ref[part, :].astype(F32), axis=1, keepdims=True)
        log = log_ref[part, HEAD * head : HEAD * head + 1]
        probs = jnp.exp2(scores * LOG_SCALE - log)
        grad_scores = (probs * (grad_probs - delta)).astype(BF)
        found.append(mm(grad_scores, keys))
        values_part = mm(grad.T, probs.astype(BF))
        keys_part = mm(query.T, grad_scores)
        dv = values_part if index == 0 else dv + values_part
        dk = keys_part if index == 0 else dk + keys_part
        if head == 1:
            dq_ref[part, :] = (jnp.where(low, found[0], found[1]) * HEAD**-0.5).astype(BF)
            found = []
    dk_ref[...] = (dk * HEAD**-0.5).T.astype(BF)
    dv_ref[...] = dv.T.astype(BF)


def attend_back(qkv, att, logs, grad, first, count, rows):
    n = qkv.shape[0]
    pair = lambda start: pl.BlockSpec((n, 2 * HEAD), lambda p: (0, start + p))
    return pl.pallas_call(
        functools.partial(attend_back_kernel, rows),
        grid=(count,),
        in_specs=[pair(third * PAIRS + first) for third in (0, 1, 2, 0, 0, 0)],
        out_specs=[pair(0)] * 3,
        out_shape=[jax.ShapeDtypeStruct((n, count * 2 * HEAD), BF)] * 3,
        compiler_params=params(24),
        cost_estimate=cost(5 * count),
        name="attend_back",
    )(qkv, qkv, qkv, att, logs, grad)


def project_back_kernel(n_grads, n_carried, n_parts, where_ref, mods_ref, *refs):
    grad_refs, refs = refs[:n_grads], refs[n_grads:]
    x_ref, gmid_ref, mod_ref, w_ref = refs[:4]
    carried = refs[4 : 4 + n_carried]
    out_ref, part_ref = refs[4 + n_carried : 6 + n_carried]
    *rows_refs, total, held_ref, mods_sum = refs[6 + n_carried :]

    @pl.when(pl.program_id(0) == 0)
    def _():
        part_ref[...] = jnp.zeros_like(part_ref)
        if carried:
            load_rows(carried[0], [total])
        else:
            start_sums([total], ())

    normed, rstd = norm_rows(x_ref[...].astype(F32))
    scale = 1.0 + mod_ref[1:2]
    hidden = (normed * scale + mod_ref[0:1]).astype(BF)
    gp = jnp.concatenate([ref[...] for ref in grad_refs], axis=1)
    total[...] += mm(hidden, gp, TN)
    gh = mm(gp, w_ref[...], NT)
    part_ref[0:1] += col_sum(gh)
    part_ref[1:2] += col_sum(gh * normed)
    out_ref[...] = (gmid_ref[...] + norm_back(gh * scale, normed, rstd)).astype(BF)

    @pl.when(pl.program_id(0) == pl.num_programs(0) - 1)
    def _():
        if n_parts == 0:
            store_rows([total], rows_refs[0])
        else:
            mods_sum[...] = mods_ref[...]
            for k in range(2):
                mods_sum[pl.ds(where_ref[2] + k, 1)] += part_ref[k : k + 1]
            store_rows([total], held_ref, mods_sum[...])
            store_parts(where_ref, held_ref, rows_refs)


def project_back(where, mods, x, grads, gmid, mod, qkv_weight, carried, rows, height, n_parts):
    n = x.shape[0]
    row = lambda width: pl.BlockSpec((rows, width), lambda i: (i, 0))
    n_out = max(n_parts, 1)
    if n_parts == 0:
        height = 3 * D
    return pl.pallas_call(
        functools.partial(project_back_kernel, len(grads), len(carried), n_parts),
        grid=(n // rows,),
        in_specs=[pl.BlockSpec(memory_space=pltpu.SMEM), whole(mods.shape)]
        + [row(grad.shape[1]) for grad in grads]
        + [row(D), row(D), whole((6, D)), weight_spec(D, 3 * D, 0)]
        + [once((3 * D, D))] * len(carried),
        out_specs=[row(D), whole((8, D))] + [once((height // n_out, D))] * n_out,
        out_shape=[
            jax.ShapeDtypeStruct((n, D), BF),
            jax.ShapeDtypeStruct((8, D), F32),
        ]
        + [jax.ShapeDtypeStruct((height // n_out, D), BF)] * n_out,
        scratch_shapes=[
            pltpu.VMEM((D, 3 * D), F32),
            pltpu.VMEM((height, D), BF),
            pltpu.VMEM(mods.shape, F32),
        ],
        compiler_params=params(24),
        cost_estimate=cost(4),
        name="project_back",
    )(where, mods, *grads, x, gmid, mod, qkv_weight, *carried)


def temporal_kernel(n_carried, n_before, *refs):
    x_ref, cot_ref, code_ref, mod_ref, wq_ref, wo_ref, wu_ref, wd_ref = refs[:8]
    carried = refs[8 : 8 + n_carried]
    refs = refs[8 + n_carried + n_before :]
    act_out_ref, g_ref, part_ref = refs[:3]
    out_refs = refs[3:7]
    sums = refs[7:11]
    qkv_ref, att_ref, probs_ref, inv_ref, gatt_ref, gqkv_ref = refs[11:]
    frames, places = x_ref.shape[0], x_ref.shape[1]
    tokens = frames * places
    wide = frames * GROUP
    first = jnp.logical_and(pl.program_id(0) == 0, pl.program_id(1) == 0)
    last = jnp.logical_and(
        pl.program_id(0) == pl.num_programs(0) - 1, pl.program_id(1) == pl.num_programs(1) - 1
    )

    @pl.when(first)
    def _():
        start_sums(sums, carried)

    @pl.when(pl.program_id(1) == 0)
    def _():
        part_ref[...] = jnp.zeros_like(part_ref)

    qkv_sum, out_sum, up_sum, down_sum = sums
    low = low_lanes()
    mod = mod_ref[...]
    x = x_ref[...].reshape(tokens, D).astype(F32)
    normed, rstd = norm_rows(x)
    scale = 1.0 + mod[1:2]
    hidden = (normed * scale + mod[0:1]).astype(BF)
    qkv_ref[...] = mm(hidden, wq_ref[...]).astype(BF).reshape(qkv_ref.shape)

    place = lambda axis: lax.broadcasted_iota(jnp.int32, (wide, wide), axis) % GROUP
    same = place(0) == place(1)
    groups = places // GROUP

    def cut(ref, group, column):
        rows = slice(group * GROUP, (group + 1) * GROUP)
        return ref[:, rows, column * 2 * HEAD : (column + 1) * 2 * HEAD].reshape(wide, 2 * HEAD)

    def put(ref, group, column, value):
        rows = slice(group * GROUP, (group + 1) * GROUP)
        ref[:, rows, column * 2 * HEAD : (column + 1) * 2 * HEAD] = value.reshape(
            frames, GROUP, 2 * HEAD
        )

    tasks = [(g, pair, head) for g in range(groups) for pair in range(PAIRS) for head in range(2)]

    def score(task):
        group, pair, head = task
        query = both_heads(cut(qkv_ref, group, pair), low)[head]
        return mm(query, cut(qkv_ref, group, PAIRS + pair), NT)

    ahead = score(tasks[0])
    mixed = []
    for index, (group, pair, head) in enumerate(tasks):
        scores = jnp.where(same, ahead, -1e38)
        if index + 1 < len(tasks):
            ahead = score(tasks[index + 1])
        top = jnp.max(scores, axis=1, keepdims=True)
        raised = jnp.exp2((scores - top) * LOG_SCALE).astype(BF)
        probs_ref[index] = raised
        mixed.append(mm(raised, both_heads(cut(qkv_ref, group, 2 * PAIRS + pair), low, 1.0)[head]))
        if head == 1:
            inverse = 1.0 / pltpu.roll(jnp.where(low, mixed[1], mixed[0]), HEAD, 1)
            put(inv_ref, group, pair, inverse)
            put(att_ref, group, pair, (jnp.where(low, mixed[0], mixed[1]) * inverse).astype(BF))
            mixed = []

    att = att_ref[...].reshape(tokens, D)
    branch = mm(att, wo_ref[...])
    gated = mod[2:3] * branch
    middle = x + gated
    normed_two, rstd_two = norm_rows(middle)
    scale_two = 1.0 + mod[4:5]
    hidden_two = (normed_two * scale_two + mod[3:4]).astype(BF)
    value, slope = gelu_pair(mm(hidden_two, wu_ref[...]))
    act = value.astype(BF)
    mlp = mm(act, wd_ref[...])
    fed = mod[5:6] * mlp
    act_out_ref[...] = (middle + fed).astype(BF).reshape(act_out_ref.shape)
    part_ref[6:7] += col_sum(x * x)
    part_ref[7:8] += col_sum(gated * gated)
    part_ref[8:9] += col_sum(fed * fed)

    g = cot_ref[...].reshape(tokens, D).astype(F32) * code_ref[0:1]
    part_ref[5:6] += col_sum(mlp * g)
    gm = (mod[5:6] * g).astype(BF)
    down_sum[...] += mm(act, gm, TN)
    gi = (slope * mm(gm, wd_ref[...], NT)).astype(BF)
    up_sum[...] += mm(hidden_two, gi, TN)
    gh = mm(gi, wu_ref[...], NT)
    part_ref[3:4] += col_sum(gh)
    part_ref[4:5] += col_sum(gh * normed_two)
    gmid = g + norm_back(gh * scale_two, normed_two, rstd_two)
    part_ref[2:3] += col_sum(branch * gmid)
    gb = (mod[2:3] * gmid).astype(BF)
    out_sum[...] += mm(att, gb, TN)
    gatt_ref[...] = mm(gb, wo_ref[...], NT).astype(BF).reshape(gatt_ref.shape)

    def begin(task):
        group, pair, head = task
        grad = both_heads(cut(gatt_ref, group, pair), low)[head]
        return grad, mm(grad, cut(qkv_ref, group, 2 * PAIRS + pair), NT)

    ahead = begin(tasks[0])
    found = []
    for index, (group, pair, head) in enumerate(tasks):
        grad, grad_probs = ahead
        if index + 1 < len(tasks):
            ahead = begin(tasks[index + 1])
        query = both_heads(cut(qkv_ref, group, pair), low)[head]
        cross = grad.astype(F32) * cut(att_ref, group, pair).astype(F32)
        delta = jnp.sum(cross, axis=1, keepdims=True)
        inverse = cut(inv_ref, group, pair)[:, HEAD * head : HEAD * head + 1]
        probs = probs_ref[index].astype(F32) * inverse
        grad_scores = (probs * (grad_probs - delta)).astype(BF)
        found.append(mm(grad_scores, cut(qkv_ref, group, PAIRS + pair)))
        values_part = mm(grad.T, probs.astype(BF))
        keys_part = mm(query.T, grad_scores)
        if head == 0:
            dv, dk = values_part, keys_part
        else:
            dq = jnp.where(low, found[0], found[1])
            put(gqkv_ref, group, pair, (dq * HEAD**-0.5).astype(BF))
            put(gqkv_ref, group, PAIRS + pair, ((dk + keys_part) * HEAD**-0.5).T.astype(BF))
            put(gqkv_ref, group, 2 * PAIRS + pair, (dv + values_part).T.astype(BF))
            found = []

    gp = gqkv_ref[...].reshape(tokens, 3 * D)
    qkv_sum[...] += mm(hidden, gp, TN)
    gh_one = mm(gp, wq_ref[...], NT)
    part_ref[0:1] += col_sum(gh_one)
    part_ref[1:2] += col_sum(gh_one * normed)
    g_next = gmid + norm_back(gh_one * scale, normed, rstd)
    g_ref[...] = g_next.astype(BF).reshape(g_ref.shape)

    @pl.when(last)
    def _():
        for total, out_ref in zip(sums, out_refs):
            out_ref[...] = total[...].astype(out_ref.dtype)


def temporal(x, cot, chunk, codes, mods, weights, carried, before, kind, places):
    clips, frames, spots, _ = x.shape
    block = lambda offset: pl.BlockSpec(
        (None, frames, places, D), lambda c, p: (offset * clips + c, 0, p, 0)
    )
    per_clip = lambda rows: pl.BlockSpec((None, rows, D), lambda c, p: (chunk * clips + c, 0, 0))
    shapes = [(D, 3 * D), (D, D), (D, FF), (FF, D)]
    kept = lambda width, kind: pltpu.VMEM((frames, places, width), kind)
    groups = places // GROUP
    return pl.pallas_call(
        functools.partial(temporal_kernel, len(carried), len(before)),
        grid=(clips, spots // places),
        in_specs=[block(0), block(chunk), per_clip(1), per_clip(6)]
        + [weight_spec(*shape, 1) for shape in shapes]
        + [once(shape) for shape in shapes[: len(carried)]]
        + [pl.BlockSpec(memory_space=pl.ANY)] * len(before),
        out_specs=[block(chunk), block(0), pl.BlockSpec((None, 16, D), lambda c, p: (c, 0, 0))]
        + [once(shape) for shape in shapes],
        out_shape=[
            jax.ShapeDtypeStruct(cot.shape, BF),
            jax.ShapeDtypeStruct(x.shape, BF),
            jax.ShapeDtypeStruct((clips, 16, D), F32),
        ]
        + [jax.ShapeDtypeStruct(shape, kind) for shape in shapes],
        scratch_shapes=[pltpu.VMEM(shape, F32) for shape in shapes]
        + [
            kept(3 * D, BF),
            kept(D, BF),
            pltpu.VMEM((groups * 2 * PAIRS, frames * GROUP, frames * GROUP), BF),
            kept(D, F32),
            kept(D, BF),
            kept(3 * D, BF),
        ],
        compiler_params=params(58),
        cost_estimate=cost(36),
        name="temporal",
        input_output_aliases={8 + len(carried): 0} if before else {},
    )(x, cot, codes, mods, *weights, *carried, *before)


def embed_steps(timesteps):
    half_width = D // 2
    frequencies = jnp.exp(
        -math.log(10000.0) * jnp.arange(half_width, dtype=F32) / half_width
    )
    angles = timesteps.astype(F32)[:, None] * frequencies[None, :]
    return jax.nn.silu(jnp.concatenate([jnp.cos(angles), jnp.sin(angles)], axis=-1))


def swap(values):
    return lax.all_to_all(values, "pos", split_axis=0, concat_axis=0, tiled=True)


def sum_clips(parts):
    total = parts[0].astype(F32)
    for s, give in enumerate(parts[1:], 1):
        total += exchange(give, "clip", len(parts), s).astype(F32)
    return total.astype(BF)


def sum_positions(part, n_pos):
    pieces = swap(part.reshape(n_pos, part.shape[0] // n_pos, D))
    return jnp.sum(pieces.astype(F32), axis=0).astype(BF)


INNER = 4


def exchange(values, axis, size, distance):
    return lax.ppermute(values, axis, [(i, i ^ distance) for i in range(size)])


def gather_outer(piece, n_pos):
    rest = [exchange(piece, "pos", n_pos, k * INNER) for k in range(1, n_pos // INNER)]
    return jnp.stack([piece] + rest)


def gather_inner(pieces, n_pos):
    rest = [exchange(pieces, "pos", n_pos, k) for k in range(1, INNER)]
    return [pieces] + rest


def gather_clips(pieces, n_clip):
    return [pieces] + [exchange(pieces, "clip", n_clip, k) for k in range(1, n_clip)]


def place_pieces(where_ref, piece_refs, rows_ref):
    inner, outer, height, _ = piece_refs[0].shape
    for s, piece_ref in enumerate(piece_refs):
        clip = where_ref[1] ^ s
        for p in range(inner * outer):
            owner = where_ref[0] ^ p
            row = (clip * (inner * outer) + owner) * height
            rows_ref[pl.ds(pl.multiple_of(row, height), height)] = piece_ref[p % inner, p // inner]


def unstack(rows_ref, at, out_ref):
    height, width = out_ref.shape
    for start in range(0, width, D):
        out_ref[:, start : start + D] = rows_ref[at : at + height].astype(F32)
        at += height
    return at


def first_block(shape):
    return pl.BlockSpec((None,) + shape, lambda *_: (0, 0, 0))


def outer_products(embed_ref, rows_ref, first, ada_ref):
    n_clips = embed_ref.shape[1]
    for part in range(6):
        total = 0.0
        for clip in range(n_clips):
            row = first + clip * 6 + part
            total += embed_ref[:, clip : clip + 1] * rows_ref[row : row + 1].astype(F32)
        ada_ref[:, part * D : (part + 1) * D] = total


def finish_feed_kernel(n_pieces, square_height, count, where_ref, *refs):
    pieces, embed_ref = refs[:n_pieces], refs[n_pieces]
    *outs, ada_ref, rms_ref, rows_ref = refs[n_pieces + 1 :]
    place_pieces(where_ref, pieces, rows_ref)
    at = 0
    for out_ref in outs:
        at = unstack(rows_ref, at, out_ref)
    outer_products(embed_ref, rows_ref, at, ada_ref)
    at += embed_ref.shape[1] * 6
    total = col_sum(rows_ref[at : at + square_height].astype(F32))
    total = sum(total[:, start : start + D // 3] for start in range(0, D, D // 3))
    rms_ref[...] = jnp.broadcast_to(jnp.sqrt(total / count), rms_ref.shape)


def block_of(shape, block):
    return pl.BlockSpec((None,) + shape, lambda *_: (block, 0, 0))


def finish_feed(where, pieces, embed_columns, square_height, count):
    height = len(pieces) * math.prod(pieces[0].shape[:3])
    ada = (D, 6 * D)
    return pl.pallas_call(
        functools.partial(finish_feed_kernel, len(pieces), square_height, count),
        grid_spec=pltpu.PrefetchScalarGridSpec(
            num_scalar_prefetch=1,
            grid=(1,),
            in_specs=[once(piece.shape) for piece in pieces] + [once(embed_columns.shape)],
            out_specs=[block_of(shape, 0) for shape in FEED_SHAPES]
            + [block_of(ada, 1), whole((8, D // 3))],
            scratch_shapes=[pltpu.VMEM((height, D), BF)],
        ),
        out_shape=[jax.ShapeDtypeStruct((2,) + shape, F32) for shape in FEED_SHAPES + [ada]]
        + [jax.ShapeDtypeStruct((8, D // 3), F32)],
        compiler_params=params(56),
        cost_estimate=cost(5),
        name="finish_feed",
    )(where, *pieces, embed_columns)


def finish_kernel(n_pieces, chunks, where_ref, *refs):
    pieces, refs = refs[:n_pieces], refs[n_pieces:]
    embed_ref, qkv_one_ref, *ones = refs[:5]
    grads = refs[5 : 5 + chunks]
    qkv_ref, ada_ref, *outs, grad_ref, rows_ref = refs[9 + chunks :]
    step = pl.program_id(0)

    @pl.when(step == 0)
    def _():
        place_pieces(where_ref, pieces, rows_ref)

    height = qkv_ref.shape[1]
    for part in range(3):
        start = pl.multiple_of(part * D + step * height, height)
        block = rows_ref[pl.ds(start, height)].astype(F32)
        qkv_ref[0, :, part * D : (part + 1) * D] = block
    qkv_ref[1] = qkv_one_ref[...].astype(F32)
    outer_products(embed_ref, rows_ref, 3 * D, ada_ref)
    for one_ref, out_ref in zip(ones, outs):
        out_ref[...] = one_ref[...].astype(F32)
    per = pl.num_programs(0) // chunks
    for c, ref in enumerate(grads):

        @pl.when(step // per == c)
        def _():
            grad_ref[...] = ref[...].astype(F32)


def finish(where, pieces, embed_columns, qkv_one, ones, ada, halves, grads):
    chunks = len(grads)
    per = 4 // chunks if chunks in (1, 2, 4) else 1
    steps = per * chunks
    height = len(pieces) * math.prod(pieces[0].shape[:3])
    cut = lambda shape: (shape[0] // steps,) + shape[1:]
    piece = (grads[0].shape[0] // per,) + grads[0].shape[1:]
    chunk = lambda c: pl.BlockSpec(
        piece, lambda i, *_: (jnp.minimum(jnp.maximum(i - c * per, 0), per - 1), 0, 0)
    )
    rows = lambda shape: pl.BlockSpec(cut(shape), lambda i, *_: (i, 0))
    block = lambda shape, b: pl.BlockSpec((None,) + cut(shape), lambda i, *_: (b, i, 0))
    first = len(pieces) + 6 + chunks
    return pl.pallas_call(
        functools.partial(finish_kernel, len(pieces), chunks),
        grid_spec=pltpu.PrefetchScalarGridSpec(
            num_scalar_prefetch=1,
            grid=(steps,),
            in_specs=[once(piece.shape) for piece in pieces]
            + [rows(embed_columns.shape), rows(qkv_one.shape)]
            + [rows(one.shape) for one in ones]
            + [chunk(c) for c in range(chunks)]
            + [pl.BlockSpec(memory_space=pl.ANY)] * (1 + len(halves)),
            out_specs=[
                pl.BlockSpec((2, D // steps, 3 * D), lambda i, *_: (0, i, 0)),
                block((D, 6 * D), 0),
            ]
            + [block(one.shape, 1) for one in ones]
            + [pl.BlockSpec(piece, lambda i, *_: (i, 0, 0))],
            scratch_shapes=[pltpu.VMEM((height, D), BF)],
        ),
        out_shape=[
            jax.ShapeDtypeStruct((2, D, 3 * D), F32),
            jax.ShapeDtypeStruct(ada.shape, F32),
        ]
        + [jax.ShapeDtypeStruct(half.shape, F32) for half in halves]
        + [jax.ShapeDtypeStruct((chunks * grads[0].shape[0],) + grads[0].shape[1:], F32)],
        input_output_aliases={first + k: 1 + k for k in range(1 + len(halves))},
        compiler_params=params(56),
        cost_estimate=cost(8),
        name="finish",
    )(where, *pieces, embed_columns, qkv_one, *ones, *grads, ada, *halves)


def round_up(value, unit):
    return -(-value // unit) * unit


def as_one_step(timesteps, function, *operands):
    def skip(*operands):
        shapes = jax.eval_shape(function, *operands)
        return jax.tree.map(lambda leaf: jnp.zeros(leaf.shape, leaf.dtype), shapes)

    return lax.cond(timesteps[0] >= 0, function, skip, *operands)


def on_device(
    tokens,
    timesteps,
    weight_codes,
    cotangent,
    ada_weight,
    qkv_weight,
    out_weight,
    up_weight,
    down_weight,
):
    clips, frames, spots, _ = tokens.shape
    n_pos = lax.axis_size("pos")
    n_clip = lax.axis_size("clip")
    chunks = clips * frames // n_pos
    span = clips // chunks
    n = n_pos * spots
    rows = 512
    places = min(spots, 32)

    n_all = n_pos * n_clip
    n_clips = n_clip * clips
    square_height = n_all
    feed_height = sum(a * b for a, b in FEED_SHAPES) // D + n_clips * 6 + square_height
    feed_height = round_up(feed_height, 16 * n_all)
    tail_height = round_up(3 * D + n_clips * 6, 16 * n_all)
    pos, clip = lax.axis_index("pos"), lax.axis_index("clip")
    mine = pos // frames
    own = clip * clips
    where = [pos, clip, (own + (chunks - 1) * span + mine) * 6, pos % INNER, pos // INNER]
    where = jnp.stack(where).astype(jnp.int32)

    def send(tokens, c):
        return tokens[c * span : (c + 1) * span].reshape(n_pos, spots, D)

    first = swap(send(tokens, 0))
    embedded = embed_steps(timesteps)
    mods = [
        jnp.dot(
            embedded, ada_weight[block].astype(F32), precision=lax.Precision.HIGHEST
        ).reshape(clips, 6, D)
        for block in range(2)
    ]
    embed_rows = lax.all_gather(embedded, "clip", axis=0, tiled=True)
    embed_columns = embed_rows.T
    scaling = jnp.exp2(0.5 * weight_codes.astype(F32) - 1.0)
    codes = jnp.broadcast_to(scaling[:, None, None], (clips, 1, D))
    arrived = [first.reshape(n, D)]
    for c in range(1, chunks):
        held, embed_columns, codes, *mods = lax.optimization_barrier(
            (tokens, embed_columns, codes, *mods)
        )
        arrived.append(swap(send(held, c)).reshape(n, D))

    kept_all = []
    streams = []
    for c in range(chunks):
        x = arrived[c]
        mod = lax.dynamic_index_in_dim(mods[0], c * span + mine, 0, keepdims=False)
        qkv = project(x, mod, qkv_weight, rows)
        att, logs = attend(qkv, 256)
        x_next, *kept, squares = feed(x, att, mod, out_weight, up_weight, down_weight, rows)
        streams.append(swap(x_next.reshape(n_pos, spots, D)).reshape(span, frames, spots, D))
        kept_all.append((x, mod, qkv, att, logs, kept, squares))

    weights = (qkv_weight, out_weight, up_weight, down_weight)
    results, returned, parts_one = (), [], []
    carried = ()
    for c in range(chunks):
        kind = BF
        result, g, part, *carried = temporal(
            streams[c], cotangent, c, codes, mods[1], weights, carried, results, kind, places
        )
        results = (result,)
        parts_one.append(part)
        returned.append(swap(g.reshape(n_pos, spots, D)).reshape(n, D))
    sums_one = carried

    def extra_rows(parts_one, squares_zero):
        part_one = jnp.concatenate(parts_one, axis=0)
        squares_zero = sum(squares_zero)[:3]
        squares_one = jnp.sum(part_one[:, 6:9], axis=0)
        squares = jnp.sum(jnp.concatenate([squares_zero, squares_one], axis=0), axis=1)
        terms = []
        for _ in range(3):
            kept = lax.reduce_precision(squares, exponent_bits=8, mantissa_bits=7)
            terms.append(kept.astype(BF))
            squares = squares - kept
        terms = jnp.pad(jnp.stack(terms), ((0, 0), (0, D // 3 - 6))).reshape(1, D)
        square_rows = lax.dynamic_update_slice(
            jnp.zeros((square_height, D), BF), terms, (pos * n_clip + clip, 0)
        )
        mod_one = lax.dynamic_update_slice(
            jnp.zeros((n_clips, 6, D), BF), part_one[:, :6].astype(BF), (own, 0, 0)
        )
        return jnp.concatenate([mod_one.reshape(n_clips * 6, D), square_rows], axis=0)

    def back_of_feed(c, g, carried, extra):
        x, mod, qkv, att, logs, kept, squares = kept_all[c]
        weights = (out_weight, up_weight, down_weight)
        n_parts = n_clip if c == chunks - 1 else 0
        return feed_back(
            where, extra, g, kept, att, mod, *weights, carried, BF, 256, feed_height, n_parts
        )

    def back_of_project(c, found, gmid, mods, carried):
        x, mod, qkv, att, logs, kept, squares = kept_all[c]
        n_parts = n_clip if c == chunks - 1 else 0
        found = [third[k] for k in range(3) for third in found]
        g, part, *carried = project_back(
            where, mods, x, found, gmid, mod, qkv_weight, carried, rows, tail_height, n_parts
        )
        return g.reshape(n_pos, spots, D), part[:6], carried

    def some_pairs(c, gatt, first, count):
        x, mod, qkv, att, logs, kept, squares = kept_all[c]
        return attend_back(qkv, att, logs, gatt, first, count, rows)

    def last_block_back(later, middle, found, carried, extra):
        middles = [middle]
        for c in range(1, chunks):
            gmid, gatt, part, *carried = back_of_feed(c, later[c - 1], carried, extra)
            middles.append((gmid, gatt, part))
        feed_part = sum_clips(carried)
        carried = ()
        grads = []
        mods = jnp.zeros((n_clips, 6, D), F32)
        for c, (gmid, gatt, part) in enumerate(middles):
            if c == 0:
                feed_part, gatt = lax.optimization_barrier((feed_part, gatt))
                feed_piece = sum_positions(feed_part, n_pos)
                found = [found]
            else:
                found = [some_pairs(c, gatt, 0, 2)]
            if c == chunks - 1:
                break
            found.append(some_pairs(c, gatt, 1, 2))
            grad, part_first, carried = back_of_project(c, found, gmid, mods.reshape(-1, D), carried)
            grads.append(grad)
            mods = lax.dynamic_update_index_in_dim(
                mods, part[:6] + part_first, own + c * span + mine, 0
            )
        mods = lax.dynamic_update_index_in_dim(mods, part[:6], own + (chunks - 1) * span + mine, 0)
        mods = mods.reshape(-1, D)

        gatt, found, feed_piece, *grads = lax.optimization_barrier((gatt, found, feed_piece, *grads))
        feed_pieces = gather_outer(feed_piece, n_pos)

        def last_step(grads, gatt, found, gmid, mods, carried):
            grads = [swap(grad) for grad in grads]
            done = 2 if chunks > 1 else 1
            found = found + [some_pairs(chunks - 1, gatt, done, PAIRS - done)]
            grad, _, parts = back_of_project(chunks - 1, found, gmid, mods, carried)
            return grads, grad, sum_clips(parts)

        grads, grad, part = as_one_step(
            timesteps, last_step, grads, gatt, found, gmid, mods, carried
        )
        part, feed_pieces = lax.optimization_barrier((part, feed_pieces))
        feed_pieces = gather_inner(feed_pieces, n_pos)
        piece = as_one_step(timesteps, lambda part: sum_positions(part, n_pos), part)
        piece, feed_pieces = lax.optimization_barrier((piece, feed_pieces))
        feed_pieces = gather_clips(jnp.stack(feed_pieces), n_clip)
        tail_pieces = as_one_step(timesteps, lambda piece: gather_outer(piece, n_pos), piece)
        grad, feed_pieces, tail_pieces = lax.optimization_barrier((grad, feed_pieces, tail_pieces))
        grads.append(swap(grad))
        tail_pieces = gather_inner(tail_pieces, n_pos)

        def feed_step(feed_pieces):
            count = clips * frames * spots * n_all
            return finish_feed(where, feed_pieces, embed_columns, square_height, count)

        *halves, ada_grad, rms = as_one_step(timesteps, feed_step, feed_pieces)
        tail_pieces, ada_grad = lax.optimization_barrier((tail_pieces, ada_grad))
        tail_pieces = gather_clips(jnp.stack(tail_pieces), n_clip)
        stream_rms = rms[0, :6].reshape(2, 3)
        return grads, tail_pieces, embed_columns, ada_grad, stream_rms, halves

    all_squares = [kept[-1] for kept in kept_all]
    if chunks > 1:
        unused = mods[0][0]
        gmid, gatt, part, *carried = back_of_feed(0, returned[0], (), unused)
        gatt, parts_one, all_squares = lax.optimization_barrier((gatt, parts_one, all_squares))
        extra = extra_rows(parts_one, all_squares)
    else:
        extra = extra_rows(parts_one, all_squares)
        gmid, gatt, part, *carried = back_of_feed(0, returned[0], (), extra)
    found = some_pairs(0, gatt, 0, 1)
    grads, tail_pieces, embed_columns, ada_grad, stream_rms, halves = as_one_step(
        timesteps, last_block_back, returned[1:], (gmid, gatt, part), found, carried, extra
    )
    qkv_one, out_one, up_one, down_one = lax.psum(tuple(sums_one), ("pos", "clip"))
    qkv_grad, ada_grad, up_grad, down_grad, out_grad, grad_tokens = finish(
        where,
        tail_pieces,
        embed_columns,
        qkv_one,
        (up_one, down_one, out_one),
        ada_grad,
        halves,
        grads,
    )
    return (
        results[0],
        grad_tokens.reshape(tokens.shape),
        ada_grad,
        qkv_grad,
        out_grad,
        up_grad,
        down_grad,
        stream_rms,
    )


def solution(mesh):
    placed = (
        P("clip", None, "pos", None),
        P("clip"),
        P("clip"),
        P("clip", None, "pos", None),
        P(),
        P(),
        P(),
        P(),
        P(),
    )
    return jax.shard_map(
        on_device,
        mesh=mesh,
        in_specs=placed,
        out_specs=(
            P("clip", None, "pos", None),
            P("clip", None, "pos", None),
            P(),
            P(),
            P(),
            P(),
            P(),
            P(),
        ),
        check_vma=False,
    )
```

```python
import functools
import math

import jax
import jax.numpy as jnp
from jax import lax
from jax.experimental import pallas as pl
from jax.experimental.pallas import tpu as pltpu
from jax.sharding import PartitionSpec as P

D = 384
HEAD = 64
PAIRS = 3
FF = 1536
EPS = 1e-06
LOG_SCALE = HEAD**-0.5 * math.log2(math.e)
GROUP = 16
FEED_SHAPES = [(D, FF), (FF, D), (D, D)]

NN = (((1,), (0,)), ((), ()))
NT = (((1,), (1,)), ((), ()))
TN = (((0,), (0,)), ((), ()))
F32 = jnp.float32
BF = jnp.bfloat16


def mm(left, right, dims=NN):
    return lax.dot_general(left, right, dims, preferred_element_type=F32)


def params(mebibytes):
    return pltpu.CompilerParams(vmem_limit_bytes=mebibytes * 2**20)


def cost(micros):
    return pl.CostEstimate(
        flops=int(micros * 1e9), transcendentals=0, bytes_accessed=int(micros * 3e6)
    )


def norm_rows(values):
    center = values - jnp.mean(values, axis=-1, keepdims=True)
    rstd = lax.rsqrt(jnp.mean(center * center, axis=-1, keepdims=True) + EPS)
    return center * rstd, rstd


def norm_back(grad_normed, normed, rstd):
    mean_grad = jnp.mean(grad_normed, axis=-1, keepdims=True)
    mean_cross = jnp.mean(grad_normed * normed, axis=-1, keepdims=True)
    return rstd * (grad_normed - mean_grad - normed * mean_cross)


def col_sum(values):
    return jnp.sum(values, axis=0, keepdims=True)


def gelu_pair(inner):
    square = inner * inner
    slope = math.sqrt(2.0 / math.pi)
    tanh = jnp.tanh(inner * (slope + (slope * 0.044715) * square))
    half = 0.5 + 0.5 * tanh
    value = inner * half
    grad = half + (value * (1.0 - tanh)) * (slope + (3.0 * 0.044715 * slope) * square)
    return value, grad


def low_lanes():
    return lax.broadcasted_iota(jnp.int32, (1, 2 * HEAD), 1) < HEAD


def both_heads(values, low, fill=0.0):
    other = jnp.full_like(values, fill)
    return (jnp.where(low, values, other), jnp.where(low, other, values))


def whole(shape):
    return pl.BlockSpec(shape, lambda *_: (0,) * len(shape))


def once(shape):
    return pl.BlockSpec(shape, lambda *_: (0,) * len(shape), pipeline_mode=pl.Buffered(1))


def weight_spec(rows, cols, block):
    return pl.BlockSpec((None, rows, cols), lambda *_: (block, 0, 0), pipeline_mode=pl.Buffered(1))


def project_kernel(x_ref, mod_ref, w_ref, out_ref):
    normed, _ = norm_rows(x_ref[...].astype(F32))
    hidden = (normed * (1.0 + mod_ref[1:2]) + mod_ref[0:1]).astype(BF)
    out_ref[...] = mm(hidden, w_ref[...]).astype(BF)


def project(x, mod, qkv_weight, rows):
    n = x.shape[0]
    return pl.pallas_call(
        project_kernel,
        grid=(n // rows,),
        in_specs=[
            pl.BlockSpec((rows, D), lambda i: (i, 0)),
            whole((6, D)),
            weight_spec(D, 3 * D, 0),
        ],
        out_specs=pl.BlockSpec((rows, 3 * D), lambda i: (i, 0)),
        out_shape=jax.ShapeDtypeStruct((n, 3 * D), BF),
        compiler_params=params(16),
        cost_estimate=cost(5),
        name="project",
    )(x, mod, qkv_weight)


def attend_kernel(rows, q_ref, k_ref, v_ref, out_ref, log_ref):
    low = low_lanes()
    keys = k_ref[...]
    values = both_heads(v_ref[...], low, 1.0)
    tasks = [(start, head) for start in range(0, q_ref.shape[0], rows) for head in range(2)]

    def score(task):
        start, head = task
        q = q_ref[start : start + rows, :]
        return mm(both_heads(q, low)[head], keys, NT)

    ahead = score(tasks[0])
    mixed, tops = [], []
    for index, (start, head) in enumerate(tasks):
        scores = ahead
        if index + 1 < len(tasks):
            ahead = score(tasks[index + 1])
        top = jnp.max(scores, axis=1, keepdims=True)
        raised = jnp.exp2((scores - top) * LOG_SCALE).astype(BF)
        mixed.append(mm(raised, values[head]))
        tops.append(top * LOG_SCALE)
        if head == 1:
            part = slice(start, start + rows)
            total = pltpu.roll(jnp.where(low, mixed[1], mixed[0]), HEAD, 1)
            out_ref[part, :] = (jnp.where(low, mixed[0], mixed[1]) / total).astype(BF)
            log_ref[part, :] = jnp.where(low, tops[0], tops[1]) + jnp.log2(total)
            mixed, tops = [], []


def attend(qkv, rows):
    n = qkv.shape[0]
    pair = lambda start: pl.BlockSpec((n, 2 * HEAD), lambda p: (0, start + p))
    return pl.pallas_call(
        functools.partial(attend_kernel, rows),
        grid=(PAIRS,),
        in_specs=[pair(0), pair(PAIRS), pair(2 * PAIRS)],
        out_specs=[pair(0), pair(0)],
        out_shape=[jax.ShapeDtypeStruct((n, D), BF), jax.ShapeDtypeStruct((n, D), F32)],
        compiler_params=params(24),
        cost_estimate=cost(14),
        name="attend",
    )(qkv, qkv, qkv)


def feed_kernel(
    x_ref,
    att_ref,
    mod_ref,
    wo_ref,
    wu_ref,
    wd_ref,
    next_ref,
    middle_ref,
    branch_ref,
    mlp_ref,
    act_ref,
    slope_ref,
    squares_ref,
):
    @pl.when(pl.program_id(0) == 0)
    def _():
        squares_ref[...] = jnp.zeros_like(squares_ref)

    x = x_ref[...].astype(F32)
    branch = mm(att_ref[...], wo_ref[...])
    gated = mod_ref[2:3] * branch
    middle = x + gated
    normed, _ = norm_rows(middle)
    hidden = (normed * (1.0 + mod_ref[4:5]) + mod_ref[3:4]).astype(BF)
    value, slope = gelu_pair(mm(hidden, wu_ref[...]))
    act = value.astype(BF)
    mlp = mm(act, wd_ref[...])
    fed = mod_ref[5:6] * mlp
    next_ref[...] = (middle + fed).astype(BF)
    middle_ref[...] = middle.astype(BF)
    branch_ref[...] = branch.astype(BF)
    mlp_ref[...] = mlp.astype(BF)
    act_ref[...] = act
    slope_ref[...] = slope.astype(BF)
    squares_ref[0:1] += col_sum(x * x)
    squares_ref[1:2] += col_sum(gated * gated)
    squares_ref[2:3] += col_sum(fed * fed)


def feed(x, att, mod, out_weight, up_weight, down_weight, rows):
    n = x.shape[0]
    row = lambda width: pl.BlockSpec((rows, width), lambda i: (i, 0))
    out = lambda width, kind: jax.ShapeDtypeStruct((n, width), kind)
    return pl.pallas_call(
        feed_kernel,
        grid=(n // rows,),
        in_specs=[
            row(D),
            row(D),
            whole((6, D)),
            weight_spec(D, D, 0),
            weight_spec(D, FF, 0),
            weight_spec(FF, D, 0),
        ],
        out_specs=[row(D), row(D), row(D), row(D), row(FF), row(FF), whole((8, D))],
        out_shape=[
            out(D, BF),
            out(D, BF),
            out(D, BF),
            out(D, BF),
            out(FF, BF),
            out(FF, BF),
            jax.ShapeDtypeStruct((8, D), F32),
        ],
        compiler_params=params(56),
        cost_estimate=cost(11),
        name="feed",
    )(x, att, mod, out_weight, up_weight, down_weight)


def start_sums(sums, carried):
    for index, total in enumerate(sums):
        total[...] = carried[index][...].astype(F32) if carried else jnp.zeros_like(total)


def row_blocks(total):
    height, width = total.shape
    return [(start, height) for start in range(0, width, D)]


def load_rows(rows_ref, sums):
    at = 0
    for total in sums:
        for start, height in row_blocks(total):
            total[:, start : start + D] = rows_ref[at : at + height].astype(F32)
            at += height


def store_rows(sums, rows_ref, extra=None):
    at = 0
    for total in sums:
        for start, height in row_blocks(total):
            rows_ref[at : at + height] = total[:, start : start + D].astype(rows_ref.dtype)
            at += height
    if extra is not None:
        rows_ref[at : at + extra.shape[0]] = extra.astype(rows_ref.dtype)
        at += extra.shape[0]
    if at < rows_ref.shape[0]:
        rows_ref[at:] = jnp.zeros((rows_ref.shape[0] - at, D), rows_ref.dtype)


def store_parts(where_ref, held_ref, rows_refs):
    part = rows_refs[0].shape[0]
    for s, rows_ref in enumerate(rows_refs):
        start = pl.multiple_of((where_ref[1] ^ s) * part, part)
        rows_ref[...] = held_ref[pl.ds(start, part)]


def feed_back_kernel(n_carried, n_parts, where_ref, extra_ref, *refs):
    (
        g_ref,
        middle_ref,
        branch_ref,
        mlp_ref,
        act_ref,
        slope_ref,
        att_ref,
        mod_ref,
        wo_ref,
        wu_ref,
        wd_ref,
    ) = refs[:11]
    carried = refs[11 : 11 + n_carried]
    gmid_ref, gatt_ref, part_ref = refs[11 + n_carried : 14 + n_carried]
    n_out = max(n_parts, 1)
    rows_refs = refs[14 + n_carried : 14 + n_carried + n_out]
    *sums, held_ref = refs[14 + n_carried + n_out :]

    @pl.when(pl.program_id(0) == 0)
    def _():
        part_ref[...] = jnp.zeros_like(part_ref)
        if carried:
            load_rows(carried[0], sums)
        else:
            start_sums(sums, ())

    up_sum, down_sum, out_sum = sums
    g = g_ref[...].astype(F32)
    part_ref[5:6] += col_sum(mlp_ref[...].astype(F32) * g)
    gm = (mod_ref[5:6] * g).astype(BF)
    down_sum[...] += mm(act_ref[...], gm, TN)
    gi = (slope_ref[...].astype(F32) * mm(gm, wd_ref[...], NT)).astype(BF)
    normed, rstd = norm_rows(middle_ref[...].astype(F32))
    scale = 1.0 + mod_ref[4:5]
    hidden = (normed * scale + mod_ref[3:4]).astype(BF)
    up_sum[...] += mm(hidden, gi, TN)
    gh = mm(gi, wu_ref[...], NT)
    part_ref[3:4] += col_sum(gh)
    part_ref[4:5] += col_sum(gh * normed)
    gmid = g + norm_back(gh * scale, normed, rstd)
    gmid_ref[...] = gmid
    part_ref[2:3] += col_sum(branch_ref[...].astype(F32) * gmid)
    gb = (mod_ref[2:3] * gmid).astype(BF)
    out_sum[...] += mm(att_ref[...], gb, TN)
    gatt_ref[...] = mm(gb, wo_ref[...], NT).astype(BF)

    @pl.when(pl.program_id(0) == pl.num_programs(0) - 1)
    def _():
        if n_parts == 0:
            store_rows(sums, rows_refs[0])
        else:
            store_rows(sums, held_ref, extra_ref[...])
            store_parts(where_ref, held_ref, rows_refs)


def feed_back(where, extra, g, kept, att, mod, out_weight, up_weight, down_weight, carried, kind, rows, height, n_parts):
    n = g.shape[0]
    row = lambda width: pl.BlockSpec((rows, width), lambda i, *_: (i, 0))
    shapes = FEED_SHAPES
    n_out = max(n_parts, 1)
    return pl.pallas_call(
        functools.partial(feed_back_kernel, len(carried), n_parts),
        grid=(n // rows,),
        in_specs=[
            pl.BlockSpec(memory_space=pltpu.SMEM),
            whole(extra.shape),
            row(D),
            row(D),
            row(D),
            row(D),
            row(FF),
            row(FF),
            row(D),
            whole((6, D)),
            weight_spec(D, D, 0),
            weight_spec(D, FF, 0),
            weight_spec(FF, D, 0),
        ]
        + [once((height, D))] * len(carried),
        out_specs=[row(D), row(D), whole((8, D)), once((height // n_out, D))]
        + [once((height // n_out, D))] * (n_out - 1),
        out_shape=[
            jax.ShapeDtypeStruct((n, D), F32),
            jax.ShapeDtypeStruct((n, D), BF),
            jax.ShapeDtypeStruct((8, D), F32),
        ]
        + [jax.ShapeDtypeStruct((height // n_out, D), kind)] * n_out,
        scratch_shapes=[pltpu.VMEM(shape, F32) for shape in shapes] + [pltpu.VMEM((height, D), BF)],
        compiler_params=params(36 if n_parts else 56),
        cost_estimate=cost(16),
        name="feed_back",
    )(where, extra, g, *kept, att, mod, out_weight, up_weight, down_weight, *carried)


def attend_back_kernel(
    rows, q_ref, k_ref, v_ref, o_ref, log_ref, g_ref, dq_ref, dk_ref, dv_ref
):
    low = low_lanes()
    keys, values = k_ref[...], v_ref[...]
    tasks = [(start, head) for start in range(0, q_ref.shape[0], rows) for head in range(2)]

    def begin(task):
        start, head = task
        part = slice(start, start + rows)
        query = both_heads(q_ref[part, :], low)[head]
        grad = both_heads(g_ref[part, :], low)[head]
        return query, grad, mm(query, keys, NT), mm(grad, values, NT)

    ahead = begin(tasks[0])
    found = []
    for index, (start, head) in enumerate(tasks):
        query, grad, scores, grad_probs = ahead
        if index + 1 < len(tasks):
            ahead = begin(tasks[index + 1])
        part = slice(start, start + rows)
        delta = jnp.sum(grad.astype(F32) * o_ref[part, :].astype(F32), axis=1, keepdims=True)
        log = log_ref[part, HEAD * head : HEAD * head + 1]
        probs = jnp.exp2(scores * LOG_SCALE - log)
        grad_scores = (probs * (grad_probs - delta)).astype(BF)
        found.append(mm(grad_scores, keys))
        values_part = mm(grad.T, probs.astype(BF))
        keys_part = mm(query.T, grad_scores)
        dv = values_part if index == 0 else dv + values_part
        dk = keys_part if index == 0 else dk + keys_part
        if head == 1:
            dq_ref[part, :] = (jnp.where(low, found[0], found[1]) * HEAD**-0.5).astype(BF)
            found = []
    dk_ref[...] = (dk * HEAD**-0.5).T.astype(BF)
    dv_ref[...] = dv.T.astype(BF)


def attend_back(qkv, att, logs, grad, first, count, rows):
    n = qkv.shape[0]
    pair = lambda start: pl.BlockSpec((n, 2 * HEAD), lambda p: (0, start + p))
    return pl.pallas_call(
        functools.partial(attend_back_kernel, rows),
        grid=(count,),
        in_specs=[pair(third * PAIRS + first) for third in (0, 1, 2, 0, 0, 0)],
        out_specs=[pair(0)] * 3,
        out_shape=[jax.ShapeDtypeStruct((n, count * 2 * HEAD), BF)] * 3,
        compiler_params=params(24),
        cost_estimate=cost(5 * count),
        name="attend_back",
    )(qkv, qkv, qkv, att, logs, grad)


def project_back_kernel(n_grads, n_carried, n_parts, where_ref, mods_ref, *refs):
    grad_refs, refs = refs[:n_grads], refs[n_grads:]
    x_ref, gmid_ref, mod_ref, w_ref = refs[:4]
    carried = refs[4 : 4 + n_carried]
    out_ref, part_ref = refs[4 + n_carried : 6 + n_carried]
    *rows_refs, total, held_ref, mods_sum = refs[6 + n_carried :]

    @pl.when(pl.program_id(0) == 0)
    def _():
        part_ref[...] = jnp.zeros_like(part_ref)
        if carried:
            load_rows(carried[0], [total])
        else:
            start_sums([total], ())

    normed, rstd = norm_rows(x_ref[...].astype(F32))
    scale = 1.0 + mod_ref[1:2]
    hidden = (normed * scale + mod_ref[0:1]).astype(BF)
    gp = jnp.concatenate([ref[...] for ref in grad_refs], axis=1)
    total[...] += mm(hidden, gp, TN)
    gh = mm(gp, w_ref[...], NT)
    part_ref[0:1] += col_sum(gh)
    part_ref[1:2] += col_sum(gh * normed)
    out_ref[...] = (gmid_ref[...] + norm_back(gh * scale, normed, rstd)).astype(BF)

    @pl.when(pl.program_id(0) == pl.num_programs(0) - 1)
    def _():
        if n_parts == 0:
            store_rows([total], rows_refs[0])
        else:
            mods_sum[...] = mods_ref[...]
            for k in range(2):
                mods_sum[pl.ds(where_ref[2] + k, 1)] += part_ref[k : k + 1]
            store_rows([total], held_ref, mods_sum[...])
            store_parts(where_ref, held_ref, rows_refs)


def project_back(where, mods, x, grads, gmid, mod, qkv_weight, carried, rows, height, n_parts):
    n = x.shape[0]
    row = lambda width: pl.BlockSpec((rows, width), lambda i: (i, 0))
    n_out = max(n_parts, 1)
    if n_parts == 0:
        height = 3 * D
    return pl.pallas_call(
        functools.partial(project_back_kernel, len(grads), len(carried), n_parts),
        grid=(n // rows,),
        in_specs=[pl.BlockSpec(memory_space=pltpu.SMEM), whole(mods.shape)]
        + [row(grad.shape[1]) for grad in grads]
        + [row(D), row(D), whole((6, D)), weight_spec(D, 3 * D, 0)]
        + [once((3 * D, D))] * len(carried),
        out_specs=[row(D), whole((8, D))] + [once((height // n_out, D))] * n_out,
        out_shape=[
            jax.ShapeDtypeStruct((n, D), BF),
            jax.ShapeDtypeStruct((8, D), F32),
        ]
        + [jax.ShapeDtypeStruct((height // n_out, D), BF)] * n_out,
        scratch_shapes=[
            pltpu.VMEM((D, 3 * D), F32),
            pltpu.VMEM((height, D), BF),
            pltpu.VMEM(mods.shape, F32),
        ],
        compiler_params=params(24),
        cost_estimate=cost(4),
        name="project_back",
    )(where, mods, *grads, x, gmid, mod, qkv_weight, *carried)


def temporal_kernel(n_carried, n_before, *refs):
    x_ref, cot_ref, code_ref, mod_ref, wq_ref, wo_ref, wu_ref, wd_ref = refs[:8]
    carried = refs[8 : 8 + n_carried]
    refs = refs[8 + n_carried + n_before :]
    act_out_ref, g_ref, part_ref = refs[:3]
    out_refs = refs[3:7]
    sums = refs[7:11]
    qkv_ref, att_ref, probs_ref, inv_ref, gatt_ref, gqkv_ref = refs[11:]
    frames, places = x_ref.shape[0], x_ref.shape[1]
    tokens = frames * places
    wide = frames * GROUP
    first = jnp.logical_and(pl.program_id(0) == 0, pl.program_id(1) == 0)
    last = jnp.logical_and(
        pl.program_id(0) == pl.num_programs(0) - 1, pl.program_id(1) == pl.num_programs(1) - 1
    )

    @pl.when(first)
    def _():
        start_sums(sums, carried)

    @pl.when(pl.program_id(1) == 0)
    def _():
        part_ref[...] = jnp.zeros_like(part_ref)

    qkv_sum, out_sum, up_sum, down_sum = sums
    low = low_lanes()
    mod = mod_ref[...]
    x = x_ref[...].reshape(tokens, D).astype(F32)
    normed, rstd = norm_rows(x)
    scale = 1.0 + mod[1:2]
    hidden = (normed * scale + mod[0:1]).astype(BF)
    qkv_ref[...] = mm(hidden, wq_ref[...]).astype(BF).reshape(qkv_ref.shape)

    place = lambda axis: lax.broadcasted_iota(jnp.int32, (wide, wide), axis) % GROUP
    same = place(0) == place(1)
    groups = places // GROUP

    def cut(ref, group, column):
        rows = slice(group * GROUP, (group + 1) * GROUP)
        return ref[:, rows, column * 2 * HEAD : (column + 1) * 2 * HEAD].reshape(wide, 2 * HEAD)

    def put(ref, group, column, value):
        rows = slice(group * GROUP, (group + 1) * GROUP)
        ref[:, rows, column * 2 * HEAD : (column + 1) * 2 * HEAD] = value.reshape(
            frames, GROUP, 2 * HEAD
        )

    tasks = [(g, pair, head) for g in range(groups) for pair in range(PAIRS) for head in range(2)]

    def score(task):
        group, pair, head = task
        query = both_heads(cut(qkv_ref, group, pair), low)[head]
        return mm(query, cut(qkv_ref, group, PAIRS + pair), NT)

    ahead = score(tasks[0])
    mixed = []
    for index, (group, pair, head) in enumerate(tasks):
        scores = jnp.where(same, ahead, -1e38)
        if index + 1 < len(tasks):
            ahead = score(tasks[index + 1])
        top = jnp.max(scores, axis=1, keepdims=True)
        raised = jnp.exp2((scores - top) * LOG_SCALE).astype(BF)
        probs_ref[index] = raised
        mixed.append(mm(raised, both_heads(cut(qkv_ref, group, 2 * PAIRS + pair), low, 1.0)[head]))
        if head == 1:
            inverse = 1.0 / pltpu.roll(jnp.where(low, mixed[1], mixed[0]), HEAD, 1)
            put(inv_ref, group, pair, inverse)
            put(att_ref, group, pair, (jnp.where(low, mixed[0], mixed[1]) * inverse).astype(BF))
            mixed = []

    att = att_ref[...].reshape(tokens, D)
    branch = mm(att, wo_ref[...])
    gated = mod[2:3] * branch
    middle = x + gated
    normed_two, rstd_two = norm_rows(middle)
    scale_two = 1.0 + mod[4:5]
    hidden_two = (normed_two * scale_two + mod[3:4]).astype(BF)
    value, slope = gelu_pair(mm(hidden_two, wu_ref[...]))
    act = value.astype(BF)
    mlp = mm(act, wd_ref[...])
    fed = mod[5:6] * mlp
    act_out_ref[...] = (middle + fed).astype(BF).reshape(act_out_ref.shape)
    part_ref[6:7] += col_sum(x * x)
    part_ref[7:8] += col_sum(gated * gated)
    part_ref[8:9] += col_sum(fed * fed)

    g = cot_ref[...].reshape(tokens, D).astype(F32) * code_ref[0:1]
    part_ref[5:6] += col_sum(mlp * g)
    gm = (mod[5:6] * g).astype(BF)
    down_sum[...] += mm(act, gm, TN)
    gi = (slope * mm(gm, wd_ref[...], NT)).astype(BF)
    up_sum[...] += mm(hidden_two, gi, TN)
    gh = mm(gi, wu_ref[...], NT)
    part_ref[3:4] += col_sum(gh)
    part_ref[4:5] += col_sum(gh * normed_two)
    gmid = g + norm_back(gh * scale_two, normed_two, rstd_two)
    part_ref[2:3] += col_sum(branch * gmid)
    gb = (mod[2:3] * gmid).astype(BF)
    out_sum[...] += mm(att, gb, TN)
    gatt_ref[...] = mm(gb, wo_ref[...], NT).astype(BF).reshape(gatt_ref.shape)

    def begin(task):
        group, pair, head = task
        grad = both_heads(cut(gatt_ref, group, pair), low)[head]
        return grad, mm(grad, cut(qkv_ref, group, 2 * PAIRS + pair), NT)

    ahead = begin(tasks[0])
    found = []
    for index, (group, pair, head) in enumerate(tasks):
        grad, grad_probs = ahead
        if index + 1 < len(tasks):
            ahead = begin(tasks[index + 1])
        query = both_heads(cut(qkv_ref, group, pair), low)[head]
        cross = grad.astype(F32) * cut(att_ref, group, pair).astype(F32)
        delta = jnp.sum(cross, axis=1, keepdims=True)
        inverse = cut(inv_ref, group, pair)[:, HEAD * head : HEAD * head + 1]
        probs = probs_ref[index].astype(F32) * inverse
        grad_scores = (probs * (grad_probs - delta)).astype(BF)
        found.append(mm(grad_scores, cut(qkv_ref, group, PAIRS + pair)))
        values_part = mm(grad.T, probs.astype(BF))
        keys_part = mm(query.T, grad_scores)
        if head == 0:
            dv, dk = values_part, keys_part
        else:
            dq = jnp.where(low, found[0], found[1])
            put(gqkv_ref, group, pair, (dq * HEAD**-0.5).astype(BF))
            put(gqkv_ref, group, PAIRS + pair, ((dk + keys_part) * HEAD**-0.5).T.astype(BF))
            put(gqkv_ref, group, 2 * PAIRS + pair, (dv + values_part).T.astype(BF))
            found = []

    gp = gqkv_ref[...].reshape(tokens, 3 * D)
    qkv_sum[...] += mm(hidden, gp, TN)
    gh_one = mm(gp, wq_ref[...], NT)
    part_ref[0:1] += col_sum(gh_one)
    part_ref[1:2] += col_sum(gh_one * normed)
    g_next = gmid + norm_back(gh_one * scale, normed, rstd)
    g_ref[...] = g_next.astype(BF).reshape(g_ref.shape)

    @pl.when(last)
    def _():
        for total, out_ref in zip(sums, out_refs):
            out_ref[...] = total[...].astype(out_ref.dtype)


def temporal(x, cot, chunk, codes, mods, weights, carried, before, kind, places):
    clips, frames, spots, _ = x.shape
    block = lambda offset: pl.BlockSpec(
        (None, frames, places, D), lambda c, p: (offset * clips + c, 0, p, 0)
    )
    per_clip = lambda rows: pl.BlockSpec((None, rows, D), lambda c, p: (chunk * clips + c, 0, 0))
    shapes = [(D, 3 * D), (D, D), (D, FF), (FF, D)]
    kept = lambda width, kind: pltpu.VMEM((frames, places, width), kind)
    groups = places // GROUP
    return pl.pallas_call(
        functools.partial(temporal_kernel, len(carried), len(before)),
        grid=(clips, spots // places),
        in_specs=[block(0), block(chunk), per_clip(1), per_clip(6)]
        + [weight_spec(*shape, 1) for shape in shapes]
        + [once(shape) for shape in shapes[: len(carried)]]
        + [pl.BlockSpec(memory_space=pl.ANY)] * len(before),
        out_specs=[block(chunk), block(0), pl.BlockSpec((None, 16, D), lambda c, p: (c, 0, 0))]
        + [once(shape) for shape in shapes],
        out_shape=[
            jax.ShapeDtypeStruct(cot.shape, BF),
            jax.ShapeDtypeStruct(x.shape, BF),
            jax.ShapeDtypeStruct((clips, 16, D), F32),
        ]
        + [jax.ShapeDtypeStruct(shape, kind) for shape in shapes],
        scratch_shapes=[pltpu.VMEM(shape, F32) for shape in shapes]
        + [
            kept(3 * D, BF),
            kept(D, BF),
            pltpu.VMEM((groups * 2 * PAIRS, frames * GROUP, frames * GROUP), BF),
            kept(D, F32),
            kept(D, BF),
            kept(3 * D, BF),
        ],
        compiler_params=params(58),
        cost_estimate=cost(36),
        name="temporal",
        input_output_aliases={8 + len(carried): 0} if before else {},
    )(x, cot, codes, mods, *weights, *carried, *before)


def embed_steps(timesteps):
    half_width = D // 2
    frequencies = jnp.exp(
        -math.log(10000.0) * jnp.arange(half_width, dtype=F32) / half_width
    )
    angles = timesteps.astype(F32)[:, None] * frequencies[None, :]
    return jax.nn.silu(jnp.concatenate([jnp.cos(angles), jnp.sin(angles)], axis=-1))


def swap(values):
    return lax.all_to_all(values, "pos", split_axis=0, concat_axis=0, tiled=True)


def sum_clips(parts):
    total = parts[0].astype(F32)
    for s, give in enumerate(parts[1:], 1):
        total += exchange(give, "clip", len(parts), s).astype(F32)
    return total.astype(BF)


def sum_positions(part, n_pos):
    pieces = swap(part.reshape(n_pos, part.shape[0] // n_pos, D))
    return jnp.sum(pieces.astype(F32), axis=0).astype(BF)


INNER = 4


def exchange(values, axis, size, distance):
    return lax.ppermute(values, axis, [(i, i ^ distance) for i in range(size)])


def gather_outer(piece, n_pos):
    rest = [exchange(piece, "pos", n_pos, k * INNER) for k in range(1, n_pos // INNER)]
    return jnp.stack([piece] + rest)


def gather_inner(pieces, n_pos):
    rest = [exchange(pieces, "pos", n_pos, k) for k in range(1, INNER)]
    return [pieces] + rest


def gather_clips(pieces, n_clip):
    return [pieces] + [exchange(pieces, "clip", n_clip, k) for k in range(1, n_clip)]


def place_pieces(where_ref, piece_refs, rows_ref):
    inner, outer, height, _ = piece_refs[0].shape
    for s, piece_ref in enumerate(piece_refs):
        clip = where_ref[1] ^ s
        for p in range(inner * outer):
            owner = where_ref[0] ^ p
            row = (clip * (inner * outer) + owner) * height
            piece = piece_ref[p % inner, p // inner].astype(rows_ref.dtype)
            rows_ref[pl.ds(pl.multiple_of(row, height), height)] = piece


def unstack(rows_ref, at, out_ref):
    height, width = out_ref.shape
    for start in range(0, width, D):
        out_ref[:, start : start + D] = rows_ref[at : at + height].astype(F32)
        at += height
    return at


def first_block(shape):
    return pl.BlockSpec((None,) + shape, lambda *_: (0, 0, 0))


def outer_products(embed_ref, rows_ref, first, ada_ref):
    n_clips = embed_ref.shape[1]
    for part in range(6):
        total = 0.0
        for clip in range(n_clips):
            row = first + clip * 6 + part
            total += embed_ref[:, clip : clip + 1] * rows_ref[row : row + 1].astype(F32)
        ada_ref[:, part * D : (part + 1) * D] = total


def finish_feed_kernel(n_pieces, n_grads, square_height, count, where_ref, *refs):
    pieces, embed_ref, refs = refs[:n_pieces], refs[n_pieces], refs[n_pieces + 1 :]
    grads, refs = refs[:n_grads], refs[n_grads:]
    up_ref, down_ref, out_ref, ada_ref = refs[:4]
    outs, rms_ref, rows_ref = (up_ref, down_ref, out_ref), refs[-2], refs[-1]
    for index, grad in enumerate(grads):
        refs[4][index * grad.shape[0] : (index + 1) * grad.shape[0]] = grad[...].astype(F32)
    place_pieces(where_ref, pieces, rows_ref)
    at = 0
    for out_ref in outs:
        at = unstack(rows_ref, at, out_ref)
    outer_products(embed_ref, rows_ref, at, ada_ref)
    at += embed_ref.shape[1] * 6
    total = col_sum(rows_ref[at : at + square_height].astype(F32))
    total = sum(total[:, start : start + D // 3] for start in range(0, D, D // 3))
    rms_ref[...] = jnp.broadcast_to(jnp.sqrt(total / count), rms_ref.shape)


def block_of(shape, block):
    return pl.BlockSpec((None,) + shape, lambda *_: (block, 0, 0))


def finish_feed(where, pieces, embed_columns, grads, square_height, count):
    height = len(pieces) * math.prod(pieces[0].shape[:3])
    ada = (D, 6 * D)
    whole_shapes = [(2,) + shape for shape in FEED_SHAPES + [ada]]
    out_specs = [block_of(shape, 0) for shape in FEED_SHAPES] + [block_of(ada, 1)]
    if grads:
        rows, inner = grads[0].shape[0], grads[0].shape[1:]
        whole_shapes.append(((len(grads) + 1) * rows,) + inner)
        out_specs.append(once((len(grads) * rows,) + inner))
    return pl.pallas_call(
        functools.partial(finish_feed_kernel, len(pieces), len(grads), square_height, count),
        grid_spec=pltpu.PrefetchScalarGridSpec(
            num_scalar_prefetch=1,
            grid=(1,),
            in_specs=[once(piece.shape) for piece in pieces]
            + [once(embed_columns.shape)]
            + [once(grad.shape) for grad in grads],
            out_specs=out_specs + [whole((8, D // 3))],
            scratch_shapes=[pltpu.VMEM((height, D), BF)],
        ),
        out_shape=[jax.ShapeDtypeStruct(shape, F32) for shape in whole_shapes]
        + [jax.ShapeDtypeStruct((8, D // 3), F32)],
        compiler_params=params(56),
        cost_estimate=cost(5),
        name="finish_feed",
    )(where, *pieces, embed_columns, *grads)


def finish_kernel(n_pieces, n_held, where_ref, *refs):
    pieces, refs = refs[:n_pieces], refs[n_pieces:]
    embed_ref, qkv_one_ref, *ones = refs[:5]
    last_ref = refs[5]
    qkv_ref, ada_ref, *outs, grad_ref, rows_ref = refs[6 + n_held :]
    step = pl.program_id(0)

    @pl.when(step == 0)
    def _():
        place_pieces(where_ref, pieces, rows_ref)

    height = qkv_ref.shape[1]
    for part in range(3):
        start = pl.multiple_of(part * D + step * height, height)
        qkv_ref[0, :, part * D : (part + 1) * D] = rows_ref[pl.ds(start, height)].astype(F32)
    qkv_ref[1] = qkv_one_ref[...].astype(F32)
    outer_products(embed_ref, rows_ref, 3 * D, ada_ref)
    for one_ref, out_ref in zip(ones, outs):
        out_ref[...] = one_ref[...].astype(F32)
    grad_ref[...] = last_ref[...].astype(F32)


def finish(where, pieces, embed_columns, qkv_one, ones, last, held, chunks):
    steps = 4
    height = len(pieces) * math.prod(pieces[0].shape[:3])
    cut = lambda shape: (shape[0] // steps,) + shape[1:]
    rows = lambda shape: pl.BlockSpec(cut(shape), lambda i, *_: (i, 0))
    block = lambda shape, b: pl.BlockSpec((None,) + cut(shape), lambda i, *_: (b, i, 0))
    grad = lambda first: pl.BlockSpec(cut(last.shape), lambda i, *_: (first + i, 0, 0))
    first = len(pieces) + 7
    return pl.pallas_call(
        functools.partial(finish_kernel, len(pieces), len(held)),
        grid_spec=pltpu.PrefetchScalarGridSpec(
            num_scalar_prefetch=1,
            grid=(steps,),
            in_specs=[once(piece.shape) for piece in pieces]
            + [rows(embed_columns.shape), rows(qkv_one.shape)]
            + [rows(one.shape) for one in ones]
            + [grad(0)]
            + [pl.BlockSpec(memory_space=pl.ANY)] * len(held),
            out_specs=[
                pl.BlockSpec((2, D // steps, 3 * D), lambda i, *_: (0, i, 0)),
                block((D, 6 * D), 0),
            ]
            + [block(one.shape, 1) for one in ones]
            + [grad((chunks - 1) * steps)],
            scratch_shapes=[pltpu.VMEM((height, D), F32)],
        ),
        out_shape=[
            jax.ShapeDtypeStruct((2, D, 3 * D), F32),
            jax.ShapeDtypeStruct((2, D, 6 * D), F32),
        ]
        + [jax.ShapeDtypeStruct((2,) + one.shape, F32) for one in ones]
        + [jax.ShapeDtypeStruct((chunks * last.shape[0],) + last.shape[1:], F32)],
        input_output_aliases={first + k: 1 + k for k in range(len(held))},
        compiler_params=params(56),
        cost_estimate=cost(8),
        name="finish",
    )(where, *pieces, embed_columns, qkv_one, *ones, last, *held)


def round_up(value, unit):
    return -(-value // unit) * unit


def as_one_step(timesteps, function, *operands):
    def skip(*operands):
        shapes = jax.eval_shape(function, *operands)
        return jax.tree.map(lambda leaf: jnp.zeros(leaf.shape, leaf.dtype), shapes)

    return lax.cond(timesteps[0] >= 0, function, skip, *operands)


def on_device(
    tokens,
    timesteps,
    weight_codes,
    cotangent,
    ada_weight,
    qkv_weight,
    out_weight,
    up_weight,
    down_weight,
):
    clips, frames, spots, _ = tokens.shape
    n_pos = lax.axis_size("pos")
    n_clip = lax.axis_size("clip")
    chunks = clips * frames // n_pos
    span = clips // chunks
    n = n_pos * spots
    rows = 512
    places = min(spots, 32)

    n_all = n_pos * n_clip
    n_clips = n_clip * clips
    square_height = n_all
    feed_height = sum(a * b for a, b in FEED_SHAPES) // D + n_clips * 6 + square_height
    feed_height = round_up(feed_height, 16 * n_all)
    tail_height = round_up(3 * D + n_clips * 6, 8 * n_all)
    pos, clip = lax.axis_index("pos"), lax.axis_index("clip")
    mine = pos // frames
    own = clip * clips
    where = [pos, clip, (own + (chunks - 1) * span + mine) * 6, pos % INNER, pos // INNER]
    where = jnp.stack(where).astype(jnp.int32)

    def send(tokens, c):
        return tokens[c * span : (c + 1) * span].reshape(n_pos, spots, D)

    first = swap(send(tokens, 0))
    embedded = embed_steps(timesteps)
    mods = [
        jnp.dot(
            embedded, ada_weight[block].astype(F32), precision=lax.Precision.HIGHEST
        ).reshape(clips, 6, D)
        for block in range(2)
    ]
    embed_rows = lax.all_gather(embedded, "clip", axis=0, tiled=True)
    embed_columns = embed_rows.T
    scaling = jnp.exp2(0.5 * weight_codes.astype(F32) - 1.0)
    codes = jnp.broadcast_to(scaling[:, None, None], (clips, 1, D))
    arrived = [first.reshape(n, D)]
    for c in range(1, chunks):
        held, embed_columns, codes, *mods = lax.optimization_barrier(
            (tokens, embed_columns, codes, *mods)
        )
        arrived.append(swap(send(held, c)).reshape(n, D))

    kept_all = []
    streams = []
    for c in range(chunks):
        x = arrived[c]
        mod = lax.dynamic_index_in_dim(mods[0], c * span + mine, 0, keepdims=False)
        qkv = project(x, mod, qkv_weight, rows)
        att, logs = attend(qkv, 256)
        x_next, *kept, squares = feed(x, att, mod, out_weight, up_weight, down_weight, rows)
        streams.append(swap(x_next.reshape(n_pos, spots, D)).reshape(span, frames, spots, D))
        kept_all.append((x, mod, qkv, att, logs, kept, squares))

    weights = (qkv_weight, out_weight, up_weight, down_weight)
    results, returned, parts_one = (), [], []
    carried = ()
    for c in range(chunks):
        kind = BF
        result, g, part, *carried = temporal(
            streams[c], cotangent, c, codes, mods[1], weights, carried, results, kind, places
        )
        results = (result,)
        parts_one.append(part)
        returned.append(swap(g.reshape(n_pos, spots, D)).reshape(n, D))
    sums_one = carried

    def extra_rows(parts_one, squares_zero):
        part_one = jnp.concatenate(parts_one, axis=0)
        squares_zero = sum(squares_zero)[:3]
        squares_one = jnp.sum(part_one[:, 6:9], axis=0)
        squares = jnp.sum(jnp.concatenate([squares_zero, squares_one], axis=0), axis=1)
        terms = []
        for _ in range(3):
            kept = lax.reduce_precision(squares, exponent_bits=8, mantissa_bits=7)
            terms.append(kept.astype(BF))
            squares = squares - kept
        terms = jnp.pad(jnp.stack(terms), ((0, 0), (0, D // 3 - 6))).reshape(1, D)
        square_rows = lax.dynamic_update_slice(
            jnp.zeros((square_height, D), BF), terms, (pos * n_clip + clip, 0)
        )
        mod_one = lax.dynamic_update_slice(
            jnp.zeros((n_clips, 6, D), BF), part_one[:, :6].astype(BF), (own, 0, 0)
        )
        return jnp.concatenate([mod_one.reshape(n_clips * 6, D), square_rows], axis=0)

    def back_of_feed(c, g, carried, extra):
        x, mod, qkv, att, logs, kept, squares = kept_all[c]
        weights = (out_weight, up_weight, down_weight)
        n_parts = n_clip if c == chunks - 1 else 0
        return feed_back(
            where, extra, g, kept, att, mod, *weights, carried, BF, 256, feed_height, n_parts
        )

    def back_of_project(c, found, gmid, mods, carried):
        x, mod, qkv, att, logs, kept, squares = kept_all[c]
        n_parts = n_clip if c == chunks - 1 else 0
        found = [third[k] for k in range(3) for third in found]
        g, part, *carried = project_back(
            where, mods, x, found, gmid, mod, qkv_weight, carried, rows, tail_height, n_parts
        )
        return g.reshape(n_pos, spots, D), part[:6], carried

    def some_pairs(c, gatt, first, count):
        x, mod, qkv, att, logs, kept, squares = kept_all[c]
        return attend_back(qkv, att, logs, gatt, first, count, rows)

    def last_block_back(later, middle, found, carried, extra):
        middles = [middle]
        for c in range(1, chunks):
            gmid, gatt, part, *carried = back_of_feed(c, later[c - 1], carried, extra)
            middles.append((gmid, gatt, part))
        feed_part = sum_clips(carried)
        carried = ()
        grads = []
        mods = jnp.zeros((n_clips, 6, D), F32)
        for c, (gmid, gatt, part) in enumerate(middles):
            if c == 0:
                feed_part, gatt = lax.optimization_barrier((feed_part, gatt))
                feed_piece = sum_positions(feed_part, n_pos)
                found = [found]
            else:
                found = [some_pairs(c, gatt, 0, 2)]
            if c == chunks - 1:
                break
            found.append(some_pairs(c, gatt, 1, 2))
            grad, part_first, carried = back_of_project(c, found, gmid, mods.reshape(-1, D), carried)
            grads.append(grad)
            mods = lax.dynamic_update_index_in_dim(
                mods, part[:6] + part_first, own + c * span + mine, 0
            )
        mods = lax.dynamic_update_index_in_dim(mods, part[:6], own + (chunks - 1) * span + mine, 0)
        mods = mods.reshape(-1, D)

        gatt, found, feed_piece, *grads = lax.optimization_barrier((gatt, found, feed_piece, *grads))
        feed_pieces = gather_outer(feed_piece, n_pos)

        def last_step(grads, gatt, found, gmid, mods, carried):
            grads = [swap(grad) for grad in grads]
            done = 2 if chunks > 1 else 1
            found = found + [some_pairs(chunks - 1, gatt, done, PAIRS - done)]
            grad, _, parts = back_of_project(chunks - 1, found, gmid, mods, carried)
            return grads, grad, sum_clips(parts)

        grads, grad, part = as_one_step(
            timesteps, last_step, grads, gatt, found, gmid, mods, carried
        )
        part, feed_pieces = lax.optimization_barrier((part, feed_pieces))
        feed_pieces = gather_inner(feed_pieces, n_pos)
        piece = as_one_step(timesteps, lambda part: sum_positions(part, n_pos), part)
        piece, feed_pieces = lax.optimization_barrier((piece, feed_pieces))
        feed_pieces = gather_clips(jnp.stack(feed_pieces), n_clip)
        tail_pieces = as_one_step(timesteps, lambda piece: gather_outer(piece, n_pos), piece)
        grad, feed_pieces, tail_pieces = lax.optimization_barrier((grad, feed_pieces, tail_pieces))
        last = swap(grad)
        tail_pieces = gather_inner(tail_pieces, n_pos)

        def feed_step(feed_pieces, grads):
            count = clips * frames * spots * n_all
            return finish_feed(where, feed_pieces, embed_columns, grads, square_height, count)

        up, down, out, *held, rms = as_one_step(timesteps, feed_step, feed_pieces, grads)
        tail_pieces, held = lax.optimization_barrier((tail_pieces, held))
        tail_pieces = gather_clips(jnp.stack(tail_pieces), n_clip)
        held = [held[0], up, down, out, *held[1:]]
        return last, tail_pieces, held, rms[0, :6].reshape(2, 3)

    all_squares = [kept[-1] for kept in kept_all]
    if chunks > 1:
        unused = mods[0][0]
        gmid, gatt, part, *carried = back_of_feed(0, returned[0], (), unused)
        gatt, parts_one, all_squares = lax.optimization_barrier((gatt, parts_one, all_squares))
        extra = extra_rows(parts_one, all_squares)
    else:
        extra = extra_rows(parts_one, all_squares)
        gmid, gatt, part, *carried = back_of_feed(0, returned[0], (), extra)
    found = some_pairs(0, gatt, 0, 1)
    last, tail_pieces, held, stream_rms = as_one_step(
        timesteps, last_block_back, returned[1:], (gmid, gatt, part), found, carried, extra
    )
    qkv_one, out_one, up_one, down_one = lax.psum(tuple(sums_one), ("pos", "clip"))
    ones = (up_one, down_one, out_one)
    qkv_grad, ada_grad, up_grad, down_grad, out_grad, grad_tokens = finish(
        where, tail_pieces, embed_columns, qkv_one, ones, last, held, chunks
    )
    return (
        results[0],
        grad_tokens.reshape(tokens.shape),
        ada_grad,
        qkv_grad,
        out_grad,
        up_grad,
        down_grad,
        stream_rms,
    )


def solution(mesh):
    placed = (
        P("clip", None, "pos", None),
        P("clip"),
        P("clip"),
        P("clip", None, "pos", None),
        P(),
        P(),
        P(),
        P(),
        P(),
    )
    return jax.shard_map(
        on_device,
        mesh=mesh,
        in_specs=placed,
        out_specs=(
            P("clip", None, "pos", None),
            P("clip", None, "pos", None),
            P(),
            P(),
            P(),
            P(),
            P(),
            P(),
        ),
        check_vma=False,
    )
```

```python
import functools
import math

import jax
import jax.numpy as jnp
from jax import lax
from jax.experimental import pallas as pl
from jax.experimental.pallas import tpu as pltpu
from jax.sharding import PartitionSpec as P

D = 384
HEAD = 64
PAIRS = 3
FF = 1536
EPS = 1e-06
LOG_SCALE = HEAD**-0.5 * math.log2(math.e)
GROUP = 16
FEED_SHAPES = [(D, FF), (FF, D), (D, D)]

NN = (((1,), (0,)), ((), ()))
NT = (((1,), (1,)), ((), ()))
TN = (((0,), (0,)), ((), ()))
F32 = jnp.float32
BF = jnp.bfloat16


def mm(left, right, dims=NN):
    return lax.dot_general(left, right, dims, preferred_element_type=F32)


def params(mebibytes):
    return pltpu.CompilerParams(vmem_limit_bytes=mebibytes * 2**20)


def cost(micros):
    return pl.CostEstimate(
        flops=int(micros * 1e9), transcendentals=0, bytes_accessed=int(micros * 3e6)
    )


def norm_rows(values):
    center = values - jnp.mean(values, axis=-1, keepdims=True)
    rstd = lax.rsqrt(jnp.mean(center * center, axis=-1, keepdims=True) + EPS)
    return center * rstd, rstd


def norm_back(grad_normed, normed, rstd):
    mean_grad = jnp.mean(grad_normed, axis=-1, keepdims=True)
    mean_cross = jnp.mean(grad_normed * normed, axis=-1, keepdims=True)
    return rstd * (grad_normed - mean_grad - normed * mean_cross)


def col_sum(values):
    return jnp.sum(values, axis=0, keepdims=True)


def gelu_pair(inner):
    square = inner * inner
    slope = math.sqrt(2.0 / math.pi)
    tanh = jnp.tanh(inner * (slope + (slope * 0.044715) * square))
    half = 0.5 + 0.5 * tanh
    value = inner * half
    grad = half + (value * (1.0 - tanh)) * (slope + (3.0 * 0.044715 * slope) * square)
    return value, grad


def low_lanes():
    return lax.broadcasted_iota(jnp.int32, (1, 2 * HEAD), 1) < HEAD


def both_heads(values, low, fill=0.0):
    other = jnp.full_like(values, fill)
    return (jnp.where(low, values, other), jnp.where(low, other, values))


def whole(shape):
    return pl.BlockSpec(shape, lambda *_: (0,) * len(shape))


def once(shape):
    return pl.BlockSpec(shape, lambda *_: (0,) * len(shape), pipeline_mode=pl.Buffered(1))


def weight_spec(rows, cols, block):
    return pl.BlockSpec((None, rows, cols), lambda *_: (block, 0, 0), pipeline_mode=pl.Buffered(1))


def project_kernel(x_ref, mod_ref, w_ref, out_ref):
    normed, _ = norm_rows(x_ref[...].astype(F32))
    hidden = (normed * (1.0 + mod_ref[1:2]) + mod_ref[0:1]).astype(BF)
    out_ref[...] = mm(hidden, w_ref[...]).astype(BF)


def project(x, mod, qkv_weight, rows):
    n = x.shape[0]
    return pl.pallas_call(
        project_kernel,
        grid=(n // rows,),
        in_specs=[
            pl.BlockSpec((rows, D), lambda i: (i, 0)),
            whole((6, D)),
            weight_spec(D, 3 * D, 0),
        ],
        out_specs=pl.BlockSpec((rows, 3 * D), lambda i: (i, 0)),
        out_shape=jax.ShapeDtypeStruct((n, 3 * D), BF),
        compiler_params=params(16),
        cost_estimate=cost(5),
        name="project",
    )(x, mod, qkv_weight)


def attend_kernel(rows, q_ref, k_ref, v_ref, out_ref, log_ref):
    low = low_lanes()
    keys = k_ref[...]
    values = both_heads(v_ref[...], low, 1.0)
    tasks = [(start, head) for start in range(0, q_ref.shape[0], rows) for head in range(2)]

    def score(task):
        start, head = task
        q = q_ref[start : start + rows, :]
        return mm(both_heads(q, low)[head], keys, NT)

    ahead = score(tasks[0])
    mixed, tops = [], []
    for index, (start, head) in enumerate(tasks):
        scores = ahead
        if index + 1 < len(tasks):
            ahead = score(tasks[index + 1])
        top = jnp.max(scores, axis=1, keepdims=True)
        raised = jnp.exp2((scores - top) * LOG_SCALE).astype(BF)
        mixed.append(mm(raised, values[head]))
        tops.append(top * LOG_SCALE)
        if head == 1:
            part = slice(start, start + rows)
            total = pltpu.roll(jnp.where(low, mixed[1], mixed[0]), HEAD, 1)
            out_ref[part, :] = (jnp.where(low, mixed[0], mixed[1]) / total).astype(BF)
            log_ref[part, :] = jnp.where(low, tops[0], tops[1]) + jnp.log2(total)
            mixed, tops = [], []


def attend(qkv, rows):
    n = qkv.shape[0]
    pair = lambda start: pl.BlockSpec((n, 2 * HEAD), lambda p: (0, start + p))
    return pl.pallas_call(
        functools.partial(attend_kernel, rows),
        grid=(PAIRS,),
        in_specs=[pair(0), pair(PAIRS), pair(2 * PAIRS)],
        out_specs=[pair(0), pair(0)],
        out_shape=[jax.ShapeDtypeStruct((n, D), BF), jax.ShapeDtypeStruct((n, D), F32)],
        compiler_params=params(24),
        cost_estimate=cost(14),
        name="attend",
    )(qkv, qkv, qkv)


def feed_kernel(
    x_ref,
    att_ref,
    mod_ref,
    wo_ref,
    wu_ref,
    wd_ref,
    next_ref,
    middle_ref,
    branch_ref,
    mlp_ref,
    act_ref,
    slope_ref,
    squares_ref,
):
    @pl.when(pl.program_id(0) == 0)
    def _():
        squares_ref[...] = jnp.zeros_like(squares_ref)

    x = x_ref[...].astype(F32)
    branch = mm(att_ref[...], wo_ref[...])
    gated = mod_ref[2:3] * branch
    middle = x + gated
    normed, _ = norm_rows(middle)
    hidden = (normed * (1.0 + mod_ref[4:5]) + mod_ref[3:4]).astype(BF)
    value, slope = gelu_pair(mm(hidden, wu_ref[...]))
    act = value.astype(BF)
    mlp = mm(act, wd_ref[...])
    fed = mod_ref[5:6] * mlp
    next_ref[...] = (middle + fed).astype(BF)
    middle_ref[...] = middle.astype(BF)
    branch_ref[...] = branch.astype(BF)
    mlp_ref[...] = mlp.astype(BF)
    act_ref[...] = act
    slope_ref[...] = slope.astype(BF)
    squares_ref[0:1] += col_sum(x * x)
    squares_ref[1:2] += col_sum(gated * gated)
    squares_ref[2:3] += col_sum(fed * fed)


def feed(x, att, mod, out_weight, up_weight, down_weight, rows):
    n = x.shape[0]
    row = lambda width: pl.BlockSpec((rows, width), lambda i: (i, 0))
    out = lambda width, kind: jax.ShapeDtypeStruct((n, width), kind)
    return pl.pallas_call(
        feed_kernel,
        grid=(n // rows,),
        in_specs=[
            row(D),
            row(D),
            whole((6, D)),
            weight_spec(D, D, 0),
            weight_spec(D, FF, 0),
            weight_spec(FF, D, 0),
        ],
        out_specs=[row(D), row(D), row(D), row(D), row(FF), row(FF), whole((8, D))],
        out_shape=[
            out(D, BF),
            out(D, BF),
            out(D, BF),
            out(D, BF),
            out(FF, BF),
            out(FF, BF),
            jax.ShapeDtypeStruct((8, D), F32),
        ],
        compiler_params=params(56),
        cost_estimate=cost(11),
        name="feed",
    )(x, att, mod, out_weight, up_weight, down_weight)


def start_sums(sums, carried):
    for index, total in enumerate(sums):
        total[...] = carried[index][...].astype(F32) if carried else jnp.zeros_like(total)


def row_blocks(total):
    height, width = total.shape
    return [(start, height) for start in range(0, width, D)]


def load_rows(rows_ref, sums):
    at = 0
    for total in sums:
        for start, height in row_blocks(total):
            total[:, start : start + D] = rows_ref[at : at + height].astype(F32)
            at += height


def store_rows(sums, rows_ref, extra=None):
    at = 0
    for total in sums:
        for start, height in row_blocks(total):
            rows_ref[at : at + height] = total[:, start : start + D].astype(rows_ref.dtype)
            at += height
    if extra is not None:
        rows_ref[at : at + extra.shape[0]] = extra.astype(rows_ref.dtype)
        at += extra.shape[0]
    if at < rows_ref.shape[0]:
        rows_ref[at:] = jnp.zeros((rows_ref.shape[0] - at, D), rows_ref.dtype)


def store_parts(where_ref, held_ref, rows_refs):
    part = rows_refs[0].shape[0]
    for s, rows_ref in enumerate(rows_refs):
        start = pl.multiple_of((where_ref[1] ^ s) * part, part)
        rows_ref[...] = held_ref[pl.ds(start, part)]


def feed_back_kernel(n_carried, n_parts, where_ref, extra_ref, *refs):
    (
        g_ref,
        middle_ref,
        branch_ref,
        mlp_ref,
        act_ref,
        slope_ref,
        att_ref,
        mod_ref,
        wo_ref,
        wu_ref,
        wd_ref,
    ) = refs[:11]
    carried = refs[11 : 11 + n_carried]
    gmid_ref, gatt_ref, part_ref = refs[11 + n_carried : 14 + n_carried]
    n_out = max(n_parts, 1)
    rows_refs = refs[14 + n_carried : 14 + n_carried + n_out]
    *sums, held_ref = refs[14 + n_carried + n_out :]

    @pl.when(pl.program_id(0) == 0)
    def _():
        part_ref[...] = jnp.zeros_like(part_ref)
        if carried:
            load_rows(carried[0], sums)
        else:
            start_sums(sums, ())

    up_sum, down_sum, out_sum = sums
    g = g_ref[...].astype(F32)
    part_ref[5:6] += col_sum(mlp_ref[...].astype(F32) * g)
    gm = (mod_ref[5:6] * g).astype(BF)
    down_sum[...] += mm(act_ref[...], gm, TN)
    gi = (slope_ref[...].astype(F32) * mm(gm, wd_ref[...], NT)).astype(BF)
    normed, rstd = norm_rows(middle_ref[...].astype(F32))
    scale = 1.0 + mod_ref[4:5]
    hidden = (normed * scale + mod_ref[3:4]).astype(BF)
    up_sum[...] += mm(hidden, gi, TN)
    gh = mm(gi, wu_ref[...], NT)
    part_ref[3:4] += col_sum(gh)
    part_ref[4:5] += col_sum(gh * normed)
    gmid = g + norm_back(gh * scale, normed, rstd)
    gmid_ref[...] = gmid
    part_ref[2:3] += col_sum(branch_ref[...].astype(F32) * gmid)
    gb = (mod_ref[2:3] * gmid).astype(BF)
    out_sum[...] += mm(att_ref[...], gb, TN)
    gatt_ref[...] = mm(gb, wo_ref[...], NT).astype(BF)

    @pl.when(pl.program_id(0) == pl.num_programs(0) - 1)
    def _():
        if n_parts == 0:
            store_rows(sums, rows_refs[0])
        else:
            store_rows(sums, held_ref, extra_ref[...])
            store_parts(where_ref, held_ref, rows_refs)


def feed_back(where, extra, g, kept, att, mod, out_weight, up_weight, down_weight, carried, kind, rows, height, n_parts):
    n = g.shape[0]
    row = lambda width: pl.BlockSpec((rows, width), lambda i, *_: (i, 0))
    shapes = FEED_SHAPES
    n_out = max(n_parts, 1)
    return pl.pallas_call(
        functools.partial(feed_back_kernel, len(carried), n_parts),
        grid=(n // rows,),
        in_specs=[
            pl.BlockSpec(memory_space=pltpu.SMEM),
            whole(extra.shape),
            row(D),
            row(D),
            row(D),
            row(D),
            row(FF),
            row(FF),
            row(D),
            whole((6, D)),
            weight_spec(D, D, 0),
            weight_spec(D, FF, 0),
            weight_spec(FF, D, 0),
        ]
        + [once((height, D))] * len(carried),
        out_specs=[row(D), row(D), whole((8, D)), once((height // n_out, D))]
        + [once((height // n_out, D))] * (n_out - 1),
        out_shape=[
            jax.ShapeDtypeStruct((n, D), F32),
            jax.ShapeDtypeStruct((n, D), BF),
            jax.ShapeDtypeStruct((8, D), F32),
        ]
        + [jax.ShapeDtypeStruct((height // n_out, D), kind)] * n_out,
        scratch_shapes=[pltpu.VMEM(shape, F32) for shape in shapes] + [pltpu.VMEM((height, D), BF)],
        compiler_params=params(36 if n_parts else 56),
        cost_estimate=cost(16),
        name="feed_back",
    )(where, extra, g, *kept, att, mod, out_weight, up_weight, down_weight, *carried)


def attend_back_kernel(
    rows, q_ref, k_ref, v_ref, o_ref, log_ref, g_ref, dq_ref, dk_ref, dv_ref
):
    low = low_lanes()
    keys, values = k_ref[...], v_ref[...]
    tasks = [(start, head) for start in range(0, q_ref.shape[0], rows) for head in range(2)]

    def begin(task):
        start, head = task
        part = slice(start, start + rows)
        query = both_heads(q_ref[part, :], low)[head]
        grad = both_heads(g_ref[part, :], low)[head]
        return query, grad, mm(query, keys, NT), mm(grad, values, NT)

    ahead = begin(tasks[0])
    found = []
    for index, (start, head) in enumerate(tasks):
        query, grad, scores, grad_probs = ahead
        if index + 1 < len(tasks):
            ahead = begin(tasks[index + 1])
        part = slice(start, start + rows)
        delta = jnp.sum(grad.astype(F32) * o_ref[part, :].astype(F32), axis=1, keepdims=True)
        log = log_ref[part, HEAD * head : HEAD * head + 1]
        probs = jnp.exp2(scores * LOG_SCALE - log)
        grad_scores = (probs * (grad_probs - delta)).astype(BF)
        found.append(mm(grad_scores, keys))
        values_part = mm(grad.T, probs.astype(BF))
        keys_part = mm(query.T, grad_scores)
        dv = values_part if index == 0 else dv + values_part
        dk = keys_part if index == 0 else dk + keys_part
        if head == 1:
            dq_ref[part, :] = (jnp.where(low, found[0], found[1]) * HEAD**-0.5).astype(BF)
            found = []
    dk_ref[...] = (dk * HEAD**-0.5).T.astype(BF)
    dv_ref[...] = dv.T.astype(BF)


def attend_back(qkv, att, logs, grad, first, count, rows):
    n = qkv.shape[0]
    pair = lambda start: pl.BlockSpec((n, 2 * HEAD), lambda p: (0, start + p))
    return pl.pallas_call(
        functools.partial(attend_back_kernel, rows),
        grid=(count,),
        in_specs=[pair(third * PAIRS + first) for third in (0, 1, 2, 0, 0, 0)],
        out_specs=[pair(0)] * 3,
        out_shape=[jax.ShapeDtypeStruct((n, count * 2 * HEAD), BF)] * 3,
        compiler_params=params(24),
        cost_estimate=cost(5 * count),
        name="attend_back",
    )(qkv, qkv, qkv, att, logs, grad)


def project_back_kernel(n_grads, n_carried, n_parts, where_ref, mods_ref, *refs):
    grad_refs, refs = refs[:n_grads], refs[n_grads:]
    x_ref, gmid_ref, mod_ref, w_ref = refs[:4]
    carried = refs[4 : 4 + n_carried]
    out_ref, part_ref = refs[4 + n_carried : 6 + n_carried]
    *rows_refs, total, held_ref, mods_sum = refs[6 + n_carried :]

    @pl.when(pl.program_id(0) == 0)
    def _():
        part_ref[...] = jnp.zeros_like(part_ref)
        if carried:
            load_rows(carried[0], [total])
        else:
            start_sums([total], ())

    normed, rstd = norm_rows(x_ref[...].astype(F32))
    scale = 1.0 + mod_ref[1:2]
    hidden = (normed * scale + mod_ref[0:1]).astype(BF)
    gp = jnp.concatenate([ref[...] for ref in grad_refs], axis=1)
    total[...] += mm(hidden, gp, TN)
    gh = mm(gp, w_ref[...], NT)
    part_ref[0:1] += col_sum(gh)
    part_ref[1:2] += col_sum(gh * normed)
    out_ref[...] = (gmid_ref[...] + norm_back(gh * scale, normed, rstd)).astype(BF)

    @pl.when(pl.program_id(0) == pl.num_programs(0) - 1)
    def _():
        if n_parts == 0:
            store_rows([total], rows_refs[0])
        else:
            mods_sum[...] = mods_ref[...]
            for k in range(2):
                mods_sum[pl.ds(where_ref[2] + k, 1)] += part_ref[k : k + 1]
            store_rows([total], held_ref, mods_sum[...])
            store_parts(where_ref, held_ref, rows_refs)


def project_back(where, mods, x, grads, gmid, mod, qkv_weight, carried, rows, height, n_parts):
    n = x.shape[0]
    row = lambda width: pl.BlockSpec((rows, width), lambda i: (i, 0))
    n_out = max(n_parts, 1)
    if n_parts == 0:
        height = 3 * D
    return pl.pallas_call(
        functools.partial(project_back_kernel, len(grads), len(carried), n_parts),
        grid=(n // rows,),
        in_specs=[pl.BlockSpec(memory_space=pltpu.SMEM), whole(mods.shape)]
        + [row(grad.shape[1]) for grad in grads]
        + [row(D), row(D), whole((6, D)), weight_spec(D, 3 * D, 0)]
        + [once((3 * D, D))] * len(carried),
        out_specs=[row(D), whole((8, D))] + [once((height // n_out, D))] * n_out,
        out_shape=[
            jax.ShapeDtypeStruct((n, D), BF),
            jax.ShapeDtypeStruct((8, D), F32),
        ]
        + [jax.ShapeDtypeStruct((height // n_out, D), BF)] * n_out,
        scratch_shapes=[
            pltpu.VMEM((D, 3 * D), F32),
            pltpu.VMEM((height, D), BF),
            pltpu.VMEM(mods.shape, F32),
        ],
        compiler_params=params(24),
        cost_estimate=cost(4),
        name="project_back",
    )(where, mods, *grads, x, gmid, mod, qkv_weight, *carried)


def temporal_kernel(n_carried, n_before, *refs):
    x_ref, cot_ref, code_ref, mod_ref, wq_ref, wo_ref, wu_ref, wd_ref = refs[:8]
    carried = refs[8 : 8 + n_carried]
    refs = refs[8 + n_carried + n_before :]
    act_out_ref, g_ref, part_ref = refs[:3]
    out_refs = refs[3:7]
    sums = refs[7:11]
    qkv_ref, att_ref, probs_ref, inv_ref, gatt_ref, gqkv_ref = refs[11:]
    frames, places = x_ref.shape[0], x_ref.shape[1]
    tokens = frames * places
    wide = frames * GROUP
    first = jnp.logical_and(pl.program_id(0) == 0, pl.program_id(1) == 0)
    last = jnp.logical_and(
        pl.program_id(0) == pl.num_programs(0) - 1, pl.program_id(1) == pl.num_programs(1) - 1
    )

    @pl.when(first)
    def _():
        start_sums(sums, carried)

    @pl.when(pl.program_id(1) == 0)
    def _():
        part_ref[...] = jnp.zeros_like(part_ref)

    qkv_sum, out_sum, up_sum, down_sum = sums
    low = low_lanes()
    mod = mod_ref[...]
    x = x_ref[...].reshape(tokens, D).astype(F32)
    normed, rstd = norm_rows(x)
    scale = 1.0 + mod[1:2]
    hidden = (normed * scale + mod[0:1]).astype(BF)
    qkv_ref[...] = mm(hidden, wq_ref[...]).astype(BF).reshape(qkv_ref.shape)

    row_place = lax.broadcasted_iota(jnp.int32, (wide, 1), 0) & (GROUP - 1)
    column_place = lax.broadcasted_iota(jnp.int32, (1, wide), 1) & (GROUP - 1)
    same = row_place == column_place
    groups = places // GROUP

    def cut(ref, group, column):
        rows = slice(group * GROUP, (group + 1) * GROUP)
        return ref[:, rows, column * 2 * HEAD : (column + 1) * 2 * HEAD].reshape(wide, 2 * HEAD)

    def put(ref, group, column, value):
        rows = slice(group * GROUP, (group + 1) * GROUP)
        ref[:, rows, column * 2 * HEAD : (column + 1) * 2 * HEAD] = value.reshape(
            frames, GROUP, 2 * HEAD
        )

    tasks = [(g, pair, head) for g in range(groups) for pair in range(PAIRS) for head in range(2)]

    def score(task):
        group, pair, head = task
        query = both_heads(cut(qkv_ref, group, pair), low)[head]
        return mm(query, cut(qkv_ref, group, PAIRS + pair), NT)

    ahead = score(tasks[0])
    mixed = []
    for index, (group, pair, head) in enumerate(tasks):
        scores = jnp.where(same, ahead, -1e38)
        if index + 1 < len(tasks):
            ahead = score(tasks[index + 1])
        top = jnp.max(scores, axis=1, keepdims=True)
        raised = jnp.exp2((scores - top) * LOG_SCALE).astype(BF)
        probs_ref[index] = raised
        mixed.append(mm(raised, both_heads(cut(qkv_ref, group, 2 * PAIRS + pair), low, 1.0)[head]))
        if head == 1:
            inverse = 1.0 / pltpu.roll(jnp.where(low, mixed[1], mixed[0]), HEAD, 1)
            put(inv_ref, group, pair, inverse)
            put(att_ref, group, pair, (jnp.where(low, mixed[0], mixed[1]) * inverse).astype(BF))
            mixed = []

    att = att_ref[...].reshape(tokens, D)
    branch = mm(att, wo_ref[...])
    gated = mod[2:3] * branch
    middle = x + gated
    normed_two, rstd_two = norm_rows(middle)
    scale_two = 1.0 + mod[4:5]
    hidden_two = (normed_two * scale_two + mod[3:4]).astype(BF)
    value, slope = gelu_pair(mm(hidden_two, wu_ref[...]))
    act = value.astype(BF)
    mlp = mm(act, wd_ref[...])
    fed = mod[5:6] * mlp
    act_out_ref[...] = (middle + fed).astype(BF).reshape(act_out_ref.shape)
    part_ref[6:7] += col_sum(x * x)
    part_ref[7:8] += col_sum(gated * gated)
    part_ref[8:9] += col_sum(fed * fed)

    g = cot_ref[...].reshape(tokens, D).astype(F32) * code_ref[0:1]
    part_ref[5:6] += col_sum(mlp * g)
    gm = (mod[5:6] * g).astype(BF)
    down_sum[...] += mm(act, gm, TN)
    gi = (slope * mm(gm, wd_ref[...], NT)).astype(BF)
    up_sum[...] += mm(hidden_two, gi, TN)
    gh = mm(gi, wu_ref[...], NT)
    part_ref[3:4] += col_sum(gh)
    part_ref[4:5] += col_sum(gh * normed_two)
    gmid = g + norm_back(gh * scale_two, normed_two, rstd_two)
    part_ref[2:3] += col_sum(branch * gmid)
    gb = (mod[2:3] * gmid).astype(BF)
    out_sum[...] += mm(att, gb, TN)
    gatt_ref[...] = mm(gb, wo_ref[...], NT).astype(BF).reshape(gatt_ref.shape)

    def begin(task):
        group, pair, head = task
        grad = both_heads(cut(gatt_ref, group, pair), low)[head]
        return grad, mm(grad, cut(qkv_ref, group, 2 * PAIRS + pair), NT)

    ahead = begin(tasks[0])
    found = []
    for index, (group, pair, head) in enumerate(tasks):
        grad, grad_probs = ahead
        if index + 1 < len(tasks):
            ahead = begin(tasks[index + 1])
        query = both_heads(cut(qkv_ref, group, pair), low)[head]
        cross = grad.astype(F32) * cut(att_ref, group, pair).astype(F32)
        delta = jnp.sum(cross, axis=1, keepdims=True)
        inverse = cut(inv_ref, group, pair)[:, HEAD * head : HEAD * head + 1]
        probs = probs_ref[index].astype(F32) * inverse
        grad_scores = (probs * (grad_probs - delta)).astype(BF)
        found.append(mm(grad_scores, cut(qkv_ref, group, PAIRS + pair)))
        values_part = mm(grad.T, probs.astype(BF))
        keys_part = mm(query.T, grad_scores)
        if head == 0:
            dv, dk = values_part, keys_part
        else:
            dq = jnp.where(low, found[0], found[1])
            put(gqkv_ref, group, pair, (dq * HEAD**-0.5).astype(BF))
            put(gqkv_ref, group, PAIRS + pair, ((dk + keys_part) * HEAD**-0.5).T.astype(BF))
            put(gqkv_ref, group, 2 * PAIRS + pair, (dv + values_part).T.astype(BF))
            found = []

    gp = gqkv_ref[...].reshape(tokens, 3 * D)
    qkv_sum[...] += mm(hidden, gp, TN)
    gh_one = mm(gp, wq_ref[...], NT)
    part_ref[0:1] += col_sum(gh_one)
    part_ref[1:2] += col_sum(gh_one * normed)
    g_next = gmid + norm_back(gh_one * scale, normed, rstd)
    g_ref[...] = g_next.astype(BF).reshape(g_ref.shape)

    @pl.when(last)
    def _():
        for total, out_ref in zip(sums, out_refs):
            out_ref[...] = total[...].astype(out_ref.dtype)


def temporal(x, cot, chunk, codes, mods, weights, carried, before, kind, places):
    clips, frames, spots, _ = x.shape
    block = lambda offset: pl.BlockSpec(
        (None, frames, places, D), lambda c, p: (offset * clips + c, 0, p, 0)
    )
    per_clip = lambda rows: pl.BlockSpec((None, rows, D), lambda c, p: (chunk * clips + c, 0, 0))
    shapes = [(D, 3 * D), (D, D), (D, FF), (FF, D)]
    kept = lambda width, kind: pltpu.VMEM((frames, places, width), kind)
    groups = places // GROUP
    return pl.pallas_call(
        functools.partial(temporal_kernel, len(carried), len(before)),
        grid=(clips, spots // places),
        in_specs=[block(0), block(chunk), per_clip(1), per_clip(6)]
        + [weight_spec(*shape, 1) for shape in shapes]
        + [once(shape) for shape in shapes[: len(carried)]]
        + [pl.BlockSpec(memory_space=pl.ANY)] * len(before),
        out_specs=[block(chunk), block(0), pl.BlockSpec((None, 16, D), lambda c, p: (c, 0, 0))]
        + [once(shape) for shape in shapes],
        out_shape=[
            jax.ShapeDtypeStruct(cot.shape, BF),
            jax.ShapeDtypeStruct(x.shape, BF),
            jax.ShapeDtypeStruct((clips, 16, D), F32),
        ]
        + [jax.ShapeDtypeStruct(shape, kind) for shape in shapes],
        scratch_shapes=[pltpu.VMEM(shape, F32) for shape in shapes]
        + [
            kept(3 * D, BF),
            kept(D, BF),
            pltpu.VMEM((groups * 2 * PAIRS, frames * GROUP, frames * GROUP), BF),
            kept(D, F32),
            kept(D, BF),
            kept(3 * D, BF),
        ],
        compiler_params=params(58),
        cost_estimate=cost(36),
        name="temporal",
        input_output_aliases={8 + len(carried): 0} if before else {},
    )(x, cot, codes, mods, *weights, *carried, *before)


def embed_steps(timesteps):
    half_width = D // 2
    frequencies = jnp.exp(
        -math.log(10000.0) * jnp.arange(half_width, dtype=F32) / half_width
    )
    angles = timesteps.astype(F32)[:, None] * frequencies[None, :]
    return jax.nn.silu(jnp.concatenate([jnp.cos(angles), jnp.sin(angles)], axis=-1))


def swap(values):
    return lax.all_to_all(values, "pos", split_axis=0, concat_axis=0, tiled=True)


def sum_clips(parts):
    total = parts[0].astype(F32)
    for s, give in enumerate(parts[1:], 1):
        total += exchange(give, "clip", len(parts), s).astype(F32)
    return total.astype(BF)


def sum_positions(part, n_pos):
    pieces = swap(part.reshape(n_pos, part.shape[0] // n_pos, D))
    return jnp.sum(pieces.astype(F32), axis=0).astype(BF)


INNER = 4


def exchange(values, axis, size, distance):
    return lax.ppermute(values, axis, [(i, i ^ distance) for i in range(size)])


def gather_outer(piece, n_pos):
    rest = [exchange(piece, "pos", n_pos, k * INNER) for k in range(1, n_pos // INNER)]
    return jnp.stack([piece] + rest)


def gather_inner(pieces, n_pos):
    rest = [exchange(pieces, "pos", n_pos, k) for k in range(1, INNER)]
    return [pieces] + rest


def gather_clips(pieces, n_clip):
    return [pieces] + [exchange(pieces, "clip", n_clip, k) for k in range(1, n_clip)]


def place_pieces(where_ref, piece_refs, rows_ref):
    inner, outer, height, _ = piece_refs[0].shape
    for s, piece_ref in enumerate(piece_refs):
        clip = where_ref[1] ^ s
        for p in range(inner * outer):
            owner = where_ref[0] ^ p
            row = (clip * (inner * outer) + owner) * height
            piece = piece_ref[p % inner, p // inner].astype(rows_ref.dtype)
            rows_ref[pl.ds(pl.multiple_of(row, height), height)] = piece


def unstack(rows_ref, at, out_ref):
    height, width = out_ref.shape
    for start in range(0, width, D):
        out_ref[:, start : start + D] = rows_ref[at : at + height].astype(F32)
        at += height
    return at


def first_block(shape):
    return pl.BlockSpec((None,) + shape, lambda *_: (0, 0, 0))


def outer_products(embed_ref, rows_ref, first, ada_ref):
    n_clips = embed_ref.shape[1]
    for part in range(6):
        total = 0.0
        for clip in range(n_clips):
            row = first + clip * 6 + part
            total += embed_ref[:, clip : clip + 1] * rows_ref[row : row + 1].astype(F32)
        ada_ref[:, part * D : (part + 1) * D] = total


def finish_feed_kernel(n_pieces, n_grads, square_height, count, where_ref, *refs):
    pieces, embed_ref, refs = refs[:n_pieces], refs[n_pieces], refs[n_pieces + 1 :]
    grads, refs = refs[:n_grads], refs[n_grads:]
    up_ref, down_ref, out_ref, ada_ref = refs[:4]
    outs, rms_ref, rows_ref = (up_ref, down_ref, out_ref), refs[-2], refs[-1]
    for index, grad in enumerate(grads):
        refs[4][index * grad.shape[0] : (index + 1) * grad.shape[0]] = grad[...].astype(F32)
    place_pieces(where_ref, pieces, rows_ref)
    at = 0
    for out_ref in outs:
        at = unstack(rows_ref, at, out_ref)
    outer_products(embed_ref, rows_ref, at, ada_ref)
    at += embed_ref.shape[1] * 6
    total = col_sum(rows_ref[at : at + square_height].astype(F32))
    total = sum(total[:, start : start + D // 3] for start in range(0, D, D // 3))
    rms_ref[...] = jnp.broadcast_to(jnp.sqrt(total / count), rms_ref.shape)


def block_of(shape, block):
    return pl.BlockSpec((None,) + shape, lambda *_: (block, 0, 0))


def finish_feed(where, pieces, embed_columns, grads, square_height, count):
    height = len(pieces) * math.prod(pieces[0].shape[:3])
    ada = (D, 6 * D)
    whole_shapes = [(2,) + shape for shape in FEED_SHAPES + [ada]]
    out_specs = [block_of(shape, 0) for shape in FEED_SHAPES] + [block_of(ada, 1)]
    if grads:
        rows, inner = grads[0].shape[0], grads[0].shape[1:]
        whole_shapes.append(((len(grads) + 1) * rows,) + inner)
        out_specs.append(once((len(grads) * rows,) + inner))
    return pl.pallas_call(
        functools.partial(finish_feed_kernel, len(pieces), len(grads), square_height, count),
        grid_spec=pltpu.PrefetchScalarGridSpec(
            num_scalar_prefetch=1,
            grid=(1,),
            in_specs=[once(piece.shape) for piece in pieces]
            + [once(embed_columns.shape)]
            + [once(grad.shape) for grad in grads],
            out_specs=out_specs + [whole((8, D // 3))],
            scratch_shapes=[pltpu.VMEM((height, D), BF)],
        ),
        out_shape=[jax.ShapeDtypeStruct(shape, F32) for shape in whole_shapes]
        + [jax.ShapeDtypeStruct((8, D // 3), F32)],
        compiler_params=params(56),
        cost_estimate=cost(5),
        name="finish_feed",
    )(where, *pieces, embed_columns, *grads)


def finish_kernel(n_pieces, n_held, where_ref, *refs):
    pieces, refs = refs[:n_pieces], refs[n_pieces:]
    embed_ref, qkv_one_ref, *ones = refs[:5]
    last_ref = refs[5]
    qkv_ref, ada_ref, *outs, grad_ref, rows_ref = refs[6 + n_held :]
    step = pl.program_id(0)

    @pl.when(step == 0)
    def _():
        place_pieces(where_ref, pieces, rows_ref)

    height = qkv_ref.shape[1]
    for part in range(3):
        start = pl.multiple_of(part * D + step * height, height)
        qkv_ref[0, :, part * D : (part + 1) * D] = rows_ref[pl.ds(start, height)].astype(F32)
    qkv_ref[1] = qkv_one_ref[...].astype(F32)
    outer_products(embed_ref, rows_ref, 3 * D, ada_ref)
    for one_ref, out_ref in zip(ones, outs):
        out_ref[...] = one_ref[...].astype(F32)
    grad_ref[...] = last_ref[...].astype(F32)


def finish(where, pieces, embed_columns, qkv_one, ones, last, held, chunks):
    steps = 4
    height = len(pieces) * math.prod(pieces[0].shape[:3])
    cut = lambda shape: (shape[0] // steps,) + shape[1:]
    rows = lambda shape: pl.BlockSpec(cut(shape), lambda i, *_: (i, 0))
    block = lambda shape, b: pl.BlockSpec((None,) + cut(shape), lambda i, *_: (b, i, 0))
    grad = lambda first: pl.BlockSpec(cut(last.shape), lambda i, *_: (first + i, 0, 0))
    first = len(pieces) + 7
    return pl.pallas_call(
        functools.partial(finish_kernel, len(pieces), len(held)),
        grid_spec=pltpu.PrefetchScalarGridSpec(
            num_scalar_prefetch=1,
            grid=(steps,),
            in_specs=[once(piece.shape) for piece in pieces]
            + [rows(embed_columns.shape), rows(qkv_one.shape)]
            + [rows(one.shape) for one in ones]
            + [grad(0)]
            + [pl.BlockSpec(memory_space=pl.ANY)] * len(held),
            out_specs=[
                pl.BlockSpec((2, D // steps, 3 * D), lambda i, *_: (0, i, 0)),
                block((D, 6 * D), 0),
            ]
            + [block(one.shape, 1) for one in ones]
            + [grad((chunks - 1) * steps)],
            scratch_shapes=[pltpu.VMEM((height, D), F32)],
        ),
        out_shape=[
            jax.ShapeDtypeStruct((2, D, 3 * D), F32),
            jax.ShapeDtypeStruct((2, D, 6 * D), F32),
        ]
        + [jax.ShapeDtypeStruct((2,) + one.shape, F32) for one in ones]
        + [jax.ShapeDtypeStruct((chunks * last.shape[0],) + last.shape[1:], F32)],
        input_output_aliases={first + k: 1 + k for k in range(len(held))},
        compiler_params=params(56),
        cost_estimate=cost(8),
        name="finish",
    )(where, *pieces, embed_columns, qkv_one, *ones, last, *held)


def round_up(value, unit):
    return -(-value // unit) * unit


def as_one_step(timesteps, function, *operands):
    def skip(*operands):
        shapes = jax.eval_shape(function, *operands)
        return jax.tree.map(lambda leaf: jnp.zeros(leaf.shape, leaf.dtype), shapes)

    return lax.cond(timesteps[0] >= 0, function, skip, *operands)


def on_device(
    tokens,
    timesteps,
    weight_codes,
    cotangent,
    ada_weight,
    qkv_weight,
    out_weight,
    up_weight,
    down_weight,
):
    clips, frames, spots, _ = tokens.shape
    n_pos = lax.axis_size("pos")
    n_clip = lax.axis_size("clip")
    chunks = clips * frames // n_pos
    span = clips // chunks
    n = n_pos * spots
    rows = 512
    places = min(spots, 32)

    n_all = n_pos * n_clip
    n_clips = n_clip * clips
    square_height = n_all
    feed_height = sum(a * b for a, b in FEED_SHAPES) // D + n_clips * 6 + square_height
    feed_height = round_up(feed_height, 16 * n_all)
    tail_height = round_up(3 * D + n_clips * 6, 8 * n_all)
    pos, clip = lax.axis_index("pos"), lax.axis_index("clip")
    mine = pos // frames
    own = clip * clips
    where = [pos, clip, (own + (chunks - 1) * span + mine) * 6, pos % INNER, pos // INNER]
    where = jnp.stack(where).astype(jnp.int32)

    def send(tokens, c):
        return tokens[c * span : (c + 1) * span].reshape(n_pos, spots, D)

    first = swap(send(tokens, 0))
    embedded = embed_steps(timesteps)
    mods = [
        jnp.dot(
            embedded, ada_weight[block].astype(F32), precision=lax.Precision.HIGHEST
        ).reshape(clips, 6, D)
        for block in range(2)
    ]
    embed_rows = lax.all_gather(embedded, "clip", axis=0, tiled=True)
    embed_columns = embed_rows.T
    scaling = jnp.exp2(0.5 * weight_codes.astype(F32) - 1.0)
    codes = jnp.broadcast_to(scaling[:, None, None], (clips, 1, D))
    arrived = [first.reshape(n, D)]
    for c in range(1, chunks):
        held, embed_columns, codes, *mods = lax.optimization_barrier(
            (tokens, embed_columns, codes, *mods)
        )
        arrived.append(swap(send(held, c)).reshape(n, D))

    kept_all = []
    streams = []
    for c in range(chunks):
        x = arrived[c]
        mod = lax.dynamic_index_in_dim(mods[0], c * span + mine, 0, keepdims=False)
        qkv = project(x, mod, qkv_weight, rows)
        att, logs = attend(qkv, 256)
        x_next, *kept, squares = feed(x, att, mod, out_weight, up_weight, down_weight, rows)
        streams.append(swap(x_next.reshape(n_pos, spots, D)).reshape(span, frames, spots, D))
        kept_all.append((x, mod, qkv, att, logs, kept, squares))

    weights = (qkv_weight, out_weight, up_weight, down_weight)
    results, returned, parts_one = (), [], []
    carried = ()
    for c in range(chunks):
        kind = BF
        result, g, part, *carried = temporal(
            streams[c], cotangent, c, codes, mods[1], weights, carried, results, kind, places
        )
        results = (result,)
        parts_one.append(part)
        returned.append(swap(g.reshape(n_pos, spots, D)).reshape(n, D))
    sums_one = carried

    def extra_rows(parts_one, squares_zero):
        part_one = jnp.concatenate(parts_one, axis=0)
        squares_zero = sum(squares_zero)[:3]
        squares_one = jnp.sum(part_one[:, 6:9], axis=0)
        squares = jnp.sum(jnp.concatenate([squares_zero, squares_one], axis=0), axis=1)
        terms = []
        for _ in range(3):
            kept = lax.reduce_precision(squares, exponent_bits=8, mantissa_bits=7)
            terms.append(kept.astype(BF))
            squares = squares - kept
        terms = jnp.pad(jnp.stack(terms), ((0, 0), (0, D // 3 - 6))).reshape(1, D)
        square_rows = lax.dynamic_update_slice(
            jnp.zeros((square_height, D), BF), terms, (pos * n_clip + clip, 0)
        )
        mod_one = lax.dynamic_update_slice(
            jnp.zeros((n_clips, 6, D), BF), part_one[:, :6].astype(BF), (own, 0, 0)
        )
        return jnp.concatenate([mod_one.reshape(n_clips * 6, D), square_rows], axis=0)

    def back_of_feed(c, g, carried, extra):
        x, mod, qkv, att, logs, kept, squares = kept_all[c]
        weights = (out_weight, up_weight, down_weight)
        n_parts = n_clip if c == chunks - 1 else 0
        return feed_back(
            where, extra, g, kept, att, mod, *weights, carried, BF, 256, feed_height, n_parts
        )

    def back_of_project(c, found, gmid, mods, carried):
        x, mod, qkv, att, logs, kept, squares = kept_all[c]
        n_parts = n_clip if c == chunks - 1 else 0
        found = [third[k] for k in range(3) for third in found]
        g, part, *carried = project_back(
            where, mods, x, found, gmid, mod, qkv_weight, carried, rows, tail_height, n_parts
        )
        return g.reshape(n_pos, spots, D), part[:6], carried

    def some_pairs(c, gatt, first, count):
        x, mod, qkv, att, logs, kept, squares = kept_all[c]
        return attend_back(qkv, att, logs, gatt, first, count, rows)

    def last_block_back(later, middle, found, carried, extra):
        middles = [middle]
        for c in range(1, chunks):
            gmid, gatt, part, *carried = back_of_feed(c, later[c - 1], carried, extra)
            middles.append((gmid, gatt, part))
        feed_part = sum_clips(carried)
        carried = ()
        grads = []
        mods = jnp.zeros((n_clips, 6, D), F32)
        for c, (gmid, gatt, part) in enumerate(middles):
            if c == 0:
                feed_part, gatt = lax.optimization_barrier((feed_part, gatt))
                feed_piece = sum_positions(feed_part, n_pos)
                found = [found]
            else:
                found = [some_pairs(c, gatt, 0, 2)]
            if c == chunks - 1:
                break
            found.append(some_pairs(c, gatt, 1, 2))
            grad, part_first, carried = back_of_project(c, found, gmid, mods.reshape(-1, D), carried)
            grads.append(grad)
            mods = lax.dynamic_update_index_in_dim(
                mods, part[:6] + part_first, own + c * span + mine, 0
            )
        mods = lax.dynamic_update_index_in_dim(mods, part[:6], own + (chunks - 1) * span + mine, 0)
        mods = mods.reshape(-1, D)

        gatt, found, feed_piece, *grads = lax.optimization_barrier((gatt, found, feed_piece, *grads))
        feed_pieces = gather_outer(feed_piece, n_pos)

        def last_step(grads, gatt, found, gmid, mods, carried):
            grads = [swap(grad) for grad in grads]
            done = 2 if chunks > 1 else 1
            found = found + [some_pairs(chunks - 1, gatt, done, PAIRS - done)]
            grad, _, parts = back_of_project(chunks - 1, found, gmid, mods, carried)
            return grads, grad, sum_clips(parts)

        grads, grad, part = as_one_step(
            timesteps, last_step, grads, gatt, found, gmid, mods, carried
        )
        part, feed_pieces = lax.optimization_barrier((part, feed_pieces))
        feed_pieces = gather_inner(feed_pieces, n_pos)
        piece = as_one_step(timesteps, lambda part: sum_positions(part, n_pos), part)
        piece, feed_pieces = lax.optimization_barrier((piece, feed_pieces))
        feed_pieces = gather_clips(jnp.stack(feed_pieces), n_clip)
        tail_pieces = as_one_step(timesteps, lambda piece: gather_outer(piece, n_pos), piece)
        grad, feed_pieces, tail_pieces = lax.optimization_barrier((grad, feed_pieces, tail_pieces))
        last = swap(grad)
        tail_pieces = gather_inner(tail_pieces, n_pos)

        def feed_step(feed_pieces, grads):
            count = clips * frames * spots * n_all
            return finish_feed(where, feed_pieces, embed_columns, grads, square_height, count)

        up, down, out, *held, rms = as_one_step(timesteps, feed_step, feed_pieces, grads)
        tail_pieces, held = lax.optimization_barrier((tail_pieces, held))
        tail_pieces = gather_clips(jnp.stack(tail_pieces), n_clip)
        held = [held[0], up, down, out, *held[1:]]
        return last, tail_pieces, held, rms[0, :6].reshape(2, 3)

    all_squares = [kept[-1] for kept in kept_all]
    if chunks > 1:
        unused = mods[0][0]
        gmid, gatt, part, *carried = back_of_feed(0, returned[0], (), unused)
        gatt, parts_one, all_squares = lax.optimization_barrier((gatt, parts_one, all_squares))
        extra = extra_rows(parts_one, all_squares)
    else:
        extra = extra_rows(parts_one, all_squares)
        gmid, gatt, part, *carried = back_of_feed(0, returned[0], (), extra)
    found = some_pairs(0, gatt, 0, 1)
    last, tail_pieces, held, stream_rms = as_one_step(
        timesteps, last_block_back, returned[1:], (gmid, gatt, part), found, carried, extra
    )
    qkv_one, out_one, up_one, down_one = lax.psum(tuple(sums_one), ("pos", "clip"))
    ones = (up_one, down_one, out_one)
    qkv_grad, ada_grad, up_grad, down_grad, out_grad, grad_tokens = finish(
        where, tail_pieces, embed_columns, qkv_one, ones, last, held, chunks
    )
    return (
        results[0],
        grad_tokens.reshape(tokens.shape),
        ada_grad,
        qkv_grad,
        out_grad,
        up_grad,
        down_grad,
        stream_rms,
    )


def solution(mesh):
    placed = (
        P("clip", None, "pos", None),
        P("clip"),
        P("clip"),
        P("clip", None, "pos", None),
        P(),
        P(),
        P(),
        P(),
        P(),
    )
    return jax.shard_map(
        on_device,
        mesh=mesh,
        in_specs=placed,
        out_specs=(
            P("clip", None, "pos", None),
            P("clip", None, "pos", None),
            P(),
            P(),
            P(),
            P(),
            P(),
            P(),
        ),
        check_vma=False,
    )
```
